128 devices in a mesh: space: 16 (over y_lo, x, core), mem: 8 (over y_hi, z).
Axes of the slice: x: 4, y: 4 (y_hi: 2, y_lo: 2; y = y_hi * 2 + y_lo), z: 4, core: 2. Of those that a mesh axis runs over, the one named last changes fastest.
Arguments:
- prior_ensemble: bfloat16 [64, 80, 256, 128], P('mem', None, 'space'), may hold values from -6 to 6
- initial_kernel_taps: bfloat16 [9, 80, 80], replicated, may hold values from -0.21875 to 0.21875
- latter_kernel_taps: bfloat16 [9, 80, 80], replicated, may hold values from -0.21875 to 0.21875
- observed_cells: int32 [16, 1024], P('space'), may hold values from 0 to 491519
- observed_count: int32 [16], P('space'), may hold values from 512 to 1024, as said below
- local_radius: int32 [16], P('space'), may hold values from 8 to 32
- observed_value: float32 [16, 1024], P('space'), may hold values from -6 to 6
- error_variance: float32 [16, 1024], P('space'), may hold values from 5.12 to 51.2
Outputs:
- analysis: bfloat16 [64, 80, 256, 128], P('mem', None, 'space')
The draws below stay inside these ranges and needn't reach their ends.
Inputs may be any that keep to these rules, and one draw needn't show every extreme that they name: observed_count reaches 1024 on some tile of every draw.
All inputs are finite; a program needn't handle non-finite values.
Results may differ from the reference program's by a relative error of at most 0.0064.
Values may be sent and summed in bfloat16 or wider, within the bound.
No kernel may reach another device: no remote copies, remote signals or barrier semaphores. Data moves between devices by JAX's collectives and lax.ppermute only.
A program may use at most 320 MiB of HBM per device.

```python
import math
import jax
import jax.numpy as jnp
from jax import lax

CH = 80
ENSEMBLE_SIZE = 64
LAT = 128
PATCH_WIDTH = 16
PROBE_PLACES = 1024
NS_ITERS = 4
PATCH_TOTAL = 16
LON = 256


def draw_observed_count(key, part):
    key = jax.random.fold_in(key, 7)
    first_key, second_key = jax.random.split(key)
    counts = jax.random.randint(first_key, (PATCH_TOTAL,), PROBE_PLACES // 2, PROBE_PLACES + 1)
    chosen = jax.random.randint(second_key, (), 0, PATCH_TOTAL)
    return counts.at[chosen].set(PROBE_PLACES).astype(jnp.int32)


def place_ends(result, own_key, low, largest):
    index_at = [jax.random.randint(jax.random.fold_in(own_key, axis), (), 0, length) for axis, length in enumerate(result.shape)]
    widest = result.shape.index(max(result.shape))
    beside = index_at[:widest] + [(index_at[widest] + 1) % result.shape[widest]] + index_at[widest + 1:]
    return result.at[tuple(index_at)].set(low).at[tuple(beside)].set(largest)


def level_of(rng, shape, cuts, smallest, high):
    gain = 1.0
    for position, parts in cuts:
        draws = jax.random.uniform(jax.random.fold_in(jax.random.fold_in(rng, 6), position), (parts,), jnp.float32, smallest / len(cuts), high / len(cuts))
        gain = gain * jnp.repeat(jnp.exp(draws), shape[position] // parts).reshape((-1,) + (1,) * (len(shape) - 1 - position))
    return gain


def normal_values(own_key, dims, scale, most, cuts=(), kind=jnp.bfloat16):
    factor_of = level_of(own_key, dims, cuts, -0.22, 0.18) if cuts else 1.0
    entries = jax.random.normal(own_key, dims, jnp.float32) * scale * factor_of
    return jnp.minimum(jnp.maximum(entries, -most), most).astype(kind)


def setup_inputs(seed: int = 0) -> dict:
    arg_keys = jax.random.split(jax.random.key(seed), 9)
    prior_ensemble = normal_values(arg_keys[0], (ENSEMBLE_SIZE, CH, LON, LAT), 1.0, 6.0, ((0, 8), (2, 16)))
    initial_kernel_taps = normal_values(arg_keys[1], (9, CH, CH), (9 * CH) ** -0.5, 0.21875)
    latter_kernel_taps = normal_values(arg_keys[2], (9, CH, CH), (9 * CH) ** -0.5, 0.21875)
    observed_cells = place_ends(jax.random.randint(arg_keys[3], (PATCH_TOTAL, PROBE_PLACES), 0, 3 * CH * PATCH_WIDTH * LAT), jax.random.fold_in(arg_keys[3], 1), 0, (3 * CH * PATCH_WIDTH * LAT) - 1).astype(jnp.int32)
    observed_count = draw_observed_count(jax.random.fold_in(arg_keys[8], 71), 0)
    local_radius = place_ends(jax.random.randint(arg_keys[5], (PATCH_TOTAL,), PATCH_WIDTH // 2, 2 * PATCH_WIDTH + 1), jax.random.fold_in(arg_keys[5], 1), PATCH_WIDTH // 2, 2 * PATCH_WIDTH).astype(jnp.int32)
    observed_value = normal_values(arg_keys[6], (PATCH_TOTAL, PROBE_PLACES), 1.0, 6.0, ((0, 16),), jnp.float32)
    error_variance = jnp.clip(jnp.exp(math.log(51.2) - 2.3025851 * jax.random.uniform(arg_keys[7], (PATCH_TOTAL, PROBE_PLACES), jnp.float32) ** level_of(arg_keys[7], (PATCH_TOTAL, PROBE_PLACES), ((0, 16),), -0.2, 0.2)), 5.12, 51.2)
    return {"prior_ensemble": prior_ensemble, "initial_kernel_taps": initial_kernel_taps, "latter_kernel_taps": latter_kernel_taps, "observed_cells": observed_cells, "observed_count": observed_count, "local_radius": local_radius, "observed_value": observed_value, "error_variance": error_variance}


STEP_SIZE = 0.5

def conv_valid(field, kernel):
    padded = jnp.pad(field, ((0, 0), (0, 0), (1, 1))).astype(jnp.float32)
    out_lon = field.shape[1] - 2
    lat_rows = field.shape[2]
    weights = kernel.astype(jnp.float32)
    accum = jnp.zeros((kernel.shape[1], out_lon, lat_rows), jnp.float32)
    for tap_index in range(9):
        shift_lon = tap_index // 3
        shift_lat = tap_index % 3
        window = padded[:, shift_lon:shift_lon + out_lon, shift_lat:shift_lat + lat_rows]
        accum = accum + jnp.einsum('oc,cxy->oxy', weights[tap_index], window, precision=lax.Precision.HIGHEST)
    return accum

def periodic(field):
    return jnp.concatenate([field[:, -1:], field, field[:, :1]], axis=1)

def tendency(field, initial_kernel_taps, latter_kernel_taps):
    hidden = jax.nn.gelu(conv_valid(periodic(field), initial_kernel_taps)).astype(jnp.bfloat16)
    return conv_valid(periodic(hidden), latter_kernel_taps)

def advance_dynamics(ensemble_position, initial_kernel_taps, latter_kernel_taps):
    first_rate = tendency(ensemble_position, initial_kernel_taps, latter_kernel_taps)
    section = (ensemble_position.astype(jnp.float32) + STEP_SIZE * first_rate).astype(jnp.bfloat16)
    second_rate = tendency(section, initial_kernel_taps, latter_kernel_taps)
    return (ensemble_position.astype(jnp.float32) + 0.5 * STEP_SIZE * (first_rate + second_rate)).astype(jnp.bfloat16)

def ensemble_transform(value_entries, cell_ids, live_count, radius, observed, variance, meridian_stripes, lat_rows):
    members = value_entries.shape[0]
    model_obs = value_entries.astype(jnp.float32)
    center = lax.optimization_barrier(jnp.mean(model_obs, axis=0))
    spread = model_obs - center
    lon_ext = cell_ids // lat_rows % (3 * meridian_stripes)
    distance = lon_ext.astype(jnp.float32) - (meridian_stripes + 0.5 * (meridian_stripes - 1))
    scaled = distance / radius.astype(jnp.float32)
    taper_weight = jnp.exp(-0.5 * scaled * scaled)
    slot_ids = jnp.arange(cell_ids.shape[0], dtype=jnp.int32)
    weight = jnp.where(slot_ids < live_count, taper_weight / variance, jnp.float32(0.0))
    weighted = spread * weight[None, :]
    gram_matrix = jnp.dot(weighted, spread.T, precision=lax.Precision.HIGHEST)
    right_side = jnp.dot(weighted, observed - center, precision=lax.Precision.HIGHEST)
    identity_mat = jnp.eye(members, dtype=jnp.float32)
    system = (members - 1.0) * identity_mat + gram_matrix
    norm_bound = members - 1.0 + jnp.sqrt(jnp.sum(gram_matrix * gram_matrix))
    iterate = system / norm_bound
    root_inv = identity_mat
    for sweep_index in range(NS_ITERS):
        factor = 1.5 * identity_mat - 0.5 * jnp.dot(root_inv, iterate, precision=lax.Precision.HIGHEST)
        iterate = jnp.dot(iterate, factor, precision=lax.Precision.HIGHEST)
        root_inv = jnp.dot(factor, root_inv, precision=lax.Precision.HIGHEST)
    inverse = jnp.dot(root_inv, root_inv, precision=lax.Precision.HIGHEST) / norm_bound
    shift_weights = jnp.dot(inverse, right_side, precision=lax.Precision.HIGHEST)
    return (shift_weights[:, None] + jnp.sqrt((members - 1.0) / norm_bound) * root_inv).astype(jnp.bfloat16)

def reference(prior_ensemble, initial_kernel_taps, latter_kernel_taps, observed_cells, observed_count, local_radius, observed_value, error_variance):
    predicted_ensemble = lax.map(lambda ensemble_position: advance_dynamics(ensemble_position, initial_kernel_taps, latter_kernel_taps), prior_ensemble)
    tile_column = jnp.arange(PATCH_TOTAL, dtype=jnp.int32)[:, None]
    channel = observed_cells // (3 * PATCH_WIDTH * LAT)
    lon_ext = observed_cells // LAT % (3 * PATCH_WIDTH)
    lat_pos = observed_cells % LAT
    lon_pos = (tile_column * PATCH_WIDTH + lon_ext - PATCH_WIDTH) % LON
    linear_position = ((channel * LON + lon_pos) * LAT + lat_pos).reshape(-1).astype(jnp.int32)
    gathered_readings = jnp.take(predicted_ensemble.reshape(ENSEMBLE_SIZE, -1), linear_position, axis=1).reshape(ENSEMBLE_SIZE, PATCH_TOTAL, PROBE_PLACES)

    def tile_transform(patch_number):
        return ensemble_transform(gathered_readings[:, patch_number], observed_cells[patch_number], observed_count[patch_number], local_radius[patch_number], observed_value[patch_number], error_variance[patch_number], PATCH_WIDTH, LAT)
    tile_list = jnp.arange(PATCH_TOTAL, dtype=jnp.int32)
    transforms = lax.map(tile_transform, tile_list)

    def tile_analysis(patch_number):
        patch_correction = lax.dynamic_slice_in_dim(predicted_ensemble, (patch_number * PATCH_WIDTH).astype(jnp.int32), PATCH_WIDTH, 2).astype(jnp.float32)
        center = lax.optimization_barrier(jnp.mean(patch_correction, axis=0))
        spread_half = (patch_correction - center).astype(jnp.bfloat16)
        mixed = jnp.einsum('ij,icxy->jcxy', transforms[patch_number].astype(jnp.float32), spread_half.astype(jnp.float32), precision=lax.Precision.HIGHEST)
        return (center + mixed).astype(jnp.bfloat16)
    blocks = lax.map(tile_analysis, tile_list)
    return jnp.transpose(blocks, (1, 2, 0, 3, 4)).reshape(ENSEMBLE_SIZE, CH, LON, LAT)
```

```python
import jax
import jax.numpy as jnp
from jax import lax
from jax.experimental import pallas as pl
from jax.experimental.pallas import tpu as pltpu
from jax.sharding import PartitionSpec as P

NS_ITERS = 4
STEP_SIZE = 0.5
HALO = 4


def gelu(x):
    c = 0.7978845608028654
    return 0.5 * x * (1.0 + jnp.tanh(c * (x + 0.044715 * (x * x * x))))


def shifted_sum(p, lane):
    below = pltpu.roll(p[0:80], 1, axis=1)
    above = pltpu.roll(p[160:240], 127, axis=1)
    return p[80:160] + jnp.where(lane == 0, 0.0, below) + jnp.where(lane == 127, 0.0, above)


def conv_columns(source, taps, columns, emit):
    lane = lax.broadcasted_iota(jnp.int32, (80, 128), 1)
    for k in range(0, columns, 2):
        window = jnp.concatenate(
            [source[pl.ds(80 * k, 240), :], source[pl.ds(80 * (k + 1), 240), :]], axis=1
        )
        partial = jnp.dot(taps, window, preferred_element_type=jnp.float32)
        emit(k, shifted_sum(partial[:, :128], lane))
        emit(k + 1, shifted_sum(partial[:, 128:], lane))


def forecast_kernel(
    rows, shifts, own, left, right, first_taps, second_taps, out, picked, v, h, s, rate, fields
):
    m = pl.program_id(0)
    v[0:320, :] = left[0].reshape(320, 128)
    v[320:1600, :] = own[0].reshape(1280, 128)
    v[1600:1920, :] = right[0].reshape(320, 128)
    taps_a = first_taps[...]
    taps_b = second_taps[...]

    def put_hidden(x, value):
        h[pl.ds(80 * x, 80), :] = gelu(value).astype(jnp.bfloat16)

    def put_section(x, value):
        base = v[pl.ds(80 * (x + 2), 80), :].astype(jnp.float32)
        s[pl.ds(80 * x, 80), :] = (base + STEP_SIZE * value).astype(jnp.bfloat16)
        if 2 <= x < 18:
            rate[pl.ds(80 * (x - 2), 80), :] = base + 0.5 * STEP_SIZE * value

    def put_forecast(x, value):
        cells = rate[pl.ds(80 * x, 80), :] + 0.5 * STEP_SIZE * value
        cells = cells.astype(jnp.bfloat16).astype(jnp.float32)
        fields[pl.ds(640 * x + m, 80, stride=8), :] = cells

    conv_columns(v, taps_a, 22, put_hidden)
    conv_columns(h, taps_b, 20, put_section)
    conv_columns(s, taps_a, 18, put_hidden)
    conv_columns(h, taps_b, 16, put_forecast)

    @pl.when(m == pl.num_programs(0) - 1)
    def _():
        out[...] = fields[...].astype(jnp.bfloat16).reshape(out.shape)
        lane = lax.broadcasted_iota(jnp.int32, (8, 128), 1)

        def block(b, carry):
            acc = jnp.zeros((8, 128), jnp.float32)
            for j in range(128):
                row = pl.multiple_of(rows[b * 128 + j], 8)
                cell = pltpu.roll(fields[pl.ds(row, 8), :], shifts[b * 128 + j], axis=1)
                acc = jnp.where(lane == j, cell, acc)
            picked[pl.ds(pl.multiple_of(b * 8, 8), 8), :] = acc
            return carry

        lax.fori_loop(0, picked.shape[0] // 8, block, 0)


def forecast(rows, shifts, own, left, right, first_taps, second_taps):
    members = own.shape[0]
    whole = lambda shape: pl.BlockSpec(shape, lambda i: (0,) * len(shape))
    slots = rows.shape[0]
    return pl.pallas_call(
        forecast_kernel,
        grid=(members,),
        in_specs=[
            pl.BlockSpec(memory_space=pltpu.SMEM),
            pl.BlockSpec(memory_space=pltpu.SMEM),
            pl.BlockSpec((1, 16, 80, 128), lambda i: (i, 0, 0, 0)),
            pl.BlockSpec((1, HALO, 80, 128), lambda i: (i, 0, 0, 0)),
            pl.BlockSpec((1, HALO, 80, 128), lambda i: (i, 0, 0, 0)),
            whole((240, 240)),
            whole((240, 240)),
        ],
        out_specs=[whole((16, 80, 8, 128)), whole((slots // 16, 128))],
        out_shape=[
            jax.ShapeDtypeStruct((16, 80, 8, 128), jnp.bfloat16),
            jax.ShapeDtypeStruct((slots // 16, 128), jnp.float32),
        ],
        scratch_shapes=[
            pltpu.VMEM((1920, 128), jnp.bfloat16),
            pltpu.VMEM((1760, 128), jnp.bfloat16),
            pltpu.VMEM((1600, 128), jnp.bfloat16),
            pltpu.VMEM((1280, 128), jnp.float32),
            pltpu.VMEM((16 * 80 * 8, 128), jnp.float32),
        ],
        compiler_params=pltpu.CompilerParams(vmem_limit_bytes=40 << 20),
        cost_estimate=pl.CostEstimate(
            flops=16_000_000_000, bytes_accessed=8_000_000, transcendentals=4_000_000
        ),
    )(rows, shifts, own, left, right, first_taps, second_taps)


def mix_kernel(parts, weights, out):
    w = weights[...]
    depth = parts.shape[2]
    for x in range(2):
        for k in range(0, depth, 8):
            centers = []
            halves = []
            for half in range(2):
                stack = []
                for q in range(4):
                    c = k + 4 * half + q
                    cells = parts[:, x, c].astype(jnp.float32)
                    center = jnp.sum(jnp.sum(cells, axis=0), axis=0, keepdims=True) * (1.0 / 64.0)
                    centers.append(center)
                    stack.append((cells.reshape(64, 128) - center).astype(jnp.bfloat16))
                halves.append(jnp.concatenate(stack, axis=0))
            mixed = jnp.dot(
                w, jnp.concatenate(halves, axis=1), preferred_element_type=jnp.float32
            )
            for half in range(2):
                for q in range(4):
                    c = k + 4 * half + q
                    value = mixed[64 * q : 64 * q + 64, 128 * half : 128 * half + 128]
                    value = value + centers[4 * half + q]
                    out[:, x, c] = value.astype(jnp.bfloat16).reshape(8, 8, 128)


def mix(parts, weights):
    depth = 16
    spec = pl.BlockSpec((8, 2, depth, 8, 128), lambda i: (0, 0, i, 0, 0))
    return pl.pallas_call(
        mix_kernel,
        grid=(80 // depth,),
        in_specs=[spec, pl.BlockSpec((256, 256), lambda i: (0, 0))],
        out_specs=spec,
        out_shape=jax.ShapeDtypeStruct((8, 2, 80, 8, 128), jnp.bfloat16),
        compiler_params=pltpu.CompilerParams(vmem_limit_bytes=40 << 20),
        cost_estimate=pl.CostEstimate(
            flops=700_000_000, bytes_accessed=5_300_000, transcendentals=0
        ),
    )(parts, weights)


def taps_matrix(taps):
    return taps.reshape(3, 3, 80, 80).transpose(1, 2, 0, 3).reshape(240, 240)


def ring(cells, step):
    count = lax.axis_size("space")
    return lax.ppermute(cells, "space", [(i, (i + step) % count) for i in range(count)])


def ensemble_transform(member_obs, weight, observed):
    members = member_obs.shape[0]
    model_obs = member_obs.astype(jnp.float32)
    center = jnp.mean(model_obs, axis=0)
    spread = model_obs - center
    weighted = spread * weight[None, :]
    gram_matrix = jnp.dot(weighted, spread.T, precision=lax.Precision.HIGHEST)
    right_side = jnp.dot(weighted, observed - center, precision=lax.Precision.HIGHEST)
    identity_mat = jnp.eye(members, dtype=jnp.float32)
    system = (members - 1.0) * identity_mat + gram_matrix
    norm_bound = members - 1.0 + jnp.sqrt(jnp.sum(gram_matrix * gram_matrix))
    iterate = system / norm_bound
    root_inv = identity_mat
    for sweep_index in range(NS_ITERS):
        factor = 1.5 * identity_mat - 0.5 * jnp.dot(
            root_inv, iterate, precision=lax.Precision.HIGHEST
        )
        iterate = jnp.dot(iterate, factor, precision=lax.Precision.HIGHEST)
        root_inv = jnp.dot(factor, root_inv, precision=lax.Precision.HIGHEST)
    inverse = jnp.dot(root_inv, root_inv, precision=lax.Precision.HIGHEST) / norm_bound
    shift_weights = jnp.dot(inverse, right_side, precision=lax.Precision.HIGHEST)
    return (shift_weights[:, None] + jnp.sqrt((members - 1.0) / norm_bound) * root_inv).astype(
        jnp.bfloat16
    )


def observation_weight(cells, live_count, radius, variance):
    lon = cells // 128 % 48
    distance = lon.astype(jnp.float32) - (16 + 0.5 * 15)
    scaled = distance / radius.astype(jnp.float32)
    taper = jnp.exp(-0.5 * scaled * scaled)
    slot_ids = jnp.arange(cells.shape[0], dtype=jnp.int32)
    return jnp.where(slot_ids < live_count, taper / variance, jnp.float32(0.0))


def per_device(
    prior_ensemble,
    initial_kernel_taps,
    latter_kernel_taps,
    observed_cells,
    observed_count,
    local_radius,
    observed_value,
    error_variance,
):
    own = jnp.swapaxes(prior_ensemble, 1, 2)
    left = ring(own[:, 16 - HALO :], 1)
    right = ring(own[:, :HALO], -1)
    cells = observed_cells[0]
    left_cells = ring(cells, 1)
    right_cells = ring(cells, -1)

    lists = jnp.stack([left_cells, cells, right_cells])
    lon = lists // 128 % 48
    here = lon // 16 == jnp.array([2, 1, 0], jnp.int32)[:, None]
    rows = jnp.where(here, (lon % 16 * 80 + lists // 6144) * 8, 0).reshape(-1)
    slot = jnp.arange(cells.shape[0], dtype=jnp.int32)
    shifts = ((slot - lists) & 127).reshape(-1)

    fields, picked = forecast(
        rows,
        shifts,
        own,
        left,
        right,
        taps_matrix(initial_kernel_taps),
        taps_matrix(latter_kernel_taps),
    )
    picked = picked.astype(jnp.bfloat16).reshape(3, 8, 8, 128)
    from_left = ring(picked[2], 1)
    from_right = ring(picked[0], -1)
    part = (cells // 128 % 48 // 16).reshape(8, 1, 128)
    obs = jnp.where(part == 0, from_left, jnp.where(part == 1, picked[1], from_right))
    everyone = lax.all_to_all(
        jnp.broadcast_to(obs[None], (8, 8, 8, 128)), "mem", split_axis=0, concat_axis=0, tiled=True
    )
    member_obs = everyone.reshape(8, 8, 8, 128).transpose(0, 2, 1, 3).reshape(64, 1024)
    weight = observation_weight(cells, observed_count[0], local_radius[0], error_variance[0])
    transform = ensemble_transform(member_obs, weight, observed_value[0])
    blocks = (
        jnp.eye(4, dtype=jnp.bfloat16)[:, None, :, None] * transform.T[None, :, None, :]
    ).reshape(256, 256)

    parts = lax.all_to_all(
        fields.reshape(8, 2, 80, 8, 128), "mem", split_axis=0, concat_axis=0, tiled=True
    )
    mixed = mix(parts, blocks)
    back = lax.all_to_all(mixed, "mem", split_axis=0, concat_axis=0, tiled=True)
    return back.reshape(16, 80, 8, 128).transpose(2, 1, 0, 3)


def solution(mesh):
    return jax.shard_map(
        per_device,
        mesh=mesh,
        in_specs=(
            P("mem", None, "space", None),
            P(),
            P(),
            P("space", None),
            P("space"),
            P("space"),
            P("space", None),
            P("space", None),
        ),
        out_specs=P("mem", None, "space", None),
        check_vma=False,
    )
```

```python
import jax
import jax.numpy as jnp
from jax import lax
from jax.experimental import pallas as pl
from jax.experimental.pallas import tpu as pltpu
from jax.sharding import PartitionSpec as P

NS_ITERS = 4
STEP_SIZE = 0.5
HALO = 4
CH = 80
COLUMNS = (4, 5, 6, 7, 8, 9, 10, 11, 0, 1, 2, 3, 12, 13, 14, 15)


def vmem_params():
    return pltpu.CompilerParams(vmem_limit_bytes=40 << 20)


def gelu(x):
    c = 0.7978845608028654
    return 0.5 * x * (1.0 + jnp.tanh(c * (x + 0.044715 * (x * x * x))))


def shifted_sum(p, lane):
    below = pltpu.roll(p[0:80], 1, axis=1)
    above = pltpu.roll(p[160:240], 127, axis=1)
    return p[80:160] + jnp.where(lane == 0, 0.0, below) + jnp.where(lane == 127, 0.0, above)


def conv_columns(source, first, taps, columns, emit):
    lane = lax.broadcasted_iota(jnp.int32, (CH, 128), 1)
    for k in range(0, columns, 2):
        at = CH * (first + k)
        window = jnp.concatenate(
            [source[pl.ds(at, 3 * CH), :], source[pl.ds(at + CH, 3 * CH), :]], axis=1
        )
        partial = jnp.dot(taps, window, preferred_element_type=jnp.float32)
        emit(k, shifted_sum(partial[:, :128], lane))
        emit(k + 1, shifted_sum(partial[:, 128:], lane))


def build_taps(taps, matrix):
    for b in range(3):
        row = jnp.concatenate([taps[3 * a + b].astype(jnp.float32) for a in range(3)], axis=1)
        matrix[pl.ds(CH * b, CH), :] = row.astype(jnp.bfloat16)


def inner_kernel(own, first_taps, second_taps, out, halves, rates, taps_a, taps_b, h, s, g, rate, fields):
    m = pl.program_id(0)

    @pl.when(m == 0)
    def _():
        build_taps(first_taps, taps_a)
        build_taps(second_taps, taps_b)

    a = taps_a[...]
    b = taps_b[...]
    v = own.at[0]

    def put_first(k, value):
        h[pl.ds(CH * k, CH), :] = gelu(value).astype(jnp.bfloat16)

    def put_section(k, value):
        base = v[pl.ds(CH * (k + 2), CH), :].astype(jnp.float32)
        s[pl.ds(CH * k, CH), :] = (base + STEP_SIZE * value).astype(jnp.bfloat16)
        rate[pl.ds(CH * k, CH), :] = base + 0.5 * STEP_SIZE * value

    def put_second(k, value):
        g[pl.ds(CH * k, CH), :] = gelu(value).astype(jnp.bfloat16)

    def put_forecast(k, value):
        cells = rate[pl.ds(CH * (k + 2), CH), :] + 0.5 * STEP_SIZE * value
        fields[pl.ds(8 * CH * k + m, CH, stride=8), :] = cells

    conv_columns(v, 0, a, 14, put_first)
    conv_columns(h, 0, b, 12, put_section)
    conv_columns(s, 0, a, 10, put_second)
    conv_columns(g, 0, b, 8, put_forecast)
    for k, (ref, left, right) in enumerate(((h, 0, 12), (s, 0, 10), (g, 0, 8))):
        halves[0, pl.ds(2 * CH * k, 2 * CH), :] = ref[pl.ds(CH * left, 2 * CH), :]
        halves[0, pl.ds(2 * CH * (k + 3), 2 * CH), :] = ref[pl.ds(CH * right, 2 * CH), :]
    rates[0, pl.ds(0, 2 * CH), :] = rate[pl.ds(0, 2 * CH), :]
    rates[0, pl.ds(2 * CH, 2 * CH), :] = rate[pl.ds(10 * CH, 2 * CH), :]

    @pl.when(m == pl.num_programs(0) - 1)
    def _():
        out[...] = fields[...].astype(jnp.bfloat16).reshape(out.shape)


def edge_kernel(
    inner, cells, first, second, left, right, low, high, halves, rates, out, rows, shifts,
    v, h, s, g, rate, fields,
):
    m = pl.program_id(0)
    a = first[...]
    b = second[...]

    @pl.when(m == 0)
    def _():
        slot = lax.broadcasted_iota(jnp.int32, (8, 128), 1)
        for k in range(3):
            cell = cells[k]
            strip = cell >> 7
            channel = (strip * 43691) >> 21
            lon = strip - 48 * channel - 16 * (2 - k)
            column = jnp.where(lon < 4, lon + 8, jnp.where(lon < 12, lon - 4, lon))
            here = (lon >= 0) & (lon < 16)
            rows[k] = jnp.where(here, column * CH + channel, 0)
            shifts[k] = (slot - cell) & 127

    for side, (x, y) in enumerate(((left, low), (high, right))):
        v[pl.ds(8 * CH * side, 4 * CH), :] = x[0]
        v[pl.ds(8 * CH * side + 4 * CH, 4 * CH), :] = y[0]
    for k, ref in enumerate((h, s, g)):
        ref[pl.ds(4 * CH, 2 * CH), :] = halves[0, pl.ds(2 * CH * k, 2 * CH), :]
        ref[pl.ds(6 * CH, 2 * CH), :] = halves[0, pl.ds(2 * CH * (k + 3), 2 * CH), :]

    def hidden(ref, at):
        def put(k, value):
            ref[pl.ds(CH * (at + k), CH), :] = gelu(value).astype(jnp.bfloat16)

        return put

    def section_left(k, value):
        base = v[pl.ds(CH * (k + 2), CH), :].astype(jnp.float32)
        s[pl.ds(CH * k, CH), :] = (base + STEP_SIZE * value).astype(jnp.bfloat16)
        if k >= 2:
            rate[pl.ds(CH * (k - 2), CH), :] = base + 0.5 * STEP_SIZE * value

    def section_right(k, value):
        base = v[pl.ds(CH * (k + 10), CH), :].astype(jnp.float32)
        s[pl.ds(CH * (8 + k), CH), :] = (base + STEP_SIZE * value).astype(jnp.bfloat16)
        if k < 2:
            rate[pl.ds(CH * (k + 2), CH), :] = base + 0.5 * STEP_SIZE * value

    def forecast_left(k, value):
        start = rate[pl.ds(CH * k, CH), :] if k < 2 else rates[0, pl.ds(CH * (k - 2), CH), :]
        fields[pl.ds(8 * CH * k + m, CH, stride=8), :] = start + 0.5 * STEP_SIZE * value

    def forecast_right(k, value):
        start = rates[0, pl.ds(CH * (k + 2), CH), :] if k < 2 else rate[pl.ds(CH * k, CH), :]
        fields[pl.ds(8 * CH * (k + 4) + m, CH, stride=8), :] = start + 0.5 * STEP_SIZE * value

    conv_columns(v, 0, a, 4, hidden(h, 0))
    conv_columns(v, 10, a, 4, hidden(h, 8))
    conv_columns(h, 0, b, 4, section_left)
    conv_columns(h, 6, b, 4, section_right)
    conv_columns(s, 0, a, 4, hidden(g, 0))
    conv_columns(s, 6, a, 4, hidden(g, 8))
    conv_columns(g, 0, b, 4, forecast_left)
    conv_columns(g, 6, b, 4, forecast_right)

    @pl.when(m == pl.num_programs(0) - 1)
    def _():
        out[...] = fields[...].astype(jnp.bfloat16).reshape(out.shape)


def whole(shape):
    return pl.BlockSpec(shape, lambda i: (0,) * len(shape))


def member(shape, at=0):
    return pl.BlockSpec((1,) + shape, lambda i: (i, at) + (0,) * (len(shape) - 1))


def inner_forecast(own, first_taps, second_taps):
    members = own.shape[0]
    bf16, f32 = jnp.bfloat16, jnp.float32
    return pl.pallas_call(
        inner_kernel,
        grid=(members,),
        in_specs=[member((16 * CH, 128)), whole((9, CH, CH)), whole((9, CH, CH))],
        out_specs=[
            whole((8, CH, 8, 128)),
            member((12 * CH, 128)),
            member((4 * CH, 128)),
            whole((3 * CH, 3 * CH)),
            whole((3 * CH, 3 * CH)),
        ],
        out_shape=[
            jax.ShapeDtypeStruct((16, CH, 8, 128), bf16),
            jax.ShapeDtypeStruct((members, 12 * CH, 128), bf16),
            jax.ShapeDtypeStruct((members, 4 * CH, 128), f32),
            jax.ShapeDtypeStruct((3 * CH, 3 * CH), bf16),
            jax.ShapeDtypeStruct((3 * CH, 3 * CH), bf16),
        ],
        scratch_shapes=[
            pltpu.VMEM((14 * CH, 128), bf16),
            pltpu.VMEM((12 * CH, 128), bf16),
            pltpu.VMEM((10 * CH, 128), bf16),
            pltpu.VMEM((12 * CH, 128), f32),
            pltpu.VMEM((8 * CH * 8, 128), f32),
        ],
        compiler_params=vmem_params(),
        cost_estimate=pl.CostEstimate(
            flops=12_000_000_000, bytes_accessed=8_000_000, transcendentals=2_000_000
        ),
    )(own, first_taps, second_taps)


def edge_forecast(inner, cells, first, second, left, right, own, halves, rates):
    members = own.shape[0]
    bf16, f32 = jnp.bfloat16, jnp.float32
    return pl.pallas_call(
        edge_kernel,
        grid=(members,),
        in_specs=[
            pl.BlockSpec(memory_space=pl.ANY),
            whole((3, 8, 128)),
            whole((3 * CH, 3 * CH)),
            whole((3 * CH, 3 * CH)),
            member((4 * CH, 128)),
            member((4 * CH, 128)),
            member((4 * CH, 128), 0),
            member((4 * CH, 128), 3),
            member((12 * CH, 128)),
            member((4 * CH, 128)),
        ],
        out_specs=[
            pl.BlockSpec((8, CH, 8, 128), lambda i: (1, 0, 0, 0)),
            whole((3, 8, 128)),
            whole((3, 8, 128)),
        ],
        out_shape=[
            jax.ShapeDtypeStruct((16, CH, 8, 128), bf16),
            jax.ShapeDtypeStruct((3, 8, 128), jnp.int32),
            jax.ShapeDtypeStruct((3, 8, 128), jnp.int32),
        ],
        scratch_shapes=[
            pltpu.VMEM((16 * CH, 128), bf16),
            pltpu.VMEM((12 * CH, 128), bf16),
            pltpu.VMEM((12 * CH, 128), bf16),
            pltpu.VMEM((12 * CH, 128), bf16),
            pltpu.VMEM((4 * CH, 128), f32),
            pltpu.VMEM((8 * CH * 8, 128), f32),
        ],
        input_output_aliases={0: 0},
        compiler_params=vmem_params(),
        cost_estimate=pl.CostEstimate(
            flops=9_000_000_000, bytes_accessed=8_000_000, transcendentals=2_000_000
        ),
    )(inner, cells, first, second, left, right, own, own, halves, rates)


def gather_kernel(rows, shifts, fields, picked):
    lane = lax.broadcasted_iota(jnp.int32, (8, 128), 1)

    def block(b, carry):
        acc = jnp.zeros((8, 128), jnp.float32)
        for j in range(128):
            cell = fields[rows[b, j]].astype(jnp.float32)
            acc = jnp.where(lane == j, pltpu.roll(cell, shifts[b, j], axis=1), acc)
        picked[b] = acc.astype(jnp.bfloat16)
        return carry

    lax.fori_loop(0, picked.shape[0], block, 0)


def gather(rows, shifts, fields):
    blocks = rows.shape[0]
    return pl.pallas_call(
        gather_kernel,
        in_specs=[
            pl.BlockSpec(memory_space=pltpu.SMEM),
            pl.BlockSpec(memory_space=pltpu.SMEM),
            pl.BlockSpec(memory_space=pltpu.VMEM),
        ],
        out_specs=pl.BlockSpec(memory_space=pltpu.VMEM),
        out_shape=jax.ShapeDtypeStruct((blocks, 8, 128), jnp.bfloat16),
        compiler_params=vmem_params(),
        cost_estimate=pl.CostEstimate(
            flops=10_000_000, bytes_accessed=3_000_000, transcendentals=0
        ),
    )(rows, shifts, fields)


def transform_kernel(here, pair, ahead, across, behind, cells, numbers, observed, variance, out, stack):
    f32 = jnp.float32
    exact = lax.Precision.HIGHEST
    depth = numbers[0]
    half = numbers[1]
    for z in range(4):
        step = (z - depth) & 3
        for y in range(2):
            other = (y ^ half) & 1
            rows = pl.ds(8 * (4 * y + z), 8)
            for block in range(8):
                lanes = pl.ds(128 * block, 128)

                def take(ref, pick=None):
                    return ref[other, block].astype(f32)

                value = jnp.where(
                    step == 0,
                    jnp.where(other == 0, here[block].astype(f32), pair[block].astype(f32)),
                    jnp.where(step == 1, take(ahead), jnp.where(step == 2, take(across), take(behind))),
                )
                stack[rows, lanes] = value
    model_obs = stack[...]
    center = jnp.sum(model_obs, axis=0, keepdims=True) * (1.0 / 64.0)
    spread = model_obs - center
    cell = cells[...]
    strip = cell >> 7
    lon = strip - 48 * ((strip * 43691) >> 21)
    scaled = (lon.astype(f32) - 23.5) / numbers[3].astype(f32)
    taper = jnp.exp(-0.5 * scaled * scaled)
    slot = lax.broadcasted_iota(jnp.int32, cell.shape, 1)
    weight = jnp.where(slot < numbers[2], taper / variance[...], 0.0)
    weighted = spread * weight

    def product(x, y):
        return jnp.dot(x, y, precision=exact, preferred_element_type=f32)

    gram = lax.dot_general(
        weighted, spread, (((1,), (1,)), ((), ())), precision=exact, preferred_element_type=f32
    )
    right_side = jnp.sum(weighted * (observed[...] - center), axis=1, keepdims=True)
    i = lax.broadcasted_iota(jnp.int32, (64, 64), 0)
    j = lax.broadcasted_iota(jnp.int32, (64, 64), 1)
    eye = jnp.where(i == j, 1.0, 0.0).astype(f32)
    norm = 63.0 + jnp.sqrt(jnp.sum(jnp.sum(gram * gram, axis=1, keepdims=True), axis=0, keepdims=True))
    iterate = (63.0 * eye + gram) / norm
    root = 1.5 * eye - 0.5 * iterate
    iterate = product(iterate, root)
    for sweep in range(1, NS_ITERS):
        factor = 1.5 * eye - 0.5 * product(root, iterate)
        if sweep < NS_ITERS - 1:
            iterate = product(iterate, factor)
        root = product(factor, root)
    wide = jnp.broadcast_to(right_side, (64, 128))
    shift = product(root, product(root, wide)) / norm
    out[...] = (shift[:, :64] + jnp.sqrt(63.0 / norm) * root).astype(jnp.bfloat16)


def transform_of(pieces, cells, numbers, observed, variance):
    vmem = pl.BlockSpec(memory_space=pltpu.VMEM)
    smem = pl.BlockSpec(memory_space=pltpu.SMEM)
    return pl.pallas_call(
        transform_kernel,
        in_specs=[vmem] * 6 + [smem] + [vmem] * 2,
        out_specs=vmem,
        out_shape=jax.ShapeDtypeStruct((64, 64), jnp.bfloat16),
        scratch_shapes=[pltpu.VMEM((64, 1024), jnp.float32)],
        compiler_params=vmem_params(),
        cost_estimate=pl.CostEstimate(
            flops=100_000_000, bytes_accessed=500_000, transcendentals=1000
        ),
    )(*pieces, cells, numbers, observed, variance)


def mix_kernel(parts, weights, out):
    w = weights[...]
    depth = parts.shape[2]
    for x in range(2):
        for k in range(0, depth, 8):
            centers = []
            halves = []
            for half in range(2):
                stack = []
                for q in range(4):
                    c = k + 4 * half + q
                    cells = parts[:, x, c].astype(jnp.float32)
                    center = jnp.sum(jnp.sum(cells, axis=0), axis=0, keepdims=True) * (1.0 / 64.0)
                    centers.append(center)
                    stack.append((cells.reshape(64, 128) - center).astype(jnp.bfloat16))
                halves.append(jnp.concatenate(stack, axis=0))
            mixed = jnp.dot(
                w, jnp.concatenate(halves, axis=1), preferred_element_type=jnp.float32
            )
            for half in range(2):
                for q in range(4):
                    c = k + 4 * half + q
                    value = mixed[64 * q : 64 * q + 64, 128 * half : 128 * half + 128]
                    value = value + centers[4 * half + q]
                    out[:, x, c] = value.astype(jnp.bfloat16).reshape(8, 8, 128)


def mix(parts, weights):
    depth = 16
    spec = pl.BlockSpec((8, 2, depth, 8, 128), lambda i: (0, 0, i, 0, 0))
    return pl.pallas_call(
        mix_kernel,
        grid=(CH // depth,),
        in_specs=[spec, whole((256, 256))],
        out_specs=spec,
        out_shape=jax.ShapeDtypeStruct((8, 2, CH, 8, 128), jnp.bfloat16),
        compiler_params=vmem_params(),
        cost_estimate=pl.CostEstimate(
            flops=700_000_000, bytes_accessed=5_300_000, transcendentals=0
        ),
    )(parts, weights)


def order_kernel(cells, out, scratch):
    depth = cells.shape[1]
    for slot, column in enumerate(COLUMNS):
        for c in range(depth):
            value = cells[slot, c].astype(jnp.float32)
            scratch[pl.ds(128 * c + column, 8, stride=16), :] = value
    for c in range(depth):
        value = scratch[pl.ds(128 * c, 128), :].astype(jnp.bfloat16)
        out[:, c] = value.reshape(8, 16, 128)


def order(cells):
    depth = 16
    return pl.pallas_call(
        order_kernel,
        grid=(CH // depth,),
        in_specs=[pl.BlockSpec((16, depth, 8, 128), lambda i: (0, i, 0, 0))],
        out_specs=pl.BlockSpec((8, depth, 16, 128), lambda i: (0, i, 0, 0)),
        out_shape=jax.ShapeDtypeStruct((8, CH, 16, 128), jnp.bfloat16),
        scratch_shapes=[pltpu.VMEM((depth * 128, 128), jnp.float32)],
        compiler_params=vmem_params(),
        cost_estimate=pl.CostEstimate(
            flops=0, bytes_accessed=5_300_000, transcendentals=0
        ),
    )(cells)


def ring(cells, step):
    count = lax.axis_size("space")
    return lax.ppermute(cells, "space", [(i, (i + step) % count) for i in range(count)])


def depth_ring(cells, step):
    return lax.ppermute(
        cells, "mem", [(4 * y + (z + step) % 4, 4 * y + z) for y in range(2) for z in range(4)]
    )


def per_device(
    prior_ensemble,
    initial_kernel_taps,
    latter_kernel_taps,
    observed_cells,
    observed_count,
    local_radius,
    observed_value,
    error_variance,
):
    members = prior_ensemble.shape[0]
    flat = lambda x: jnp.swapaxes(x, 1, 2).reshape(members, -1, 128)
    left = ring(flat(prior_ensemble[:, :, 16 - HALO :]), 1)
    right = ring(flat(prior_ensemble[:, :, :HALO]), -1)
    cells = observed_cells.reshape(8, 128)
    lists = jnp.stack([ring(cells, 1), cells, ring(cells, -1)])
    own = flat(prior_ensemble)

    inner, halves, rates, first, second = inner_forecast(
        own, initial_kernel_taps, latter_kernel_taps
    )
    fields, rows, shifts = edge_forecast(
        inner, lists, first, second, left, right, own, halves, rates
    )
    parts = lax.all_to_all(
        fields.reshape(8, 2, CH, 8, 128), "mem", split_axis=0, concat_axis=0, tiled=True
    )

    picked = gather(
        rows.reshape(24, 128), shifts.reshape(24, 128), fields.reshape(16 * CH, 8, 128)
    ).reshape(3, 8, 8, 128)
    from_left = ring(picked[2], 1)
    from_right = ring(picked[0], -1)
    part = (cells // 128 % 48 // 16).reshape(8, 1, 128)
    here = jnp.where(part == 0, from_left, jnp.where(part == 1, picked[1], from_right))
    pair = lax.ppermute(here, "mem", [(i, i ^ 4) for i in range(8)])
    both = jnp.stack([here, pair])
    group = lax.axis_index("mem").astype(jnp.int32)
    numbers = jnp.stack([group % 4, group // 4, observed_count[0], local_radius[0]])
    transform = transform_of(
        (here, pair, depth_ring(both, 1), depth_ring(both, 2), depth_ring(both, 3)),
        observed_cells,
        numbers,
        observed_value,
        error_variance,
    )
    blocks = (
        jnp.eye(4, dtype=jnp.bfloat16)[:, None, :, None] * transform.T[None, :, None, :]
    ).reshape(256, 256)
    mixed = mix(parts, blocks)
    back = lax.all_to_all(mixed, "mem", split_axis=0, concat_axis=0, tiled=True)
    return order(back.reshape(16, CH, 8, 128))


def solution(mesh):
    return jax.shard_map(
        per_device,
        mesh=mesh,
        in_specs=(
            P("mem", None, "space", None),
            P(),
            P(),
            P("space", None),
            P("space"),
            P("space"),
            P("space", None),
            P("space", None),
        ),
        out_specs=P("mem", None, "space", None),
        check_vma=False,
    )
```

```python
import jax
import jax.numpy as jnp
from jax import lax
from jax.experimental import pallas as pl
from jax.experimental.pallas import tpu as pltpu
from jax.sharding import PartitionSpec as P

NS_ITERS = 4
STEP_SIZE = 0.5
HALO = 4
CH = 80


def vmem_params():
    return pltpu.CompilerParams(vmem_limit_bytes=40 << 20)


def gelu(x):
    c = 0.7978845608028654
    return 0.5 * x * (1.0 + jnp.tanh(c * (x + 0.044715 * (x * x * x))))


def shifted_sum(p, lane):
    below = pltpu.roll(p[0:80], 1, axis=1)
    above = pltpu.roll(p[160:240], 127, axis=1)
    return p[80:160] + jnp.where(lane == 0, 0.0, below) + jnp.where(lane == 127, 0.0, above)


def conv_columns(source, first, taps, columns, emit):
    lane = lax.broadcasted_iota(jnp.int32, (CH, 128), 1)
    for k in range(0, columns, 2):
        at = CH * (first + k)
        window = jnp.concatenate(
            [source[pl.ds(at, 3 * CH), :], source[pl.ds(at + CH, 3 * CH), :]], axis=1
        )
        partial = jnp.dot(taps, window, preferred_element_type=jnp.float32)
        emit(k, shifted_sum(partial[:, :128], lane))
        emit(k + 1, shifted_sum(partial[:, 128:], lane))


def build_taps(taps, matrix):
    for b in range(3):
        row = jnp.concatenate([taps[3 * a + b].astype(jnp.float32) for a in range(3)], axis=1)
        matrix[pl.ds(CH * b, CH), :] = row.astype(jnp.bfloat16)


def inner_kernel(own, first_taps, second_taps, out, halves, rates, taps_a, taps_b, h, s, g, rate, fields):
    build_taps(first_taps, taps_a)
    build_taps(second_taps, taps_b)
    a = taps_a[...]
    b = taps_b[...]

    def one(m, carry):
        v = own.at[m]

        def put_first(k, value):
            h[pl.ds(CH * k, CH), :] = gelu(value).astype(jnp.bfloat16)

        def put_section(k, value):
            base = v[pl.ds(CH * (k + 2), CH), :].astype(jnp.float32)
            s[pl.ds(CH * k, CH), :] = (base + STEP_SIZE * value).astype(jnp.bfloat16)
            rate[pl.ds(CH * k, CH), :] = base + 0.5 * STEP_SIZE * value

        def put_second(k, value):
            g[pl.ds(CH * k, CH), :] = gelu(value).astype(jnp.bfloat16)

        def put_forecast(k, value):
            cells = rate[pl.ds(CH * (k + 2), CH), :] + 0.5 * STEP_SIZE * value
            fields[pl.ds(8 * CH * k + m, CH, stride=8), :] = cells

        conv_columns(v, 0, a, 14, put_first)
        conv_columns(h, 0, b, 12, put_section)
        conv_columns(s, 0, a, 10, put_second)
        conv_columns(g, 0, b, 8, put_forecast)
        for k, (ref, right) in enumerate(((h, 12), (s, 10), (g, 8))):
            halves[m, pl.ds(2 * CH * k, 2 * CH), :] = ref[pl.ds(0, 2 * CH), :]
            halves[m, pl.ds(2 * CH * (k + 3), 2 * CH), :] = ref[pl.ds(CH * right, 2 * CH), :]
        rates[m, pl.ds(0, 2 * CH), :] = rate[pl.ds(0, 2 * CH), :]
        rates[m, pl.ds(2 * CH, 2 * CH), :] = rate[pl.ds(10 * CH, 2 * CH), :]
        return carry

    lax.fori_loop(0, own.shape[0], one, 0)
    out[...] = fields[...].astype(jnp.bfloat16).reshape(out.shape)


def place_of(channel, lon, lat, part):
    slot = lax.broadcasted_iota(jnp.int32, (8, 128), 1)
    lon = lon - 16 * part
    column = jnp.where(lon < 4, lon + 8, jnp.where(lon < 12, lon - 4, lon))
    here = (lon >= 0) & (lon < 16)
    return jnp.where(here, (column * CH + channel) * 8, 0), (slot - lat) & 127


def edge_kernel(
    inner, cells, first, second, left, right, own, halves, rates, out, picked,
    v, h, s, g, rate, fields, places, rows, turns, sems,
):
    members = own.shape[0]
    a = first[...]
    b = second[...]
    digits = CH * HALO * members
    for k, source in enumerate((left, cells, right)):
        if k == 1:
            cell = source[...]
            strip = cell >> 7
            channel = (strip * 43691) >> 21
            parts = (channel, strip - 48 * channel, cell & 127)
        else:
            block = source[pl.ds(digits, 32), :].astype(jnp.float32).astype(jnp.int32)
            parts = (block[0:8], block[8:16], block[16:24])
        row, turn = place_of(*parts, 2 - k)
        places[0, pl.ds(8 * k, 8), :] = row
        places[1, pl.ds(8 * k, 8), :] = turn
    copies = [
        pltpu.make_async_copy(places.at[0], rows, sems.at[0]),
        pltpu.make_async_copy(places.at[1], turns, sems.at[1]),
    ]
    for copy in copies:
        copy.start()
    fields[pl.ds(0, 64 * CH), :] = inner[...].astype(jnp.float32).reshape(64 * CH, 128)

    def one(m, carry):
        halo = pl.ds(pl.multiple_of(CH * HALO * m, CH * HALO), CH * HALO)
        v[pl.ds(0, 4 * CH), :] = left[halo, :]
        v[pl.ds(4 * CH, 4 * CH), :] = own[m, pl.ds(0, 4 * CH), :]
        v[pl.ds(8 * CH, 4 * CH), :] = own[m, pl.ds(12 * CH, 4 * CH), :]
        v[pl.ds(12 * CH, 4 * CH), :] = right[halo, :]
        for k, ref in enumerate((h, s, g)):
            ref[pl.ds(4 * CH, 2 * CH), :] = halves[m, pl.ds(2 * CH * k, 2 * CH), :]
            ref[pl.ds(6 * CH, 2 * CH), :] = halves[m, pl.ds(2 * CH * (k + 3), 2 * CH), :]

        def hidden(ref, at):
            def put(k, value):
                ref[pl.ds(CH * (at + k), CH), :] = gelu(value).astype(jnp.bfloat16)

            return put

        def section_left(k, value):
            base = v[pl.ds(CH * (k + 2), CH), :].astype(jnp.float32)
            s[pl.ds(CH * k, CH), :] = (base + STEP_SIZE * value).astype(jnp.bfloat16)
            if k >= 2:
                rate[pl.ds(CH * (k - 2), CH), :] = base + 0.5 * STEP_SIZE * value

        def section_right(k, value):
            base = v[pl.ds(CH * (k + 10), CH), :].astype(jnp.float32)
            s[pl.ds(CH * (8 + k), CH), :] = (base + STEP_SIZE * value).astype(jnp.bfloat16)
            if k < 2:
                rate[pl.ds(CH * (k + 2), CH), :] = base + 0.5 * STEP_SIZE * value

        def put_field(column, start, value):
            value = (start + 0.5 * STEP_SIZE * value).astype(jnp.bfloat16).astype(jnp.float32)
            fields[pl.ds(8 * CH * (8 + column) + m, CH, stride=8), :] = value

        def forecast_left(k, value):
            start = rate[pl.ds(CH * k, CH), :] if k < 2 else rates[m, pl.ds(CH * (k - 2), CH), :]
            put_field(k, start, value)

        def forecast_right(k, value):
            start = rates[m, pl.ds(CH * (k + 2), CH), :] if k < 2 else rate[pl.ds(CH * k, CH), :]
            put_field(k + 4, start, value)

        conv_columns(v, 0, a, 4, hidden(h, 0))
        conv_columns(v, 10, a, 4, hidden(h, 8))
        conv_columns(h, 0, b, 4, section_left)
        conv_columns(h, 6, b, 4, section_right)
        conv_columns(s, 0, a, 4, hidden(g, 0))
        conv_columns(s, 6, a, 4, hidden(g, 8))
        conv_columns(g, 0, b, 4, forecast_left)
        conv_columns(g, 6, b, 4, forecast_right)
        return carry

    lax.fori_loop(0, members, one, 0)
    out[...] = fields[pl.ds(64 * CH, 64 * CH), :].astype(jnp.bfloat16).reshape(out.shape)
    for copy in copies:
        copy.wait()
    lane = lax.broadcasted_iota(jnp.int32, (8, 128), 1)

    def block(k, carry):
        acc = jnp.zeros((8, 128), jnp.float32)
        for j in range(128):
            cell = fields[pl.ds(pl.multiple_of(rows[k, j], 8), 8), :]
            acc = jnp.where(lane == j, pltpu.roll(cell, turns[k, j], axis=1), acc)
        picked[k] = acc.astype(jnp.bfloat16)
        return carry

    lax.fori_loop(0, picked.shape[0], block, 0)


def vmem():
    return pl.BlockSpec(memory_space=pltpu.VMEM)


def inner_forecast(own, first_taps, second_taps):
    members = own.shape[0]
    bf16, f32 = jnp.bfloat16, jnp.float32
    return pl.pallas_call(
        inner_kernel,
        in_specs=[vmem()] * 3,
        out_specs=[vmem()] * 5,
        out_shape=[
            jax.ShapeDtypeStruct((8, CH, 8, 128), bf16),
            jax.ShapeDtypeStruct((members, 12 * CH, 128), bf16),
            jax.ShapeDtypeStruct((members, 4 * CH, 128), f32),
            jax.ShapeDtypeStruct((3 * CH, 3 * CH), bf16),
            jax.ShapeDtypeStruct((3 * CH, 3 * CH), bf16),
        ],
        scratch_shapes=[
            pltpu.VMEM((14 * CH, 128), bf16),
            pltpu.VMEM((12 * CH, 128), bf16),
            pltpu.VMEM((10 * CH, 128), bf16),
            pltpu.VMEM((12 * CH, 128), f32),
            pltpu.VMEM((64 * CH, 128), f32),
        ],
        compiler_params=vmem_params(),
        cost_estimate=pl.CostEstimate(
            flops=12_000_000_000, bytes_accessed=8_000_000, transcendentals=2_000_000
        ),
    )(own, first_taps, second_taps)


def edge_forecast(inner, cells, first, second, left, right, own, halves, rates):
    bf16, f32 = jnp.bfloat16, jnp.float32
    return pl.pallas_call(
        edge_kernel,
        in_specs=[vmem()] * 9,
        out_specs=[vmem()] * 2,
        out_shape=[
            jax.ShapeDtypeStruct((8, CH, 8, 128), bf16),
            jax.ShapeDtypeStruct((24, 8, 128), bf16),
        ],
        scratch_shapes=[
            pltpu.VMEM((16 * CH, 128), bf16),
            pltpu.VMEM((12 * CH, 128), bf16),
            pltpu.VMEM((12 * CH, 128), bf16),
            pltpu.VMEM((12 * CH, 128), bf16),
            pltpu.VMEM((4 * CH, 128), f32),
            pltpu.VMEM((128 * CH, 128), f32),
            pltpu.VMEM((2, 24, 128), jnp.int32),
            pltpu.SMEM((24, 128), jnp.int32),
            pltpu.SMEM((24, 128), jnp.int32),
            pltpu.SemaphoreType.DMA((2,)),
        ],
        compiler_params=vmem_params(),
        cost_estimate=pl.CostEstimate(
            flops=9_000_000_000, bytes_accessed=8_000_000, transcendentals=2_000_000
        ),
    )(inner, cells, first, second, left, right, own, halves, rates)


def transform_kernel(here, pair, ahead, across, behind, cells, numbers, observed, variance, out, stack):
    f32 = jnp.float32
    exact = lax.Precision.HIGHEST
    depth = numbers[0]
    half = numbers[1]
    for z in range(4):
        step = (z - depth) & 3
        for y in range(2):
            other = (y ^ half) & 1
            rows = pl.ds(8 * (4 * y + z), 8)
            for block in range(8):
                lanes = pl.ds(128 * block, 128)

                def take(ref, pick=None):
                    return ref[other, block].astype(f32)

                value = jnp.where(
                    step == 0,
                    jnp.where(other == 0, here[block].astype(f32), pair[block].astype(f32)),
                    jnp.where(step == 1, take(ahead), jnp.where(step == 2, take(across), take(behind))),
                )
                stack[rows, lanes] = value
    model_obs = stack[...]
    center = jnp.sum(model_obs, axis=0, keepdims=True) * (1.0 / 64.0)
    spread = model_obs - center
    cell = cells[...]
    strip = cell >> 7
    lon = strip - 48 * ((strip * 43691) >> 21)
    scaled = (lon.astype(f32) - 23.5) / numbers[3].astype(f32)
    taper = jnp.exp(-0.5 * scaled * scaled)
    slot = lax.broadcasted_iota(jnp.int32, cell.shape, 1)
    weight = jnp.where(slot < numbers[2], taper / variance[...], 0.0)
    weighted = spread * weight

    def product(x, y):
        return jnp.dot(x, y, precision=exact, preferred_element_type=f32)

    gram = lax.dot_general(
        weighted, spread, (((1,), (1,)), ((), ())), precision=exact, preferred_element_type=f32
    )
    right_side = jnp.sum(weighted * (observed[...] - center), axis=1, keepdims=True)
    i = lax.broadcasted_iota(jnp.int32, (64, 64), 0)
    j = lax.broadcasted_iota(jnp.int32, (64, 64), 1)
    eye = jnp.where(i == j, 1.0, 0.0).astype(f32)
    norm = 63.0 + jnp.sqrt(jnp.sum(jnp.sum(gram * gram, axis=1, keepdims=True), axis=0, keepdims=True))
    iterate = (63.0 * eye + gram) / norm
    root = 1.5 * eye - 0.5 * iterate
    iterate = product(iterate, root)
    for sweep in range(1, NS_ITERS):
        factor = 1.5 * eye - 0.5 * product(root, iterate)
        if sweep < NS_ITERS - 1:
            iterate = product(iterate, factor)
        root = product(factor, root)
    wide = jnp.broadcast_to(right_side, (64, 128))
    shift = product(root, product(root, wide)) / norm
    transform = (shift[:, :64] + jnp.sqrt(63.0 / norm) * root).astype(jnp.bfloat16)
    i = lax.broadcasted_iota(jnp.int32, (64, 256), 0)
    j = lax.broadcasted_iota(jnp.int32, (64, 256), 1)
    for q in range(4):
        place = jnp.where(j == i + 64 * q, 1.0, 0.0).astype(jnp.bfloat16)
        turned = lax.dot_general(
            transform, place, (((0,), (0,)), ((), ())), preferred_element_type=f32
        )
        out[pl.ds(64 * q, 64), :] = turned.astype(jnp.bfloat16)


def transform_of(pieces, cells, numbers, observed, variance):
    smem = pl.BlockSpec(memory_space=pltpu.SMEM)
    return pl.pallas_call(
        transform_kernel,
        in_specs=[vmem()] * 6 + [smem] + [vmem()] * 2,
        out_specs=vmem(),
        out_shape=jax.ShapeDtypeStruct((256, 256), jnp.bfloat16),
        scratch_shapes=[pltpu.VMEM((64, 1024), jnp.float32)],
        compiler_params=vmem_params(),
        cost_estimate=pl.CostEstimate(
            flops=100_000_000, bytes_accessed=500_000, transcendentals=1000
        ),
    )(*pieces, cells, numbers, observed, variance)


def mix_kernel(inner, edge, weights, out):
    w = weights[...]

    def block(k, carry):
        for x, parts in enumerate((inner, edge)):
            centers = []
            halves = []
            for half in range(2):
                stack = []
                for q in range(4):
                    cells = parts[:, 8 * k + 4 * half + q].astype(jnp.float32)
                    center = jnp.sum(jnp.sum(cells, axis=0), axis=0, keepdims=True) * (1.0 / 64.0)
                    centers.append(center)
                    stack.append((cells.reshape(64, 128) - center).astype(jnp.bfloat16))
                halves.append(jnp.concatenate(stack, axis=0))
            mixed = jnp.dot(
                w, jnp.concatenate(halves, axis=1), preferred_element_type=jnp.float32
            )
            for half in range(2):
                for q in range(4):
                    value = mixed[64 * q : 64 * q + 64, 128 * half : 128 * half + 128]
                    value = value + centers[4 * half + q]
                    out[:, x, 8 * k + 4 * half + q] = value.astype(jnp.bfloat16).reshape(8, 8, 128)
        return carry

    lax.fori_loop(0, CH // 8, block, 0)


def mix(inner, edge, weights):
    return pl.pallas_call(
        mix_kernel,
        in_specs=[vmem()] * 3,
        out_specs=vmem(),
        out_shape=jax.ShapeDtypeStruct((8, 2, CH, 8, 128), jnp.bfloat16),
        compiler_params=vmem_params(),
        cost_estimate=pl.CostEstimate(
            flops=700_000_000, bytes_accessed=5_300_000, transcendentals=0
        ),
    )(inner, edge, weights)


CHUNKS = 5


def order_kernel(cells, out, scratch, sems):
    to = lax.broadcasted_iota(jnp.int32, (128, 128), 0)
    at = lax.broadcasted_iota(jnp.int32, (128, 128), 1)
    source = at >> 4
    side = (at >> 3) & 1
    column = jnp.where(side == 0, source + 4, jnp.where(source < 4, source, source + 8))
    move = jnp.where(to == (at & 7) * 16 + column, 1.0, 0.0).astype(jnp.bfloat16)
    depth = CH // CHUNKS
    copies = []
    for chunk in range(CHUNKS):
        for c in range(depth * chunk, depth * (chunk + 1), 2):
            both = jnp.concatenate(
                [cells[:, c].reshape(128, 128), cells[:, c + 1].reshape(128, 128)], axis=1
            )
            moved = jnp.dot(move, both, preferred_element_type=jnp.float32).astype(jnp.bfloat16)
            scratch[:, c] = moved[:, :128].reshape(8, 16, 128)
            scratch[:, c + 1] = moved[:, 128:].reshape(8, 16, 128)
        rows = pl.ds(depth * chunk, depth)
        copy = pltpu.make_async_copy(scratch.at[:, rows], out.at[:, rows], sems.at[chunk])
        copy.start()
        copies.append(copy)
    for copy in copies:
        copy.wait()


def order(cells):
    return pl.pallas_call(
        order_kernel,
        in_specs=[vmem()],
        out_specs=pl.BlockSpec(memory_space=pl.ANY),
        out_shape=jax.ShapeDtypeStruct((8, CH, 16, 128), jnp.bfloat16),
        scratch_shapes=[
            pltpu.VMEM((8, CH, 16, 128), jnp.bfloat16),
            pltpu.SemaphoreType.DMA((CHUNKS,)),
        ],
        compiler_params=vmem_params(),
        cost_estimate=pl.CostEstimate(
            flops=600_000_000, bytes_accessed=5_300_000, transcendentals=0
        ),
    )(cells)


def ring(cells, step):
    count = lax.axis_size("space")
    return lax.ppermute(cells, "space", [(i, (i + step) % count) for i in range(count)])


def depth_ring(cells, step):
    return lax.ppermute(
        cells, "mem", [(4 * y + (z + step) % 4, 4 * y + z) for y in range(2) for z in range(4)]
    )


def per_device(
    prior_ensemble,
    initial_kernel_taps,
    latter_kernel_taps,
    observed_cells,
    observed_count,
    local_radius,
    observed_value,
    error_variance,
):
    members = prior_ensemble.shape[0]
    bf16 = jnp.bfloat16
    own = jnp.swapaxes(prior_ensemble, 1, 2).reshape(members, 16 * CH, 128)
    cells = observed_cells.reshape(8, 128)
    digits = jnp.stack([cells // 6144, cells // 128 % 48, cells % 128]).reshape(24, 128).astype(bf16)
    digits = jnp.concatenate([digits, jnp.zeros((8, 128), bf16)])
    tail = own[:, (16 - HALO) * CH :].reshape(-1, 128)
    head = own[:, : HALO * CH].reshape(-1, 128)
    left = ring(jnp.concatenate([tail, digits]), 1)
    right = ring(jnp.concatenate([head, digits]), -1)

    inner, halves, rates, first, second = inner_forecast(
        own, initial_kernel_taps, latter_kernel_taps
    )
    inner_parts = lax.all_to_all(inner, "mem", split_axis=0, concat_axis=0, tiled=True)
    edge, picked = edge_forecast(inner, cells, first, second, left, right, own, halves, rates)
    edge_parts = lax.all_to_all(edge, "mem", split_axis=0, concat_axis=0, tiled=True)

    picked = picked.reshape(3, 8, 8, 128)
    from_left = ring(picked[2], 1)
    from_right = ring(picked[0], -1)
    part = (cells // 128 % 48 // 16).reshape(8, 1, 128)
    here = jnp.where(part == 0, from_left, jnp.where(part == 1, picked[1], from_right))
    pair = lax.ppermute(here, "mem", [(i, i ^ 4) for i in range(8)])
    both = jnp.stack([here, pair])
    group = lax.axis_index("mem").astype(jnp.int32)
    numbers = jnp.stack([group % 4, group // 4, observed_count[0], local_radius[0]])
    weights = transform_of(
        (here, pair, depth_ring(both, 1), depth_ring(both, 2), depth_ring(both, 3)),
        observed_cells,
        numbers,
        observed_value,
        error_variance,
    )
    mixed = mix(inner_parts, edge_parts, weights)
    back = lax.all_to_all(mixed, "mem", split_axis=0, concat_axis=0, tiled=True)
    return order(back.reshape(16, CH, 8, 128))


def solution(mesh):
    return jax.shard_map(
        per_device,
        mesh=mesh,
        in_specs=(
            P("mem", None, "space", None),
            P(),
            P(),
            P("space", None),
            P("space"),
            P("space"),
            P("space", None),
            P("space", None),
        ),
        out_specs=P("mem", None, "space", None),
        check_vma=False,
    )
```

```python
import jax
import jax.numpy as jnp
from jax import lax
from jax.experimental import pallas as pl
from jax.experimental.pallas import tpu as pltpu
from jax.sharding import PartitionSpec as P

NS_ITERS = 4
STEP_SIZE = 0.5
HALO = 4
CH = 80
PAIR_A = 4
PAIR_B = 8
LAG = 3


def vmem_params():
    return pltpu.CompilerParams(vmem_limit_bytes=40 << 20)


def gelu(x):
    c = 0.7978845608028654
    return 0.5 * x * (1.0 + jnp.tanh(c * (x + 0.044715 * (x * x * x))))


def shifted_sum(p, lane):
    below = pltpu.roll(p[0:80], 1, axis=1)
    above = pltpu.roll(p[160:240], 127, axis=1)
    return p[80:160] + jnp.where(lane == 0, 0.0, below) + jnp.where(lane == 127, 0.0, above)


def conv_pair(source, at, taps, emit, k):
    lane = lax.broadcasted_iota(jnp.int32, (CH, 128), 1)
    window = jnp.concatenate(
        [source[pl.ds(CH * at, 3 * CH), :], source[pl.ds(CH * (at + 1), 3 * CH), :]], axis=1
    )
    partial = jnp.dot(taps, window, preferred_element_type=jnp.float32)
    emit(k, shifted_sum(partial[:, :128], lane))
    emit(k + 1, shifted_sum(partial[:, 128:], lane))


def build_taps(taps, matrix):
    for b in range(3):
        row = jnp.concatenate([taps[3 * a + b].astype(jnp.float32) for a in range(3)], axis=1)
        matrix[pl.ds(CH * b, CH), :] = row.astype(jnp.bfloat16)


def run_interleaved(jobs):
    for _, step in sorted(jobs, key=lambda job: job[0]):
        step()


def inner_kernel(
    own, first_taps, second_taps, out, halves, rates, edges, taps_out,
    taps, h, s, g, rate, fields, cells16, sems,
):
    members = own.shape[0]
    build_taps(first_taps, taps.at[0])
    build_taps(second_taps, taps.at[1])
    a = taps[0]
    b = taps[1]
    copies = [
        pltpu.make_async_copy(own.at[:, pl.ds(0, 4 * CH)], edges.at[:, pl.ds(0, 4 * CH)], sems.at[0]),
        pltpu.make_async_copy(own.at[:, pl.ds(12 * CH, 4 * CH)], edges.at[:, pl.ds(4 * CH, 4 * CH)], sems.at[1]),
        pltpu.make_async_copy(taps, taps_out, sems.at[2]),
    ]
    for copy in copies:
        copy.start()

    def group(n, carry):
        jobs = []
        for i in range(PAIR_A):
            m = n * PAIR_A + i
            v, hm, sm, gm, rm = own.at[m], h.at[m], s.at[m], g.at[m], rate.at[m]

            def put_first(k, value, hm=hm):
                hm[pl.ds(CH * k, CH), :] = gelu(value).astype(jnp.bfloat16)

            def put_section(k, value, v=v, sm=sm, rm=rm):
                base = v[pl.ds(CH * (k + 2), CH), :].astype(jnp.float32)
                sm[pl.ds(CH * k, CH), :] = (base + STEP_SIZE * value).astype(jnp.bfloat16)
                rm[pl.ds(CH * k, CH), :] = base + 0.5 * STEP_SIZE * value

            def put_second(k, value, gm=gm):
                gm[pl.ds(CH * k, CH), :] = gelu(value).astype(jnp.bfloat16)

            def put_forecast(k, value, rm=rm, m=m):
                cells = rm[pl.ds(CH * (k + 2), CH), :] + 0.5 * STEP_SIZE * value
                fields[pl.ds(8 * CH * k + m, CH, stride=8), :] = cells

            stages = ((v, a, 14, put_first), (hm, b, 12, put_section), (sm, a, 10, put_second), (gm, b, 8, put_forecast))
            for level, (source, matrix, columns, emit) in enumerate(stages):
                for k in range(0, columns, 2):
                    jobs.append(((k // 2 + LAG * level, i, level), lambda source=source, k=k, matrix=matrix, emit=emit: conv_pair(source, k, matrix, emit, k)))
        run_interleaved(jobs)
        return carry

    lax.fori_loop(0, members // PAIR_A, group, 0)
    for k, (ref, right) in enumerate(((h, 12), (s, 10), (g, 8))):
        for side, at in enumerate((0, right)):
            copies.append(pltpu.make_async_copy(
                ref.at[:, pl.ds(CH * at, 2 * CH)],
                halves.at[:, pl.ds(2 * CH * (k + 3 * side), 2 * CH)],
                sems.at[3 + 2 * k + side],
            ))
    for side, at in enumerate((0, 10)):
        copies.append(pltpu.make_async_copy(
            rate.at[:, pl.ds(CH * at, 2 * CH)], rates.at[:, pl.ds(2 * CH * side, 2 * CH)], sems.at[9 + side]
        ))
    for copy in copies[3:]:
        copy.start()
    cells16[...] = fields[...].astype(jnp.bfloat16).reshape(out.shape)
    last = pltpu.make_async_copy(cells16, out, sems.at[11])
    last.start()
    for copy in copies:
        copy.wait()
    last.wait()


def vmem():
    return pl.BlockSpec(memory_space=pltpu.VMEM)

def hbm():
    return pl.BlockSpec(memory_space=pltpu.HBM)

def inner_forecast(own, first_taps, second_taps):
    members = own.shape[0]
    bf16, f32 = jnp.bfloat16, jnp.float32
    return pl.pallas_call(
        inner_kernel,
        in_specs=[vmem()] * 3,
        out_specs=[hbm()] * 5,
        out_shape=[
            jax.ShapeDtypeStruct((8, CH, 8, 128), bf16),
            jax.ShapeDtypeStruct((members, 12 * CH, 128), bf16),
            jax.ShapeDtypeStruct((members, 4 * CH, 128), f32),
            jax.ShapeDtypeStruct((members, 8 * CH, 128), bf16),
            jax.ShapeDtypeStruct((2, 3 * CH, 3 * CH), bf16),
        ],
        scratch_shapes=[
            pltpu.VMEM((2, 3 * CH, 3 * CH), bf16),
            pltpu.VMEM((members, 14 * CH, 128), bf16),
            pltpu.VMEM((members, 12 * CH, 128), bf16),
            pltpu.VMEM((members, 10 * CH, 128), bf16),
            pltpu.VMEM((members, 12 * CH, 128), f32),
            pltpu.VMEM((64 * CH, 128), f32),
            pltpu.VMEM((8, CH, 8, 128), bf16),
            pltpu.SemaphoreType.DMA((12,)),
        ],
        compiler_params=vmem_params(),
        cost_estimate=pl.CostEstimate(
            flops=12_000_000_000, bytes_accessed=8_000_000, transcendentals=2_000_000
        ),
    )(own, first_taps, second_taps)


def place_of(channel, lon, lat, part):
    slot = lax.broadcasted_iota(jnp.int32, (8, 128), 1)
    lon = lon - 16 * part
    column = jnp.where(lon < 4, lon + 8, jnp.where(lon < 12, lon - 4, lon))
    here = (lon >= 0) & (lon < 16)
    return jnp.where(here, (column * CH + channel) * 8, 0), (slot - lat) & 127


def edge_kernel(
    inner, cells, taps_in, left, right, edges, halves, rates, out, picked,
    taps, v, h, s, g, rate, rated, fields, cells16, inner16, lists, drawn, places, rows, turns, sems, list_sems, out_sems, place_sems,
):
    members = edges.shape[0]
    halo = CH * HALO
    digits = halo * members

    def loads(n):
        at = pl.ds(n * PAIR_B, PAIR_B)
        parts = []
        for i in range(PAIR_B):
            m = n * PAIR_B + i
            spot = pl.ds(pl.multiple_of(halo * m, halo), halo)
            parts.append((left.at[spot], v.at[m, pl.ds(0, 4 * CH)]))
            parts.append((right.at[spot], v.at[m, pl.ds(12 * CH, 4 * CH)]))
        parts.append((edges.at[at], v.at[at, pl.ds(4 * CH, 8 * CH)]))
        for k, ref in enumerate((h, s, g)):
            for side in range(2):
                parts.append((
                    halves.at[at, pl.ds(2 * CH * (k + 3 * side), 2 * CH)],
                    ref.at[at, pl.ds((4 + 2 * side) * CH, 2 * CH)],
                ))
        parts.append((rates.at[at], rated.at[at]))
        return [
            pltpu.make_async_copy(source, target, sems.at[n, i])
            for i, (source, target) in enumerate(parts)
        ]

    groups = members // PAIR_B
    firsts = [pltpu.make_async_copy(taps_in, taps, list_sems.at[0])]
    for i, source in enumerate((left, right)):
        firsts.append(pltpu.make_async_copy(source.at[pl.ds(digits, 32)], lists.at[i], list_sems.at[1 + i]))
    for copy in firsts:
        copy.start()
    for n in range(groups):
        for copy in loads(n):
            copy.start()
    inner_copy = pltpu.make_async_copy(inner, inner16, list_sems.at[3])
    inner_copy.start()
    for copy in firsts:
        copy.wait()
    for k in range(3):
        if k == 1:
            cell = cells[...]
            strip = cell >> 7
            channel = (strip * 43691) >> 21
            parts = (channel, strip - 48 * channel, cell & 127)
        else:
            block = lists[k // 2].astype(jnp.float32).astype(jnp.int32)
            parts = (block[0:8], block[8:16], block[16:24])
        row, turn = place_of(*parts, 2 - k)
        places[0, pl.ds(8 * k, 8), :] = row
        places[1, pl.ds(8 * k, 8), :] = turn
    place_copies = [
        pltpu.make_async_copy(places.at[0], rows, place_sems.at[0]),
        pltpu.make_async_copy(places.at[1], turns, place_sems.at[1]),
    ]
    for copy in place_copies:
        copy.start()
    a = taps[0]
    b = taps[1]

    def group(n, carry):
        for copy in loads(n):
            copy.wait()
        jobs = []
        for i in range(PAIR_B):
            m = n * PAIR_B + i
            vm, hm, sm, gm, rm, rdm = v.at[m], h.at[m], s.at[m], g.at[m], rate.at[m], rated.at[m]

            def hidden(ref, at):
                def put(k, value):
                    ref[pl.ds(CH * (at + k), CH), :] = gelu(value).astype(jnp.bfloat16)

                return put

            def section_left(k, value, vm=vm, sm=sm, rm=rm):
                base = vm[pl.ds(CH * (k + 2), CH), :].astype(jnp.float32)
                sm[pl.ds(CH * k, CH), :] = (base + STEP_SIZE * value).astype(jnp.bfloat16)
                if k >= 2:
                    rm[pl.ds(CH * (k - 2), CH), :] = base + 0.5 * STEP_SIZE * value

            def section_right(k, value, vm=vm, sm=sm, rm=rm):
                base = vm[pl.ds(CH * (k + 10), CH), :].astype(jnp.float32)
                sm[pl.ds(CH * (8 + k), CH), :] = (base + STEP_SIZE * value).astype(jnp.bfloat16)
                if k < 2:
                    rm[pl.ds(CH * (k + 2), CH), :] = base + 0.5 * STEP_SIZE * value

            def put_field(column, start, value, m):
                value = (start + 0.5 * STEP_SIZE * value).astype(jnp.bfloat16).astype(jnp.float32)
                fields[pl.ds(8 * CH * (8 + column) + m, CH, stride=8), :] = value

            def forecast_left(k, value, rm=rm, rdm=rdm, m=m):
                start = rm[pl.ds(CH * k, CH), :] if k < 2 else rdm[pl.ds(CH * (k - 2), CH), :]
                put_field(k, start, value, m)

            def forecast_right(k, value, rm=rm, rdm=rdm, m=m):
                start = rdm[pl.ds(CH * (k + 2), CH), :] if k < 2 else rm[pl.ds(CH * k, CH), :]
                put_field(k + 4, start, value, m)

            stages = (
                (vm, 0, a, hidden(hm, 0)), (vm, 10, a, hidden(hm, 8)),
                (hm, 0, b, section_left), (hm, 6, b, section_right),
                (sm, 0, a, hidden(gm, 0)), (sm, 6, a, hidden(gm, 8)),
                (gm, 0, b, forecast_left), (gm, 6, b, forecast_right),
            )
            for level, (source, at, matrix, emit) in enumerate(stages):
                for k in (0, 2):
                    jobs.append(((level // 2, i, level, k), lambda source=source, at=at, k=k, matrix=matrix, emit=emit: conv_pair(source, at + k, matrix, emit, k)))
        run_interleaved(jobs)
        return carry

    lax.fori_loop(0, groups, group, 0)
    cells16[...] = fields[pl.ds(64 * CH, 64 * CH), :].astype(jnp.bfloat16).reshape(out.shape)
    out_copy = pltpu.make_async_copy(cells16, out, out_sems.at[0])
    out_copy.start()
    inner_copy.wait()
    fields[pl.ds(0, 64 * CH), :] = inner16[...].astype(jnp.float32).reshape(64 * CH, 128)
    for copy in place_copies:
        copy.wait()
    lane = lax.broadcasted_iota(jnp.int32, (8, 128), 1)

    def block(k, carry):
        acc = jnp.zeros((8, 128), jnp.float32)
        for j in range(128):
            cell = fields[pl.ds(pl.multiple_of(rows[k, j], 8), 8), :]
            acc = jnp.where(lane == j, pltpu.roll(cell, turns[k, j], axis=1), acc)
        drawn[k] = acc.astype(jnp.bfloat16)
        return carry

    lax.fori_loop(0, drawn.shape[0], block, 0)
    drawn_copy = pltpu.make_async_copy(drawn, picked, out_sems.at[1])
    drawn_copy.start()
    drawn_copy.wait()
    out_copy.wait()


def edge_forecast(inner, cells, taps, left, right, edges, halves, rates):
    bf16, f32 = jnp.bfloat16, jnp.float32
    members = edges.shape[0]
    return pl.pallas_call(
        edge_kernel,
        in_specs=[hbm(), vmem()] + [hbm()] * 6,
        out_specs=[hbm()] * 2,
        out_shape=[
            jax.ShapeDtypeStruct((8, CH, 8, 128), bf16),
            jax.ShapeDtypeStruct((24, 8, 128), bf16),
        ],
        scratch_shapes=[
            pltpu.VMEM((2, 3 * CH, 3 * CH), bf16),
            pltpu.VMEM((members, 16 * CH, 128), bf16),
            pltpu.VMEM((members, 12 * CH, 128), bf16),
            pltpu.VMEM((members, 12 * CH, 128), bf16),
            pltpu.VMEM((members, 12 * CH, 128), bf16),
            pltpu.VMEM((members, 4 * CH, 128), f32),
            pltpu.VMEM((members, 4 * CH, 128), f32),
            pltpu.VMEM((128 * CH, 128), f32),
            pltpu.VMEM((8, CH, 8, 128), bf16),
            pltpu.VMEM((8, CH, 8, 128), bf16),
            pltpu.VMEM((2, 32, 128), bf16),
            pltpu.VMEM((24, 8, 128), bf16),
            pltpu.VMEM((2, 24, 128), jnp.int32),
            pltpu.SMEM((24, 128), jnp.int32),
            pltpu.SMEM((24, 128), jnp.int32),
            pltpu.SemaphoreType.DMA((members // PAIR_B, 8 + 2 * PAIR_B)),
            pltpu.SemaphoreType.DMA((4,)),
            pltpu.SemaphoreType.DMA((2,)),
            pltpu.SemaphoreType.DMA((2,)),
        ],
        compiler_params=vmem_params(),
        cost_estimate=pl.CostEstimate(
            flops=9_000_000_000, bytes_accessed=8_000_000, transcendentals=2_000_000
        ),
    )(inner, cells, taps, left, right, edges, halves, rates)


def transform_kernel(here, pair, ahead, across, behind, cells, numbers, observed, variance, out, stack):
    f32 = jnp.float32
    exact = lax.Precision.HIGHEST
    depth = numbers[0]
    half = numbers[1]
    for z in range(4):
        step = (z - depth) & 3
        for y in range(2):
            other = (y ^ half) & 1
            rows = pl.ds(8 * (4 * y + z), 8)
            for block in range(8):
                lanes = pl.ds(128 * block, 128)

                def take(ref, pick=None):
                    return ref[other, block].astype(f32)

                value = jnp.where(
                    step == 0,
                    jnp.where(other == 0, here[block].astype(f32), pair[block].astype(f32)),
                    jnp.where(step == 1, take(ahead), jnp.where(step == 2, take(across), take(behind))),
                )
                stack[rows, lanes] = value
    model_obs = stack[...]
    center = jnp.sum(model_obs, axis=0, keepdims=True) * (1.0 / 64.0)
    spread = model_obs - center
    cell = cells[...]
    strip = cell >> 7
    lon = strip - 48 * ((strip * 43691) >> 21)
    scaled = (lon.astype(f32) - 23.5) / numbers[3].astype(f32)
    taper = jnp.exp(-0.5 * scaled * scaled)
    slot = lax.broadcasted_iota(jnp.int32, cell.shape, 1)
    weight = jnp.where(slot < numbers[2], taper / variance[...], 0.0)
    weighted = spread * weight

    def product(x, y):
        return jnp.dot(x, y, precision=exact, preferred_element_type=f32)

    gram = lax.dot_general(
        weighted, spread, (((1,), (1,)), ((), ())), precision=exact, preferred_element_type=f32
    )
    right_side = jnp.sum(weighted * (observed[...] - center), axis=1, keepdims=True)
    i = lax.broadcasted_iota(jnp.int32, (64, 64), 0)
    j = lax.broadcasted_iota(jnp.int32, (64, 64), 1)
    eye = jnp.where(i == j, 1.0, 0.0).astype(f32)
    norm = 63.0 + jnp.sqrt(jnp.sum(jnp.sum(gram * gram, axis=1, keepdims=True), axis=0, keepdims=True))
    iterate = (63.0 * eye + gram) / norm
    root = 1.5 * eye - 0.5 * iterate
    iterate = product(iterate, root)
    for sweep in range(1, NS_ITERS):
        factor = 1.5 * eye - 0.5 * product(root, iterate)
        if sweep < NS_ITERS - 1:
            iterate = product(iterate, factor)
        root = product(factor, root)
    wide = jnp.broadcast_to(right_side, (64, 128))
    shift = product(root, product(root, wide)) / norm
    transform = (shift[:, :64] + jnp.sqrt(63.0 / norm) * root).astype(jnp.bfloat16)
    i = lax.broadcasted_iota(jnp.int32, (64, 256), 0)
    j = lax.broadcasted_iota(jnp.int32, (64, 256), 1)
    for q in range(4):
        place = jnp.where(j == i + 64 * q, 1.0, 0.0).astype(jnp.bfloat16)
        turned = lax.dot_general(
            transform, place, (((0,), (0,)), ((), ())), preferred_element_type=f32
        )
        out[pl.ds(64 * q, 64), :] = turned.astype(jnp.bfloat16)


def transform_of(pieces, cells, numbers, observed, variance):
    smem = pl.BlockSpec(memory_space=pltpu.SMEM)
    return pl.pallas_call(
        transform_kernel,
        in_specs=[vmem()] * 6 + [smem] + [vmem()] * 2,
        out_specs=vmem(),
        out_shape=jax.ShapeDtypeStruct((256, 256), jnp.bfloat16),
        scratch_shapes=[pltpu.VMEM((64, 1024), jnp.float32)],
        compiler_params=vmem_params(),
        cost_estimate=pl.CostEstimate(
            flops=100_000_000, bytes_accessed=500_000, transcendentals=1000
        ),
    )(*pieces, cells, numbers, observed, variance)


def mix_kernel(inner, edge, weights, out, cells, sems):
    w = weights[...]
    blocks = CH // 8
    copies = []
    for k in range(blocks):
        for x, parts in enumerate((inner, edge)):
            copy = pltpu.make_async_copy(
                parts.at[:, pl.ds(8 * k, 8)], cells.at[x, k], sems.at[x, k]
            )
            copy.start()
            copies.append(copy)
    for k in range(blocks):
        for x in range(2):
            copies[2 * k + x].wait()
            centers = []
            halves = []
            for half in range(2):
                stack = []
                for q in range(4):
                    value = cells[x, k, :, 4 * half + q].astype(jnp.float32)
                    center = jnp.sum(jnp.sum(value, axis=0), axis=0, keepdims=True) * (1.0 / 64.0)
                    centers.append(center)
                    stack.append((value.reshape(64, 128) - center).astype(jnp.bfloat16))
                halves.append(jnp.concatenate(stack, axis=0))
            mixed = jnp.dot(
                w, jnp.concatenate(halves, axis=1), preferred_element_type=jnp.float32
            )
            for half in range(2):
                for q in range(4):
                    value = mixed[64 * q : 64 * q + 64, 128 * half : 128 * half + 128]
                    value = value + centers[4 * half + q]
                    out[:, x, 8 * k + 4 * half + q] = value.astype(jnp.bfloat16).reshape(8, 8, 128)


def mix(inner, edge, weights):
    return pl.pallas_call(
        mix_kernel,
        in_specs=[pl.BlockSpec(memory_space=pl.ANY)] * 2 + [vmem()],
        out_specs=vmem(),
        out_shape=jax.ShapeDtypeStruct((8, 2, CH, 8, 128), jnp.bfloat16),
        scratch_shapes=[
            pltpu.VMEM((2, CH // 8, 8, 8, 8, 128), jnp.bfloat16),
            pltpu.SemaphoreType.DMA((2, CH // 8)),
        ],
        compiler_params=vmem_params(),
        cost_estimate=pl.CostEstimate(
            flops=700_000_000, bytes_accessed=5_300_000, transcendentals=0
        ),
    )(inner, edge, weights)


CHUNKS = 5


def order_kernel(cells, out, scratch, sems):
    to = lax.broadcasted_iota(jnp.int32, (128, 128), 0)
    at = lax.broadcasted_iota(jnp.int32, (128, 128), 1)
    source = at >> 4
    side = (at >> 3) & 1
    column = jnp.where(side == 0, source + 4, jnp.where(source < 4, source, source + 8))
    move = jnp.where(to == (at & 7) * 16 + column, 1.0, 0.0).astype(jnp.bfloat16)
    depth = CH // CHUNKS
    copies = []
    for chunk in range(CHUNKS):
        for c in range(depth * chunk, depth * (chunk + 1), 2):
            both = jnp.concatenate(
                [cells[:, c].reshape(128, 128), cells[:, c + 1].reshape(128, 128)], axis=1
            )
            moved = jnp.dot(move, both, preferred_element_type=jnp.float32).astype(jnp.bfloat16)
            scratch[:, c] = moved[:, :128].reshape(8, 16, 128)
            scratch[:, c + 1] = moved[:, 128:].reshape(8, 16, 128)
        rows = pl.ds(depth * chunk, depth)
        copy = pltpu.make_async_copy(scratch.at[:, rows], out.at[:, rows], sems.at[chunk])
        copy.start()
        copies.append(copy)
    for copy in copies:
        copy.wait()


def order(cells):
    return pl.pallas_call(
        order_kernel,
        in_specs=[vmem()],
        out_specs=pl.BlockSpec(memory_space=pl.ANY),
        out_shape=jax.ShapeDtypeStruct((8, CH, 16, 128), jnp.bfloat16),
        scratch_shapes=[
            pltpu.VMEM((8, CH, 16, 128), jnp.bfloat16),
            pltpu.SemaphoreType.DMA((CHUNKS,)),
        ],
        compiler_params=vmem_params(),
        cost_estimate=pl.CostEstimate(
            flops=600_000_000, bytes_accessed=5_300_000, transcendentals=0
        ),
    )(cells)


def ring(cells, step):
    count = lax.axis_size("space")
    return lax.ppermute(cells, "space", [(i, (i + step) % count) for i in range(count)])


def depth_ring(cells, step):
    return lax.ppermute(
        cells, "mem", [(4 * y + (z + step) % 4, 4 * y + z) for y in range(2) for z in range(4)]
    )


def per_device(
    prior_ensemble,
    initial_kernel_taps,
    latter_kernel_taps,
    observed_cells,
    observed_count,
    local_radius,
    observed_value,
    error_variance,
):
    members = prior_ensemble.shape[0]
    bf16 = jnp.bfloat16
    own = jnp.swapaxes(prior_ensemble, 1, 2).reshape(members, 16 * CH, 128)
    cells = observed_cells.reshape(8, 128)
    digits = jnp.stack([cells // 6144, cells // 128 % 48, cells % 128]).reshape(24, 128).astype(bf16)
    digits = jnp.concatenate([digits, jnp.zeros((8, 128), bf16)])
    tail = own[:, (16 - HALO) * CH :].reshape(-1, 128)
    head = own[:, : HALO * CH].reshape(-1, 128)
    left = ring(jnp.concatenate([tail, digits]), 1)
    right = ring(jnp.concatenate([head, digits]), -1)

    inner, halves, rates, edges, taps = inner_forecast(
        own, initial_kernel_taps, latter_kernel_taps
    )
    inner_parts = lax.all_to_all(inner, "mem", split_axis=0, concat_axis=0, tiled=True)
    edge, picked = edge_forecast(inner, cells, taps, left, right, edges, halves, rates)
    edge_parts = lax.all_to_all(edge, "mem", split_axis=0, concat_axis=0, tiled=True)

    picked = picked.reshape(3, 8, 8, 128)
    from_left = ring(picked[2], 1)
    from_right = ring(picked[0], -1)
    part = (cells // 128 % 48 // 16).reshape(8, 1, 128)
    here = jnp.where(part == 0, from_left, jnp.where(part == 1, picked[1], from_right))
    pair = lax.ppermute(here, "mem", [(i, i ^ 4) for i in range(8)])
    both = jnp.stack([here, pair])
    group = lax.axis_index("mem").astype(jnp.int32)
    numbers = jnp.stack([group % 4, group // 4, observed_count[0], local_radius[0]])
    weights = transform_of(
        (here, pair, depth_ring(both, 1), depth_ring(both, 2), depth_ring(both, 3)),
        observed_cells,
        numbers,
        observed_value,
        error_variance,
    )
    mixed = mix(inner_parts, edge_parts, weights)
    back = lax.all_to_all(mixed, "mem", split_axis=0, concat_axis=0, tiled=True)
    return order(back.reshape(16, CH, 8, 128))


def solution(mesh):
    return jax.shard_map(
        per_device,
        mesh=mesh,
        in_specs=(
            P("mem", None, "space", None),
            P(),
            P(),
            P("space", None),
            P("space"),
            P("space"),
            P("space", None),
            P("space", None),
        ),
        out_specs=P("mem", None, "space", None),
        check_vma=False,
    )
```

```python
import functools

import jax
import jax.numpy as jnp
from jax import lax
from jax.experimental import pallas as pl
from jax.experimental.pallas import tpu as pltpu
from jax.sharding import PartitionSpec as P

NS_ITERS = 4
STEP_SIZE = 0.5
HALO = 4
CH = 80
PAIR_A = 4
LAG = 3


def vmem_params():
    return pltpu.CompilerParams(vmem_limit_bytes=40 << 20)


def gelu(x):
    c = 0.7978845608028654
    return 0.5 * x * (1.0 + jnp.tanh(c * (x + 0.044715 * (x * x * x))))


def shifted_sum(p, lane):
    below = pltpu.roll(p[0:80], 1, axis=1)
    above = pltpu.roll(p[160:240], 127, axis=1)
    return p[80:160] + jnp.where(lane == 0, 0.0, below) + jnp.where(lane == 127, 0.0, above)


def conv_pair(source, at, taps, emit, k):
    lane = lax.broadcasted_iota(jnp.int32, (CH, 128), 1)
    window = jnp.concatenate(
        [source[pl.ds(CH * at, 3 * CH), :], source[pl.ds(CH * (at + 1), 3 * CH), :]], axis=1
    )
    partial = jnp.dot(taps, window, preferred_element_type=jnp.float32)
    emit(k, shifted_sum(partial[:, :128], lane))
    emit(k + 1, shifted_sum(partial[:, 128:], lane))


def build_taps(taps, matrix):
    for b in range(3):
        row = jnp.concatenate([taps[3 * a + b].astype(jnp.float32) for a in range(3)], axis=1)
        matrix[pl.ds(CH * b, CH), :] = row.astype(jnp.bfloat16)


def run_interleaved(jobs):
    for _, step in sorted(jobs, key=lambda job: job[0]):
        step()


def inner_kernel(
    own, first_taps, second_taps, out, left_halves, left_rates, right_halves, right_rates, taps_out,
    taps, h, s, g, rate, fields, cells16, sems,
):
    members = own.shape[0]
    build_taps(first_taps, taps.at[0])
    build_taps(second_taps, taps.at[1])
    a = taps[0]
    b = taps[1]
    copies = [
        pltpu.make_async_copy(taps, taps_out, sems.at[0]),
        pltpu.make_async_copy(
            own.at[:, pl.ds(12 * CH, 4 * CH)], right_halves.at[:, pl.ds(6 * CH, 4 * CH)], sems.at[1]
        ),
    ]
    for copy in copies:
        copy.start()

    def group(n, carry):
        jobs = []
        for i in range(PAIR_A):
            m = n * PAIR_A + i
            v, hm, sm, gm, rm = own.at[m], h.at[m], s.at[m], g.at[m], rate.at[m]

            def put_first(k, value, hm=hm):
                hm[pl.ds(CH * k, CH), :] = gelu(value).astype(jnp.bfloat16)

            def put_section(k, value, v=v, sm=sm, rm=rm):
                base = v[pl.ds(CH * (k + 2), CH), :].astype(jnp.float32)
                sm[pl.ds(CH * k, CH), :] = (base + STEP_SIZE * value).astype(jnp.bfloat16)
                rm[pl.ds(CH * k, CH), :] = base + 0.5 * STEP_SIZE * value

            def put_second(k, value, gm=gm):
                gm[pl.ds(CH * k, CH), :] = gelu(value).astype(jnp.bfloat16)

            def put_forecast(k, value, rm=rm, m=m):
                cells = rm[pl.ds(CH * (k + 2), CH), :] + 0.5 * STEP_SIZE * value
                fields[pl.ds(8 * CH * k + m, CH, stride=8), :] = cells

            stages = (
                (v, a, 14, put_first),
                (hm, b, 12, put_section),
                (sm, a, 10, put_second),
                (gm, b, 8, put_forecast),
            )
            for level, (source, matrix, columns, emit) in enumerate(stages):
                for k in range(0, columns, 2):
                    step = functools.partial(conv_pair, source, k, matrix, emit, k)
                    jobs.append(((k // 2 + LAG * level, i, level), step))
        run_interleaved(jobs)
        return carry

    lax.fori_loop(0, members // PAIR_A, group, 0)
    for k, (ref, at) in enumerate(((h, 12), (s, 10), (g, 8))):
        target = pl.ds(2 * CH * k, 2 * CH)
        copies.append(
            pltpu.make_async_copy(ref.at[:, pl.ds(0, 2 * CH)], left_halves.at[:, target], sems.at[2 + k])
        )
        copies.append(
            pltpu.make_async_copy(
                ref.at[:, pl.ds(CH * at, 2 * CH)], right_halves.at[:, target], sems.at[5 + k]
            )
        )
    pair = pl.ds(0, 2 * CH)
    copies.append(pltpu.make_async_copy(rate.at[:, pair], left_rates, sems.at[8]))
    copies.append(
        pltpu.make_async_copy(
            rate.at[:, pl.ds(CH * 10, 2 * CH)], right_rates.at[:, pair], sems.at[9]
        )
    )
    for copy in copies[2:]:
        copy.start()
    cells16[...] = fields[...].astype(jnp.bfloat16).reshape(cells16.shape)
    last = pltpu.make_async_copy(cells16, out.at[pl.ds(0, 8)], sems.at[10])
    last.start()
    for copy in copies:
        copy.wait()
    last.wait()


def vmem():
    return pl.BlockSpec(memory_space=pltpu.VMEM)


def anywhere():
    return pl.BlockSpec(memory_space=pl.ANY)


WIDE16 = 32768
WIDE32 = 16384


def inner_forecast(own, first_taps, second_taps):
    members = own.shape[0]
    bf16, f32 = jnp.bfloat16, jnp.float32
    return pl.pallas_call(
        inner_kernel,
        in_specs=[vmem()] * 3,
        out_specs=[anywhere()] * 6,
        out_shape=[
            jax.ShapeDtypeStruct((12, CH, 8, 128), bf16),
            jax.ShapeDtypeStruct((members, 6 * CH, 128), bf16),
            jax.ShapeDtypeStruct((members, 2 * CH, 128), f32),
            jax.ShapeDtypeStruct((members, WIDE16, 128), bf16),
            jax.ShapeDtypeStruct((members, WIDE32, 128), f32),
            jax.ShapeDtypeStruct((2, 3 * CH, 3 * CH), bf16),
        ],
        scratch_shapes=[
            pltpu.VMEM((2, 3 * CH, 3 * CH), bf16),
            pltpu.VMEM((members, 14 * CH, 128), bf16),
            pltpu.VMEM((members, 12 * CH, 128), bf16),
            pltpu.VMEM((members, 10 * CH, 128), bf16),
            pltpu.VMEM((members, 12 * CH, 128), f32),
            pltpu.VMEM((64 * CH, 128), f32),
            pltpu.VMEM((8, CH, 8, 128), bf16),
            pltpu.SemaphoreType.DMA((11,)),
        ],
        compiler_params=vmem_params(),
        cost_estimate=pl.CostEstimate(
            flops=12_000_000_000, bytes_accessed=8_000_000, transcendentals=2_000_000
        ),
    )(own, first_taps, second_taps)


def edge_loads(side, halves, rates, own, halo, v, h, s, g, rated, sems):
    members = v.shape[0]
    saved = 4 if side == 0 else 0
    copies = []
    for m in range(members):
        source = halo.at[pl.ds(CH * HALO * m, CH * HALO)]
        copies.append((source, v.at[m, pl.ds(0 if side == 0 else 4 * CH, 4 * CH)]))
    copies.append((own, v.at[:, pl.ds(4 * CH if side == 0 else 0, 4 * CH)]))
    for k, ref in enumerate((h, s, g)):
        copies.append((halves.at[:, pl.ds(2 * CH * k, 2 * CH)], ref.at[:, pl.ds(saved * CH, 2 * CH)]))
    copies.append((rates, rated))
    return [
        pltpu.make_async_copy(source, target, sems.at[i])
        for i, (source, target) in enumerate(copies)
    ]


def edge_columns(side, taps, v, h, s, g, rate, rated, fields, start):
    a = taps[0]
    b = taps[1]
    jobs = []
    made = 0 if side == 0 else 2
    for m in range(v.shape[0]):
        vm, hm, sm, gm, rm, rdm = v.at[m], h.at[m], s.at[m], g.at[m], rate.at[m], rated.at[m]

        def hidden(ref):
            def put(k, value):
                ref[pl.ds(CH * (made + k), CH), :] = gelu(value).astype(jnp.bfloat16)

            return put

        def section(k, value, vm=vm, sm=sm, rm=rm):
            base = vm[pl.ds(CH * (k + 2), CH), :].astype(jnp.float32)
            sm[pl.ds(CH * (made + k), CH), :] = (base + STEP_SIZE * value).astype(jnp.bfloat16)
            inside = k - 2 if side == 0 else k
            if 0 <= inside < 2:
                rm[pl.ds(CH * inside, CH), :] = base + 0.5 * STEP_SIZE * value

        def forecast(k, value, rm=rm, rdm=rdm, m=m):
            source = rm if (k < 2) == (side == 0) else rdm
            value = source[pl.ds(CH * (k % 2), CH), :] + 0.5 * STEP_SIZE * value
            value = value.astype(jnp.bfloat16).astype(jnp.float32)
            fields[pl.ds(start + 8 * CH * k + m, CH, stride=8), :] = value

        stages = (
            (vm, made, a, hidden(hm)),
            (hm, 0, b, section),
            (sm, 0, a, hidden(gm)),
            (gm, 0, b, forecast),
        )
        for level, (source, at, matrix, emit) in enumerate(stages):
            for k in (0, 2):
                step = functools.partial(conv_pair, source, at + k, matrix, emit, k)
                jobs.append(((level, m, k), step))
    run_interleaved(jobs)


def edge_scratch(members):
    bf16, f32 = jnp.bfloat16, jnp.float32
    return [
        pltpu.VMEM((members, 8 * CH, 128), bf16),
        pltpu.VMEM((members, 6 * CH, 128), bf16),
        pltpu.VMEM((members, 6 * CH, 128), bf16),
        pltpu.VMEM((members, 6 * CH, 128), bf16),
        pltpu.VMEM((members, 2 * CH, 128), f32),
        pltpu.VMEM((members, 2 * CH, 128), f32),
        pltpu.VMEM((4, CH, 8, 128), bf16),
        pltpu.SemaphoreType.DMA((members + 6,)),
    ]


def left_kernel(
    chunk, taps, halo, own, halves, rates, out, v, h, s, g, rate, rated, cells16, sems, fields
):
    copies = edge_loads(0, halves, rates, own.at[:, pl.ds(0, 4 * CH)], halo, v, h, s, g, rated, sems)
    for copy in copies:
        copy.start()
    for copy in copies:
        copy.wait()
    edge_columns(0, taps, v, h, s, g, rate, rated, fields, 0)
    cells16[...] = fields[...].astype(jnp.bfloat16).reshape(cells16.shape)
    last = pltpu.make_async_copy(cells16, out.at[pl.ds(8, 4)], sems.at[len(copies)])
    last.start()
    last.wait()


def left_forecast(chunk, taps, halo, own, halves, rates):
    members = own.shape[0]
    return pl.pallas_call(
        left_kernel,
        in_specs=[anywhere(), vmem()] + [anywhere()] * 4,
        out_specs=anywhere(),
        out_shape=jax.ShapeDtypeStruct((12, CH, 8, 128), jnp.bfloat16),
        scratch_shapes=edge_scratch(members) + [pltpu.VMEM((32 * CH, 128), jnp.float32)],
        input_output_aliases={0: 0},
        compiler_params=vmem_params(),
        cost_estimate=pl.CostEstimate(
            flops=5_000_000_000, bytes_accessed=4_000_000, transcendentals=1_000_000
        ),
    )(chunk, taps, halo, own, halves, rates)


def place_of(channel, lon, lat, part):
    slot = lax.broadcasted_iota(jnp.int32, (8, 128), 1)
    lon = lon - 16 * part
    column = jnp.where(lon < 4, lon + 8, jnp.where(lon < 12, lon - 4, lon))
    here = (lon >= 0) & (lon < 16)
    return jnp.where(here, (column * CH + channel) * 8, 0), (slot - lat) & 127


def right_kernel(
    chunk, cells, first_taps, second_taps, left, right, halves, rates, out, picked,
    v, h, s, g, rate, rated, cells16, sems, taps, fields, chunk16, lists, drawn, places, rows, turns, list_sems, place_sems,
):
    members = v.shape[0]
    digits = CH * HALO * members
    copies = edge_loads(
        1,
        halves,
        rates.at[:, pl.ds(0, 2 * CH)],
        halves.at[:, pl.ds(6 * CH, 4 * CH)],
        right, v, h, s, g, rated, sems,
    )
    list_copies = [
        pltpu.make_async_copy(source.at[pl.ds(digits, 32)], lists.at[i], list_sems.at[i])
        for i, source in enumerate((left, right))
    ]
    chunk_copy = pltpu.make_async_copy(chunk, chunk16, list_sems.at[2])
    for copy in list_copies + copies + [chunk_copy]:
        copy.start()
    build_taps(first_taps, taps.at[0])
    build_taps(second_taps, taps.at[1])
    for copy in list_copies:
        copy.wait()
    for k in range(3):
        if k == 1:
            cell = cells[...]
            strip = cell >> 7
            channel = (strip * 43691) >> 21
            parts = (channel, strip - 48 * channel, cell & 127)
        else:
            block = lists[k // 2].astype(jnp.float32).astype(jnp.int32)
            parts = (block[0:8], block[8:16], block[16:24])
        row, turn = place_of(*parts, 2 - k)
        places[0, pl.ds(8 * k, 8), :] = row
        places[1, pl.ds(8 * k, 8), :] = turn
    place_copies = [
        pltpu.make_async_copy(places.at[0], rows, place_sems.at[0]),
        pltpu.make_async_copy(places.at[1], turns, place_sems.at[1]),
    ]
    for copy in place_copies:
        copy.start()
    for copy in copies:
        copy.wait()
    edge_columns(1, taps, v, h, s, g, rate, rated, fields, 96 * CH)
    cells16[...] = fields[pl.ds(96 * CH, 32 * CH), :].astype(jnp.bfloat16).reshape(cells16.shape)
    out_copy = pltpu.make_async_copy(cells16, out, sems.at[len(copies)])
    out_copy.start()
    chunk_copy.wait()
    fields[pl.ds(0, 96 * CH), :] = chunk16[...].astype(jnp.float32).reshape(96 * CH, 128)
    for copy in place_copies:
        copy.wait()
    lane = lax.broadcasted_iota(jnp.int32, (8, 128), 1)

    def block(k, carry):
        acc = jnp.zeros((8, 128), jnp.float32)
        for j in range(128):
            cell = fields[pl.ds(pl.multiple_of(rows[k, j], 8), 8), :]
            acc = jnp.where(lane == j, pltpu.roll(cell, turns[k, j], axis=1), acc)
        drawn[k] = acc.astype(jnp.bfloat16)
        return carry

    lax.fori_loop(0, drawn.shape[0], block, 0)
    drawn_copy = pltpu.make_async_copy(drawn, picked, place_sems.at[2])
    drawn_copy.start()
    drawn_copy.wait()
    out_copy.wait()


def right_forecast(chunk, cells, first_taps, second_taps, left, right, halves, rates):
    bf16, f32 = jnp.bfloat16, jnp.float32
    members = halves.shape[0]
    return pl.pallas_call(
        right_kernel,
        in_specs=[anywhere()] + [vmem()] * 3 + [anywhere()] * 4,
        out_specs=[anywhere()] * 2,
        out_shape=[
            jax.ShapeDtypeStruct((4, CH, 8, 128), bf16),
            jax.ShapeDtypeStruct((24, 8, 128), bf16),
        ],
        scratch_shapes=edge_scratch(members) + [
            pltpu.VMEM((2, 3 * CH, 3 * CH), bf16),
            pltpu.VMEM((128 * CH, 128), f32),
            pltpu.VMEM((12, CH, 8, 128), bf16),
            pltpu.VMEM((2, 32, 128), bf16),
            pltpu.VMEM((24, 8, 128), bf16),
            pltpu.VMEM((2, 24, 128), jnp.int32),
            pltpu.SMEM((24, 128), jnp.int32),
            pltpu.SMEM((24, 128), jnp.int32),
            pltpu.SemaphoreType.DMA((3,)),
            pltpu.SemaphoreType.DMA((3,)),
        ],
        compiler_params=vmem_params(),
        cost_estimate=pl.CostEstimate(
            flops=5_000_000_000, bytes_accessed=8_000_000, transcendentals=1_000_000
        ),
    )(chunk, cells, first_taps, second_taps, left, right, halves, rates)


def transform_kernel(parts, cells, numbers, observed, variance, out, values, stack, sem):
    f32 = jnp.float32
    exact = lax.Precision.HIGHEST
    load = pltpu.make_async_copy(parts.at[:, pl.ds(40, 8)], values, sem)
    load.start()
    load.wait()
    for group in range(8):
        for block in range(8):
            stack[pl.ds(8 * group, 8), pl.ds(128 * block, 128)] = values[group, block].astype(f32)
    model_obs = stack[...]
    center = jnp.sum(model_obs, axis=0, keepdims=True) * (1.0 / 64.0)
    spread = model_obs - center
    cell = cells[...]
    strip = cell >> 7
    lon = strip - 48 * ((strip * 43691) >> 21)
    scaled = (lon.astype(f32) - 23.5) / numbers[1].astype(f32)
    taper = jnp.exp(-0.5 * scaled * scaled)
    slot = lax.broadcasted_iota(jnp.int32, cell.shape, 1)
    weight = jnp.where(slot < numbers[0], taper / variance[...], 0.0)
    weighted = spread * weight

    def product(x, y):
        return jnp.dot(x, y, precision=exact, preferred_element_type=f32)

    gram = lax.dot_general(
        weighted, spread, (((1,), (1,)), ((), ())), precision=exact, preferred_element_type=f32
    )
    right_side = jnp.sum(weighted * (observed[...] - center), axis=1, keepdims=True)
    i = lax.broadcasted_iota(jnp.int32, (64, 64), 0)
    j = lax.broadcasted_iota(jnp.int32, (64, 64), 1)
    eye = jnp.where(i == j, 1.0, 0.0).astype(f32)
    norm = 63.0 + jnp.sqrt(jnp.sum(jnp.sum(gram * gram, axis=1, keepdims=True), axis=0, keepdims=True))
    iterate = (63.0 * eye + gram) / norm
    root = 1.5 * eye - 0.5 * iterate
    iterate = product(iterate, root)
    for sweep in range(1, NS_ITERS):
        factor = 1.5 * eye - 0.5 * product(root, iterate)
        if sweep < NS_ITERS - 1:
            iterate = product(iterate, factor)
        root = product(factor, root)
    wide = jnp.broadcast_to(right_side, (64, 128))
    shift = product(root, product(root, wide)) / norm
    transform = (shift[:, :64] + jnp.sqrt(63.0 / norm) * root).astype(jnp.bfloat16)
    i = lax.broadcasted_iota(jnp.int32, (64, 256), 0)
    j = lax.broadcasted_iota(jnp.int32, (64, 256), 1)
    for q in range(4):
        place = jnp.where(j == i + 64 * q, 1.0, 0.0).astype(jnp.bfloat16)
        turned = lax.dot_general(
            transform, place, (((0,), (0,)), ((), ())), preferred_element_type=f32
        )
        out[pl.ds(64 * q, 64), :] = turned.astype(jnp.bfloat16)


def transform_of(parts, cells, numbers, observed, variance):
    smem = pl.BlockSpec(memory_space=pltpu.SMEM)
    return pl.pallas_call(
        transform_kernel,
        in_specs=[anywhere(), vmem(), smem, vmem(), vmem()],
        out_specs=vmem(),
        out_shape=jax.ShapeDtypeStruct((256, 256), jnp.bfloat16),
        scratch_shapes=[
            pltpu.VMEM((8, 8, 8, 128), jnp.bfloat16),
            pltpu.VMEM((64, 1024), jnp.float32),
            pltpu.SemaphoreType.DMA,
        ],
        compiler_params=vmem_params(),
        cost_estimate=pl.CostEstimate(
            flops=100_000_000, bytes_accessed=500_000, transcendentals=1000
        ),
    )(parts, cells, numbers, observed, variance)


def mix_rows(parts, first, w, out, start):
    centers = []
    halves = []
    for half in range(2):
        stack = []
        for q in range(4):
            value = parts[:, first + 4 * half + q].astype(jnp.float32)
            center = jnp.sum(jnp.sum(value, axis=0), axis=0, keepdims=True) * (1.0 / 64.0)
            centers.append(center)
            stack.append((value.reshape(64, 128) - center).astype(jnp.bfloat16))
        halves.append(jnp.concatenate(stack, axis=0))
    mixed = jnp.dot(w, jnp.concatenate(halves, axis=1), preferred_element_type=jnp.float32)
    for half in range(2):
        for q in range(4):
            value = mixed[64 * q : 64 * q + 64, 128 * half : 128 * half + 128]
            value = value + centers[4 * half + q]
            out[:, start + 4 * half + q] = value.astype(jnp.bfloat16).reshape(8, 8, 128)


def mix_kernel(first, second, weights, out):
    w = weights[...]

    def block(n, carry):
        for k in range(5):
            row = (5 * n + k) * 8
            mix_rows(first, row, w, out, row)
        return carry

    lax.fori_loop(0, 3, block, 0)
    for k in range(5):
        mix_rows(second, 8 * k, w, out, 120 + 8 * k)


def mix(first, second, weights):
    return pl.pallas_call(
        mix_kernel,
        in_specs=[vmem()] * 3,
        out_specs=vmem(),
        out_shape=jax.ShapeDtypeStruct((8, 160, 8, 128), jnp.bfloat16),
        compiler_params=vmem_params(),
        cost_estimate=pl.CostEstimate(
            flops=700_000_000, bytes_accessed=5_300_000, transcendentals=0
        ),
    )(first, second, weights)


CHUNKS = 5


def order_kernel(cells, out, scratch, sems):
    to = lax.broadcasted_iota(jnp.int32, (128, 128), 0)
    at = lax.broadcasted_iota(jnp.int32, (128, 128), 1)
    slot = at >> 3
    column = jnp.where(slot < 8, slot + 4, jnp.where(slot < 12, slot - 8, slot))
    move = jnp.where(to == (at & 7) * 16 + column, 1.0, 0.0).astype(jnp.bfloat16)

    def cell(i, c):
        if i < 12:
            return cells[(CH * i + c) // 120, (CH * i + c) % 120]
        return cells[(CH * (i - 12) + c) // 40, 120 + (CH * (i - 12) + c) % 40]

    def rows(c):
        return jnp.stack([cell(i, c) for i in range(16)]).reshape(128, 128)

    depth = CH // CHUNKS
    copies = []
    for chunk in range(CHUNKS):
        for c in range(depth * chunk, depth * (chunk + 1), 2):
            both = jnp.concatenate([rows(c), rows(c + 1)], axis=1)
            moved = jnp.dot(move, both, preferred_element_type=jnp.float32).astype(jnp.bfloat16)
            scratch[:, c] = moved[:, :128].reshape(8, 16, 128)
            scratch[:, c + 1] = moved[:, 128:].reshape(8, 16, 128)
        span = pl.ds(depth * chunk, depth)
        copy = pltpu.make_async_copy(scratch.at[:, span], out.at[:, span], sems.at[chunk])
        copy.start()
        copies.append(copy)
    for copy in copies:
        copy.wait()


def order(cells):
    return pl.pallas_call(
        order_kernel,
        in_specs=[vmem()],
        out_specs=anywhere(),
        out_shape=jax.ShapeDtypeStruct((8, CH, 16, 128), jnp.bfloat16),
        scratch_shapes=[
            pltpu.VMEM((8, CH, 16, 128), jnp.bfloat16),
            pltpu.SemaphoreType.DMA((CHUNKS,)),
        ],
        compiler_params=vmem_params(),
        cost_estimate=pl.CostEstimate(
            flops=600_000_000, bytes_accessed=5_300_000, transcendentals=0
        ),
    )(cells)


def ring(cells, step):
    count = lax.axis_size("space")
    return lax.ppermute(cells, "space", [(i, (i + step) % count) for i in range(count)])


def per_device(
    prior_ensemble,
    initial_kernel_taps,
    latter_kernel_taps,
    observed_cells,
    observed_count,
    local_radius,
    observed_value,
    error_variance,
):
    members = prior_ensemble.shape[0]
    bf16 = jnp.bfloat16
    own = jnp.swapaxes(prior_ensemble, 1, 2).reshape(members, 16 * CH, 128)
    cells = observed_cells.reshape(8, 128)
    digits = jnp.stack([cells // 6144, cells // 128 % 48, cells % 128]).reshape(24, 128).astype(bf16)
    digits = jnp.concatenate([digits, jnp.zeros((8, 128), bf16)])
    tail = own[:, (16 - HALO) * CH :].reshape(-1, 128)
    head = own[:, : HALO * CH].reshape(-1, 128)
    left = ring(jnp.concatenate([tail, digits]), 1)
    right = ring(jnp.concatenate([head, digits]), -1)

    chunk, left_halves, left_rates, right_halves, right_rates, taps = inner_forecast(
        own, initial_kernel_taps, latter_kernel_taps
    )
    chunk = left_forecast(chunk, taps, left, own, left_halves, left_rates)
    first_parts = lax.all_to_all(
        chunk.reshape(8, 120, 8, 128), "mem", split_axis=0, concat_axis=0, tiled=True
    )
    edge, picked = right_forecast(
        chunk, cells, initial_kernel_taps, latter_kernel_taps, left, right, right_halves, right_rates
    )

    picked = picked.reshape(3, 8, 8, 128)
    from_left = ring(picked[2], 1)
    from_right = ring(picked[0], -1)
    part = (cells // 128 % 48 // 16).reshape(8, 1, 128)
    here = jnp.where(part == 0, from_left, jnp.where(part == 1, picked[1], from_right))
    message = jnp.concatenate(
        [edge.reshape(8, 40, 8, 128), jnp.broadcast_to(here[None], (8, 8, 8, 128))], axis=1
    )
    second_parts = lax.all_to_all(message, "mem", split_axis=0, concat_axis=0, tiled=True)
    numbers = jnp.stack([observed_count[0], local_radius[0]])
    weights = transform_of(
        second_parts, observed_cells, numbers, observed_value, error_variance
    )
    mixed = mix(first_parts, second_parts, weights)
    back = lax.all_to_all(mixed, "mem", split_axis=0, concat_axis=0, tiled=True)
    return order(back)


def solution(mesh):
    return jax.shard_map(
        per_device,
        mesh=mesh,
        in_specs=(
            P("mem", None, "space", None),
            P(),
            P(),
            P("space", None),
            P("space"),
            P("space"),
            P("space", None),
            P("space", None),
        ),
        out_specs=P("mem", None, "space", None),
        check_vma=False,
    )
```

```python
import functools

import jax
import jax.numpy as jnp
from jax import lax
from jax.experimental import pallas as pl
from jax.experimental.pallas import tpu as pltpu
from jax.sharding import PartitionSpec as P

NS_ITERS = 4
STEP_SIZE = 0.5
HALO = 4
CH = 80
PAIR_A = 4
LAG = 3


def vmem_params():
    return pltpu.CompilerParams(vmem_limit_bytes=40 << 20)


def gelu(x):
    c = 0.7978845608028654
    return 0.5 * x * (1.0 + jnp.tanh(c * (x + 0.044715 * (x * x * x))))


def shifted_sum(p, lane):
    below = pltpu.roll(p[0:80], 1, axis=1)
    above = pltpu.roll(p[160:240], 127, axis=1)
    return p[80:160] + jnp.where(lane == 0, 0.0, below) + jnp.where(lane == 127, 0.0, above)


def conv_pair(source, at, taps, emit, k):
    lane = lax.broadcasted_iota(jnp.int32, (CH, 128), 1)
    window = jnp.concatenate(
        [source[pl.ds(CH * at, 3 * CH), :], source[pl.ds(CH * (at + 1), 3 * CH), :]], axis=1
    )
    partial = jnp.dot(taps, window, preferred_element_type=jnp.float32)
    emit(k, shifted_sum(partial[:, :128], lane))
    emit(k + 1, shifted_sum(partial[:, 128:], lane))


def build_taps(taps, matrix):
    for b in range(3):
        row = jnp.concatenate([taps[3 * a + b].astype(jnp.float32) for a in range(3)], axis=1)
        matrix[pl.ds(CH * b, CH), :] = row.astype(jnp.bfloat16)


def run_interleaved(jobs):
    for _, step in sorted(jobs, key=lambda job: job[0]):
        step()


def inner_kernel(
    own, first_taps, second_taps, out, left_halves, left_rates, right_halves, right_rates, taps_out,
    taps, h, s, g, rate, fields, cells16, sems,
):
    members = own.shape[0]
    build_taps(first_taps, taps.at[0])
    build_taps(second_taps, taps.at[1])
    a = taps[0]
    b = taps[1]
    copies = [
        pltpu.make_async_copy(taps, taps_out, sems.at[0]),
        pltpu.make_async_copy(
            own.at[:, pl.ds(12 * CH, 4 * CH)], right_halves.at[:, pl.ds(6 * CH, 4 * CH)], sems.at[1]
        ),
    ]
    for copy in copies:
        copy.start()

    def group(n, carry):
        jobs = []
        for i in range(PAIR_A):
            m = n * PAIR_A + i
            v, hm, sm, gm, rm = own.at[m], h.at[m], s.at[m], g.at[m], rate.at[m]

            def put_first(k, value, hm=hm):
                hm[pl.ds(CH * k, CH), :] = gelu(value).astype(jnp.bfloat16)

            def put_section(k, value, v=v, sm=sm, rm=rm):
                base = v[pl.ds(CH * (k + 2), CH), :].astype(jnp.float32)
                sm[pl.ds(CH * k, CH), :] = (base + STEP_SIZE * value).astype(jnp.bfloat16)
                rm[pl.ds(CH * k, CH), :] = base + 0.5 * STEP_SIZE * value

            def put_second(k, value, gm=gm):
                gm[pl.ds(CH * k, CH), :] = gelu(value).astype(jnp.bfloat16)

            def put_forecast(k, value, rm=rm, m=m):
                cells = rm[pl.ds(CH * (k + 2), CH), :] + 0.5 * STEP_SIZE * value
                fields[pl.ds(8 * CH * k + m, CH, stride=8), :] = cells

            stages = (
                (v, a, 14, put_first),
                (hm, b, 12, put_section),
                (sm, a, 10, put_second),
                (gm, b, 8, put_forecast),
            )
            for level, (source, matrix, columns, emit) in enumerate(stages):
                for k in range(0, columns, 2):
                    step = functools.partial(conv_pair, source, k, matrix, emit, k)
                    jobs.append(((k // 2 + LAG * level, i, level), step))
        run_interleaved(jobs)
        return carry

    lax.fori_loop(0, members // PAIR_A, group, 0)
    for k, (ref, at) in enumerate(((h, 12), (s, 10), (g, 8))):
        target = pl.ds(2 * CH * k, 2 * CH)
        copies.append(
            pltpu.make_async_copy(ref.at[:, pl.ds(0, 2 * CH)], left_halves.at[:, target], sems.at[2 + k])
        )
        copies.append(
            pltpu.make_async_copy(
                ref.at[:, pl.ds(CH * at, 2 * CH)], right_halves.at[:, target], sems.at[5 + k]
            )
        )
    pair = pl.ds(0, 2 * CH)
    copies.append(pltpu.make_async_copy(rate.at[:, pair], left_rates, sems.at[8]))
    copies.append(
        pltpu.make_async_copy(
            rate.at[:, pl.ds(CH * 10, 2 * CH)], right_rates.at[:, pair], sems.at[9]
        )
    )
    for copy in copies[2:]:
        copy.start()
    cells16[...] = fields[...].astype(jnp.bfloat16).reshape(cells16.shape)
    last = pltpu.make_async_copy(cells16, out.at[pl.ds(0, 8)], sems.at[10])
    last.start()
    for copy in copies:
        copy.wait()
    last.wait()


def vmem():
    return pl.BlockSpec(memory_space=pltpu.VMEM)


def anywhere():
    return pl.BlockSpec(memory_space=pl.ANY)


WIDE16 = 32768
WIDE32 = 16384


def inner_forecast(own, first_taps, second_taps):
    members = own.shape[0]
    bf16, f32 = jnp.bfloat16, jnp.float32
    return pl.pallas_call(
        inner_kernel,
        in_specs=[vmem()] * 3,
        out_specs=[anywhere()] * 6,
        out_shape=[
            jax.ShapeDtypeStruct((12, CH, 8, 128), bf16),
            jax.ShapeDtypeStruct((members, 6 * CH, 128), bf16),
            jax.ShapeDtypeStruct((members, 2 * CH, 128), f32),
            jax.ShapeDtypeStruct((members, WIDE16, 128), bf16),
            jax.ShapeDtypeStruct((members, WIDE32, 128), f32),
            jax.ShapeDtypeStruct((2, 3 * CH, 3 * CH), bf16),
        ],
        scratch_shapes=[
            pltpu.VMEM((2, 3 * CH, 3 * CH), bf16),
            pltpu.VMEM((members, 14 * CH, 128), bf16),
            pltpu.VMEM((members, 12 * CH, 128), bf16),
            pltpu.VMEM((members, 10 * CH, 128), bf16),
            pltpu.VMEM((members, 12 * CH, 128), f32),
            pltpu.VMEM((64 * CH, 128), f32),
            pltpu.VMEM((8, CH, 8, 128), bf16),
            pltpu.SemaphoreType.DMA((11,)),
        ],
        compiler_params=vmem_params(),
        cost_estimate=pl.CostEstimate(
            flops=12_000_000_000, bytes_accessed=8_000_000, transcendentals=2_000_000
        ),
    )(own, first_taps, second_taps)


def edge_loads(side, halves, rates, own, halo, v, h, s, g, rated, sems):
    members = v.shape[0]
    saved = 4 if side == 0 else 0
    copies = []
    for m in range(members):
        source = halo.at[pl.ds(CH * HALO * m, CH * HALO)]
        copies.append((source, v.at[m, pl.ds(0 if side == 0 else 4 * CH, 4 * CH)]))
    copies.append((own, v.at[:, pl.ds(4 * CH if side == 0 else 0, 4 * CH)]))
    for k, ref in enumerate((h, s, g)):
        copies.append((halves.at[:, pl.ds(2 * CH * k, 2 * CH)], ref.at[:, pl.ds(saved * CH, 2 * CH)]))
    copies.append((rates, rated))
    return [
        pltpu.make_async_copy(source, target, sems.at[i])
        for i, (source, target) in enumerate(copies)
    ]


def edge_columns(side, taps, v, h, s, g, rate, rated, fields, start):
    a = taps[0]
    b = taps[1]
    jobs = []
    made = 0 if side == 0 else 2
    for m in range(v.shape[0]):
        vm, hm, sm, gm, rm, rdm = v.at[m], h.at[m], s.at[m], g.at[m], rate.at[m], rated.at[m]

        def hidden(ref):
            def put(k, value):
                ref[pl.ds(CH * (made + k), CH), :] = gelu(value).astype(jnp.bfloat16)

            return put

        def section(k, value, vm=vm, sm=sm, rm=rm):
            base = vm[pl.ds(CH * (k + 2), CH), :].astype(jnp.float32)
            sm[pl.ds(CH * (made + k), CH), :] = (base + STEP_SIZE * value).astype(jnp.bfloat16)
            inside = k - 2 if side == 0 else k
            if 0 <= inside < 2:
                rm[pl.ds(CH * inside, CH), :] = base + 0.5 * STEP_SIZE * value

        def forecast(k, value, rm=rm, rdm=rdm, m=m):
            source = rm if (k < 2) == (side == 0) else rdm
            value = source[pl.ds(CH * (k % 2), CH), :] + 0.5 * STEP_SIZE * value
            value = value.astype(jnp.bfloat16).astype(jnp.float32)
            fields[pl.ds(start + 8 * CH * k + m, CH, stride=8), :] = value

        stages = (
            (vm, made, a, hidden(hm)),
            (hm, 0, b, section),
            (sm, 0, a, hidden(gm)),
            (gm, 0, b, forecast),
        )
        for level, (source, at, matrix, emit) in enumerate(stages):
            for k in (0, 2):
                step = functools.partial(conv_pair, source, at + k, matrix, emit, k)
                jobs.append(((level, m, k), step))
    run_interleaved(jobs)


def edge_scratch(members):
    bf16, f32 = jnp.bfloat16, jnp.float32
    return [
        pltpu.VMEM((members, 8 * CH, 128), bf16),
        pltpu.VMEM((members, 6 * CH, 128), bf16),
        pltpu.VMEM((members, 6 * CH, 128), bf16),
        pltpu.VMEM((members, 6 * CH, 128), bf16),
        pltpu.VMEM((members, 2 * CH, 128), f32),
        pltpu.VMEM((members, 2 * CH, 128), f32),
        pltpu.VMEM((4, CH, 8, 128), bf16),
        pltpu.SemaphoreType.DMA((members + 6,)),
    ]


def left_kernel(
    chunk, taps, halo, own, halves, rates, out, v, h, s, g, rate, rated, cells16, sems, fields
):
    copies = edge_loads(0, halves, rates, own.at[:, pl.ds(0, 4 * CH)], halo, v, h, s, g, rated, sems)
    for copy in copies:
        copy.start()
    for copy in copies:
        copy.wait()
    edge_columns(0, taps, v, h, s, g, rate, rated, fields, 0)
    cells16[...] = fields[...].astype(jnp.bfloat16).reshape(cells16.shape)
    last = pltpu.make_async_copy(cells16, out.at[pl.ds(8, 4)], sems.at[len(copies)])
    last.start()
    last.wait()


def left_forecast(chunk, taps, halo, own, halves, rates):
    members = own.shape[0]
    return pl.pallas_call(
        left_kernel,
        in_specs=[anywhere(), vmem()] + [anywhere()] * 4,
        out_specs=anywhere(),
        out_shape=jax.ShapeDtypeStruct((12, CH, 8, 128), jnp.bfloat16),
        scratch_shapes=edge_scratch(members) + [pltpu.VMEM((32 * CH, 128), jnp.float32)],
        input_output_aliases={0: 0},
        compiler_params=vmem_params(),
        cost_estimate=pl.CostEstimate(
            flops=5_000_000_000, bytes_accessed=4_000_000, transcendentals=1_000_000
        ),
    )(chunk, taps, halo, own, halves, rates)


def place_of(channel, lon, lat, part):
    slot = lax.broadcasted_iota(jnp.int32, (8, 128), 1)
    lon = lon - 16 * part
    column = jnp.where(lon < 4, lon + 8, jnp.where(lon < 12, lon - 4, lon))
    here = (lon >= 0) & (lon < 16)
    return jnp.where(here, (column * CH + channel) * 8, 0), (slot - lat) & 127


def right_kernel(
    chunk, cells, first_taps, second_taps, left, right, halves, rates, out, picked,
    v, h, s, g, rate, rated, cells16, sems, taps, fields, chunk16, lists, drawn, places, rows, turns, list_sems, place_sems,
):
    members = v.shape[0]
    digits = CH * HALO * members
    copies = edge_loads(
        1,
        halves,
        rates.at[:, pl.ds(0, 2 * CH)],
        halves.at[:, pl.ds(6 * CH, 4 * CH)],
        right, v, h, s, g, rated, sems,
    )
    list_copies = [
        pltpu.make_async_copy(source.at[pl.ds(digits, 32)], lists.at[i], list_sems.at[i])
        for i, source in enumerate((left, right))
    ]
    chunk_copy = pltpu.make_async_copy(chunk, chunk16, list_sems.at[2])
    for copy in list_copies + copies + [chunk_copy]:
        copy.start()
    build_taps(first_taps, taps.at[0])
    build_taps(second_taps, taps.at[1])
    for copy in list_copies:
        copy.wait()
    for k in range(3):
        if k == 1:
            cell = cells[...]
            strip = cell >> 7
            channel = (strip * 43691) >> 21
            parts = (channel, strip - 48 * channel, cell & 127)
        else:
            block = lists[k // 2].astype(jnp.float32).astype(jnp.int32)
            parts = (block[0:8], block[8:16], block[16:24])
        row, turn = place_of(*parts, 2 - k)
        places[0, pl.ds(8 * k, 8), :] = row
        places[1, pl.ds(8 * k, 8), :] = turn
    place_copies = [
        pltpu.make_async_copy(places.at[0], rows, place_sems.at[0]),
        pltpu.make_async_copy(places.at[1], turns, place_sems.at[1]),
    ]
    for copy in place_copies:
        copy.start()
    for copy in copies:
        copy.wait()
    edge_columns(1, taps, v, h, s, g, rate, rated, fields, 96 * CH)
    cells16[...] = fields[pl.ds(96 * CH, 32 * CH), :].astype(jnp.bfloat16).reshape(cells16.shape)
    out_copy = pltpu.make_async_copy(cells16, out, sems.at[len(copies)])
    out_copy.start()
    chunk_copy.wait()
    fields[pl.ds(0, 96 * CH), :] = chunk16[...].astype(jnp.float32).reshape(96 * CH, 128)
    for copy in place_copies:
        copy.wait()
    lane = lax.broadcasted_iota(jnp.int32, (8, 128), 1)

    def block(k, carry):
        acc = jnp.zeros((8, 128), jnp.float32)
        for j in range(128):
            cell = fields[pl.ds(pl.multiple_of(rows[k, j], 8), 8), :]
            acc = jnp.where(lane == j, pltpu.roll(cell, turns[k, j], axis=1), acc)
        drawn[k] = acc.astype(jnp.bfloat16)
        return carry

    lax.fori_loop(0, drawn.shape[0], block, 0)
    drawn_copy = pltpu.make_async_copy(drawn, picked, place_sems.at[2])
    drawn_copy.start()
    drawn_copy.wait()
    out_copy.wait()


def right_forecast(chunk, cells, first_taps, second_taps, left, right, halves, rates):
    bf16, f32 = jnp.bfloat16, jnp.float32
    members = halves.shape[0]
    return pl.pallas_call(
        right_kernel,
        in_specs=[anywhere()] + [vmem()] * 3 + [anywhere()] * 4,
        out_specs=[anywhere()] * 2,
        out_shape=[
            jax.ShapeDtypeStruct((4, CH, 8, 128), bf16),
            jax.ShapeDtypeStruct((24, 8, 128), bf16),
        ],
        scratch_shapes=edge_scratch(members) + [
            pltpu.VMEM((2, 3 * CH, 3 * CH), bf16),
            pltpu.VMEM((128 * CH, 128), f32),
            pltpu.VMEM((12, CH, 8, 128), bf16),
            pltpu.VMEM((2, 32, 128), bf16),
            pltpu.VMEM((24, 8, 128), bf16),
            pltpu.VMEM((2, 24, 128), jnp.int32),
            pltpu.SMEM((24, 128), jnp.int32),
            pltpu.SMEM((24, 128), jnp.int32),
            pltpu.SemaphoreType.DMA((3,)),
            pltpu.SemaphoreType.DMA((3,)),
        ],
        compiler_params=vmem_params(),
        cost_estimate=pl.CostEstimate(
            flops=5_000_000_000, bytes_accessed=8_000_000, transcendentals=1_000_000
        ),
    )(chunk, cells, first_taps, second_taps, left, right, halves, rates)


def transform_kernel(parts, cells, numbers, observed, variance, out, values, stack, sem):
    f32 = jnp.float32
    exact = lax.Precision.HIGHEST
    load = pltpu.make_async_copy(parts.at[:, pl.ds(40, 8)], values, sem)
    load.start()
    load.wait()
    for group in range(8):
        for block in range(8):
            stack[pl.ds(8 * group, 8), pl.ds(128 * block, 128)] = values[group, block].astype(f32)
    model_obs = stack[...]
    center = jnp.sum(model_obs, axis=0, keepdims=True) * (1.0 / 64.0)
    spread = model_obs - center
    cell = cells[...]
    strip = cell >> 7
    lon = strip - 48 * ((strip * 43691) >> 21)
    scaled = (lon.astype(f32) - 23.5) / numbers[1].astype(f32)
    taper = jnp.exp(-0.5 * scaled * scaled)
    slot = lax.broadcasted_iota(jnp.int32, cell.shape, 1)
    weight = jnp.where(slot < numbers[0], taper / variance[...], 0.0)
    weighted = spread * weight

    def product(x, y):
        return jnp.dot(x, y, precision=exact, preferred_element_type=f32)

    gram = lax.dot_general(
        weighted, spread, (((1,), (1,)), ((), ())), precision=exact, preferred_element_type=f32
    )
    right_side = jnp.sum(weighted * (observed[...] - center), axis=1, keepdims=True)
    i = lax.broadcasted_iota(jnp.int32, (64, 64), 0)
    j = lax.broadcasted_iota(jnp.int32, (64, 64), 1)
    eye = jnp.where(i == j, 1.0, 0.0).astype(f32)
    norm = 63.0 + jnp.sqrt(jnp.sum(jnp.sum(gram * gram, axis=1, keepdims=True), axis=0, keepdims=True))
    iterate = (63.0 * eye + gram) / norm
    root = 1.5 * eye - 0.5 * iterate
    iterate = product(iterate, root)
    for sweep in range(1, NS_ITERS):
        factor = 1.5 * eye - 0.5 * product(root, iterate)
        if sweep < NS_ITERS - 1:
            iterate = product(iterate, factor)
        root = product(factor, root)
    wide = jnp.broadcast_to(right_side, (64, 128))
    shift = product(root, product(root, wide)) / norm
    transform = (shift[:, :64] + jnp.sqrt(63.0 / norm) * root).astype(jnp.bfloat16)
    i = lax.broadcasted_iota(jnp.int32, (64, 256), 0)
    j = lax.broadcasted_iota(jnp.int32, (64, 256), 1)
    for q in range(4):
        place = jnp.where(j == i + 64 * q, 1.0, 0.0).astype(jnp.bfloat16)
        turned = lax.dot_general(
            transform, place, (((0,), (0,)), ((), ())), preferred_element_type=f32
        )
        out[pl.ds(64 * q, 64), :] = turned.astype(jnp.bfloat16)


def transform_of(parts, cells, numbers, observed, variance):
    smem = pl.BlockSpec(memory_space=pltpu.SMEM)
    return pl.pallas_call(
        transform_kernel,
        in_specs=[anywhere(), vmem(), smem, vmem(), vmem()],
        out_specs=vmem(),
        out_shape=jax.ShapeDtypeStruct((256, 256), jnp.bfloat16),
        scratch_shapes=[
            pltpu.VMEM((8, 8, 8, 128), jnp.bfloat16),
            pltpu.VMEM((64, 1024), jnp.float32),
            pltpu.SemaphoreType.DMA,
        ],
        compiler_params=vmem_params(),
        cost_estimate=pl.CostEstimate(
            flops=100_000_000, bytes_accessed=500_000, transcendentals=1000
        ),
    )(parts, cells, numbers, observed, variance)


def mix_rows(parts, first, w, out, start):
    centers = []
    halves = []
    for half in range(2):
        stack = []
        for q in range(4):
            value = parts[:, first + 4 * half + q].astype(jnp.float32)
            center = jnp.sum(jnp.sum(value, axis=0), axis=0, keepdims=True) * (1.0 / 64.0)
            centers.append(center)
            stack.append((value.reshape(64, 128) - center).astype(jnp.bfloat16))
        halves.append(jnp.concatenate(stack, axis=0))
    mixed = jnp.dot(w, jnp.concatenate(halves, axis=1), preferred_element_type=jnp.float32)
    for half in range(2):
        for q in range(4):
            value = mixed[64 * q : 64 * q + 64, 128 * half : 128 * half + 128]
            value = value + centers[4 * half + q]
            out[:, start + 4 * half + q] = value.astype(jnp.bfloat16).reshape(8, 8, 128)


def mix_kernel(first, second, weights, out):
    w = weights[...]

    def block(n, carry):
        for k in range(5):
            row = (5 * n + k) * 8
            mix_rows(first, row, w, out, row)
        return carry

    lax.fori_loop(0, 3, block, 0)
    for k in range(5):
        mix_rows(second, 8 * k, w, out, 120 + 8 * k)


def mix(first, second, weights):
    return pl.pallas_call(
        mix_kernel,
        in_specs=[vmem()] * 3,
        out_specs=vmem(),
        out_shape=jax.ShapeDtypeStruct((8, 160, 8, 128), jnp.bfloat16),
        compiler_params=vmem_params(),
        cost_estimate=pl.CostEstimate(
            flops=700_000_000, bytes_accessed=5_300_000, transcendentals=0
        ),
    )(first, second, weights)


CHUNKS = 5


def order_kernel(cells, out, scratch, sems):
    to = lax.broadcasted_iota(jnp.int32, (128, 128), 0)
    at = lax.broadcasted_iota(jnp.int32, (128, 128), 1)
    slot = at >> 3
    column = jnp.where(slot < 8, slot + 4, jnp.where(slot < 12, slot - 8, slot))
    move = jnp.where(to == (at & 7) * 16 + column, 1.0, 0.0).astype(jnp.bfloat16)

    def cell(i, c):
        if i < 12:
            return cells[(CH * i + c) // 120, (CH * i + c) % 120]
        return cells[(CH * (i - 12) + c) // 40, 120 + (CH * (i - 12) + c) % 40]

    def rows(c):
        return jnp.stack([cell(i, c) for i in range(16)]).reshape(128, 128)

    depth = CH // CHUNKS
    copies = []
    for chunk in range(CHUNKS):
        for c in range(depth * chunk, depth * (chunk + 1), 2):
            both = jnp.concatenate([rows(c), rows(c + 1)], axis=1)
            moved = jnp.dot(move, both, preferred_element_type=jnp.float32).astype(jnp.bfloat16)
            scratch[:, c] = moved[:, :128].reshape(8, 16, 128)
            scratch[:, c + 1] = moved[:, 128:].reshape(8, 16, 128)
        span = pl.ds(depth * chunk, depth)
        copy = pltpu.make_async_copy(scratch.at[:, span], out.at[:, span], sems.at[chunk])
        copy.start()
        copies.append(copy)
    for copy in copies:
        copy.wait()


def order(cells):
    return pl.pallas_call(
        order_kernel,
        in_specs=[vmem()],
        out_specs=anywhere(),
        out_shape=jax.ShapeDtypeStruct((8, CH, 16, 128), jnp.bfloat16),
        scratch_shapes=[
            pltpu.VMEM((8, CH, 16, 128), jnp.bfloat16),
            pltpu.SemaphoreType.DMA((CHUNKS,)),
        ],
        compiler_params=vmem_params(),
        cost_estimate=pl.CostEstimate(
            flops=600_000_000, bytes_accessed=5_300_000, transcendentals=0
        ),
    )(cells)


def ring(cells, step):
    count = lax.axis_size("space")
    return lax.ppermute(cells, "space", [(i, (i + step) % count) for i in range(count)])


def per_device(
    prior_ensemble,
    initial_kernel_taps,
    latter_kernel_taps,
    observed_cells,
    observed_count,
    local_radius,
    observed_value,
    error_variance,
):
    members = prior_ensemble.shape[0]
    bf16 = jnp.bfloat16
    own = jnp.swapaxes(prior_ensemble, 1, 2).reshape(members, 16 * CH, 128)
    cells = observed_cells.reshape(8, 128)
    digits = jnp.stack([cells // 6144, cells // 128 % 48, cells % 128]).reshape(24, 128).astype(bf16)
    digits = jnp.concatenate([digits, jnp.zeros((8, 128), bf16)])
    tail = own[:, (16 - HALO) * CH :].reshape(-1, 128)
    head = own[:, : HALO * CH].reshape(-1, 128)
    left = ring(jnp.concatenate([tail, digits]), 1)
    right = ring(jnp.concatenate([head, digits]), -1)

    chunk, left_halves, left_rates, right_halves, right_rates, taps = inner_forecast(
        own, initial_kernel_taps, latter_kernel_taps
    )
    chunk = left_forecast(chunk, taps, left, own, left_halves, left_rates)
    first_parts = lax.all_to_all(
        chunk.reshape(8, 120, 8, 128), "mem", split_axis=0, concat_axis=0, tiled=True
    )
    edge, picked = right_forecast(
        chunk, cells, initial_kernel_taps, latter_kernel_taps, left, right, right_halves, right_rates
    )

    picked = picked.reshape(3, 8, 8, 128)
    from_left = ring(picked[2], 1)
    from_right = ring(picked[0], -1)
    part = (cells // 128 % 48 // 16).reshape(8, 1, 128)
    here = jnp.where(part == 0, from_left, jnp.where(part == 1, picked[1], from_right))
    message = jnp.concatenate(
        [edge.reshape(8, 40, 8, 128), jnp.broadcast_to(here[None], (8, 8, 8, 128))], axis=1
    )
    message, first_parts = lax.optimization_barrier((message, first_parts))
    second_parts = lax.all_to_all(message, "mem", split_axis=0, concat_axis=0, tiled=True)
    numbers = jnp.stack([observed_count[0], local_radius[0]])
    weights = transform_of(
        second_parts, observed_cells, numbers, observed_value, error_variance
    )
    mixed = mix(first_parts, second_parts, weights)
    back = lax.all_to_all(mixed, "mem", split_axis=0, concat_axis=0, tiled=True)
    return order(back)


def solution(mesh):
    return jax.shard_map(
        per_device,
        mesh=mesh,
        in_specs=(
            P("mem", None, "space", None),
            P(),
            P(),
            P("space", None),
            P("space"),
            P("space"),
            P("space", None),
            P("space", None),
        ),
        out_specs=P("mem", None, "space", None),
        check_vma=False,
    )
```

```python
import functools

import jax
import jax.numpy as jnp
from jax import lax
from jax.experimental import pallas as pl
from jax.experimental.pallas import tpu as pltpu
from jax.sharding import PartitionSpec as P

NS_ITERS = 4
STEP_SIZE = 0.5
HALO = 4
CH = 80
PAIR_A = 8
LAG = 3


def vmem_params():
    return pltpu.CompilerParams(vmem_limit_bytes=40 << 20)


def gelu(x):
    c = 0.7978845608028654
    return 0.5 * x * (1.0 + jnp.tanh(c * (x + 0.044715 * (x * x * x))))


def shifted_sum(p, lane):
    below = pltpu.roll(p[0:80], 1, axis=1)
    above = pltpu.roll(p[160:240], 127, axis=1)
    return p[80:160] + jnp.where(lane == 0, 0.0, below) + jnp.where(lane == 127, 0.0, above)


def conv_pair(source, at, taps, emit, k):
    lane = lax.broadcasted_iota(jnp.int32, (CH, 128), 1)
    window = jnp.concatenate(
        [source[pl.ds(CH * at, 3 * CH), :], source[pl.ds(CH * (at + 1), 3 * CH), :]], axis=1
    )
    partial = jnp.dot(taps, window, preferred_element_type=jnp.float32)
    emit(k, shifted_sum(partial[:, :128], lane))
    emit(k + 1, shifted_sum(partial[:, 128:], lane))


def build_taps(taps, matrix):
    for b in range(3):
        row = jnp.concatenate([taps[3 * a + b].astype(jnp.float32) for a in range(3)], axis=1)
        row = jnp.concatenate([row, jnp.zeros((CH, 256 - 3 * CH), jnp.float32)], axis=1)
        matrix[pl.ds(CH * b, CH), :] = row.astype(jnp.bfloat16)


def run_interleaved(jobs):
    for _, step in sorted(jobs, key=lambda job: job[0]):
        step()


SAVED = 0
OWN = 12 * CH
TAPS = 20 * CH
WIDE16 = 32768
WIDE32 = 16384


def vmem():
    return pl.BlockSpec(memory_space=pltpu.VMEM)


def anywhere():
    return pl.BlockSpec(memory_space=pl.ANY)


def begin(copies, sems, first=0):
    copies = [
        pltpu.make_async_copy(source, target, sems.at[first + i])
        for i, (source, target) in enumerate(copies)
    ]
    for copy in copies:
        copy.start()
    return copies


def finish(copies):
    for copy in copies:
        copy.wait()


def taps_moves(taps, wide):
    moves = []
    for t in range(2):
        for half in range(2):
            here = taps.at[t, :, pl.ds(128 * half, 128)]
            moves.append((here, wide.at[2 * t + half, pl.ds(TAPS, 3 * CH)]))
    return moves


def inner_kernel(
    own, first_taps, second_taps, out, wide16, wide32, taps, h, s, g, rate, fields, cells16, sems
):
    members = own.shape[0]
    build_taps(first_taps, taps.at[0])
    build_taps(second_taps, taps.at[1])
    a = taps[0, :, : 3 * CH]
    b = taps[1, :, : 3 * CH]
    early = [
        (own.at[:, pl.ds(12 * CH * side, 4 * CH)], wide16.at[:, pl.ds(OWN + 4 * CH * side, 4 * CH)])
        for side in range(2)
    ]
    early = begin(early + taps_moves(taps, wide16), sems)

    def group(n, carry):
        jobs = []
        for i in range(PAIR_A):
            m = n * PAIR_A + i
            v, hm, sm, gm, rm = own.at[m], h.at[m], s.at[m], g.at[m], rate.at[m]

            def put_first(k, value, hm=hm):
                hm[pl.ds(CH * k, CH), :] = gelu(value).astype(jnp.bfloat16)

            def put_section(k, value, v=v, sm=sm, rm=rm):
                base = v[pl.ds(CH * (k + 2), CH), :].astype(jnp.float32)
                sm[pl.ds(CH * k, CH), :] = (base + STEP_SIZE * value).astype(jnp.bfloat16)
                rm[pl.ds(CH * k, CH), :] = base + 0.5 * STEP_SIZE * value

            def put_second(k, value, gm=gm):
                gm[pl.ds(CH * k, CH), :] = gelu(value).astype(jnp.bfloat16)

            def put_forecast(k, value, rm=rm, m=m):
                cells = rm[pl.ds(CH * (k + 2), CH), :] + 0.5 * STEP_SIZE * value
                fields[pl.ds(8 * CH * k + m, CH, stride=8), :] = cells

            stages = (
                (v, a, 14, put_first),
                (hm, b, 12, put_section),
                (sm, a, 10, put_second),
                (gm, b, 8, put_forecast),
            )
            for level, (source, matrix, columns, emit) in enumerate(stages):
                for k in range(0, columns, 2):
                    step = functools.partial(conv_pair, source, k, matrix, emit, k)
                    jobs.append(((k // 2 + LAG * level, i, level), step))
        run_interleaved(jobs)
        return carry

    lax.fori_loop(0, members // PAIR_A, group, 0)
    late = []
    for side in range(2):
        for k, (ref, right) in enumerate(((h, 12), (s, 10), (g, 8))):
            target = wide16.at[:, pl.ds(SAVED + 6 * CH * side + 2 * CH * k, 2 * CH)]
            late.append((ref.at[:, pl.ds(CH * right * side, 2 * CH)], target))
        target = wide32.at[:, pl.ds(2 * CH * side, 2 * CH)]
        late.append((rate.at[:, pl.ds(10 * CH * side, 2 * CH)], target))
    late = begin(late, sems, len(early))
    last = []
    for x in range(8):
        column = fields[pl.ds(8 * CH * x, 8 * CH), :].astype(jnp.bfloat16)
        cells16[x] = column.reshape(CH, 8, 128)
        if x % 2:
            pair = pl.ds(x - 1, 2)
            last += begin([(cells16.at[pair], out.at[pair])], sems, len(early) + len(late) + x // 2)
    finish(early + late + last)


def inner_forecast(own, first_taps, second_taps):
    members = own.shape[0]
    bf16, f32 = jnp.bfloat16, jnp.float32
    return pl.pallas_call(
        inner_kernel,
        in_specs=[vmem()] * 3,
        out_specs=[anywhere()] * 3,
        out_shape=[
            jax.ShapeDtypeStruct((8, CH, 8, 128), bf16),
            jax.ShapeDtypeStruct((members, WIDE16, 128), bf16),
            jax.ShapeDtypeStruct((members, WIDE32, 128), f32),
        ],
        scratch_shapes=[
            pltpu.VMEM((2, 3 * CH, 256), bf16),
            pltpu.VMEM((members, 14 * CH, 128), bf16),
            pltpu.VMEM((members, 12 * CH, 128), bf16),
            pltpu.VMEM((members, 10 * CH, 128), bf16),
            pltpu.VMEM((members, 12 * CH, 128), f32),
            pltpu.VMEM((64 * CH, 128), f32),
            pltpu.VMEM((8, CH, 8, 128), bf16),
            pltpu.SemaphoreType.DMA((18,)),
        ],
        compiler_params=vmem_params(),
        cost_estimate=pl.CostEstimate(
            flops=12_000_000_000, bytes_accessed=8_000_000, transcendentals=2_000_000
        ),
    )(own, first_taps, second_taps)


def edge_jobs(side, taps, v, h, s, g, rate, rated, fields, start):
    a = taps[0, :, : 3 * CH]
    b = taps[1, :, : 3 * CH]
    jobs = []
    made = 0 if side == 0 else 2
    for m in range(v.shape[1]):
        vm, hm, sm, gm = v.at[side, m], h.at[side, m], s.at[side, m], g.at[side, m]
        rm, rdm = rate.at[side, m], rated.at[m, pl.ds(2 * CH * side, 2 * CH)]

        def hidden(ref):
            def put(k, value):
                ref[pl.ds(CH * (made + k), CH), :] = gelu(value).astype(jnp.bfloat16)

            return put

        def section(k, value, vm=vm, sm=sm, rm=rm):
            base = vm[pl.ds(CH * (k + 2), CH), :].astype(jnp.float32)
            sm[pl.ds(CH * (made + k), CH), :] = (base + STEP_SIZE * value).astype(jnp.bfloat16)
            inside = k - 2 if side == 0 else k
            if 0 <= inside < 2:
                rm[pl.ds(CH * inside, CH), :] = base + 0.5 * STEP_SIZE * value

        def forecast(k, value, rm=rm, rdm=rdm, m=m):
            source = rm if (k < 2) == (side == 0) else rdm
            value = source[pl.ds(CH * (k % 2), CH), :] + 0.5 * STEP_SIZE * value
            value = value.astype(jnp.bfloat16).astype(jnp.float32)
            fields[pl.ds(start + 8 * CH * k + m, CH, stride=8), :] = value

        stages = (
            (vm, made, a, hidden(hm)),
            (hm, 0, b, section),
            (sm, 0, a, hidden(gm)),
            (gm, 0, b, forecast),
        )
        for level, (source, at, matrix, emit) in enumerate(stages):
            for k in (0, 2):
                step = functools.partial(conv_pair, source, at + k, matrix, emit, k)
                jobs.append(((level, m, side, k), step))
    return jobs


def place_of(channel, lon, lat, part):
    slot = lax.broadcasted_iota(jnp.int32, (8, 128), 1)
    lon = lon - 16 * part
    column = jnp.where(lon < 4, lon + 8, jnp.where(lon < 12, lon - 4, lon))
    here = (lon >= 0) & (lon < 16)
    return jnp.where(here, (column * CH + channel) * 8, 0), (slot - lat) & 127


def edge_kernel(
    inner, cells, left, right, wide16, wide32, out, picked,
    taps, v, h, s, g, rate, rated, fields, inner16, lists, own_list, places, rows, turns,
    sems, list_sems, place_sems,
):
    members = v.shape[1]
    halo = CH * HALO
    digits = halo * members
    early = begin([(there, here) for here, there in taps_moves(taps, wide16)], sems)
    list_copies = begin(
        [(left.at[pl.ds(digits, 32)], lists.at[0]), (right.at[pl.ds(digits, 32)], lists.at[1]), (cells, own_list)],
        list_sems,
    )
    columns = []
    used = len(early)
    for m in range(members):
        moves = []
        for side, source in enumerate((left, right)):
            edge = v.at[side, m]
            moves.append((source.at[pl.ds(halo * m, halo)], edge.at[pl.ds(4 * CH * side, 4 * CH)]))
            source = wide16.at[m, pl.ds(OWN + 4 * CH * side, 4 * CH)]
            moves.append((source, edge.at[pl.ds(4 * CH * (1 - side), 4 * CH)]))
        columns.append(begin(moves, sems, used))
        used += len(moves)
    moves = []
    for k, ref in enumerate((h, s, g)):
        for side in range(2):
            source = wide16.at[:, pl.ds(SAVED + 6 * CH * side + 2 * CH * k, 2 * CH)]
            moves.append((source, ref.at[side, :, pl.ds(4 * CH * (1 - side), 2 * CH)]))
    moves.append((wide32.at[:, pl.ds(0, 4 * CH)], rated))
    later = begin(moves, sems, used)
    inner_copy = begin([(inner, inner16)], list_sems, 3)
    finish(list_copies)
    for k in range(3):
        if k == 1:
            cell = own_list[...]
            strip = cell >> 7
            channel = (strip * 43691) >> 21
            parts = (channel, strip - 48 * channel, cell & 127)
        else:
            block = lists[k // 2].astype(jnp.float32).astype(jnp.int32)
            parts = (block[0:8], block[8:16], block[16:24])
        row, turn = place_of(*parts, 2 - k)
        places[0, pl.ds(8 * k, 8), :] = row
        places[1, pl.ds(8 * k, 8), :] = turn
    place_copies = begin([(places.at[0], rows), (places.at[1], turns)], place_sems)
    finish(early)
    jobs = []
    for side in range(2):
        jobs += edge_jobs(side, taps, v, h, s, g, rate, rated, fields, (64 + 32 * side) * CH)

    for n in range(2):
        for m in range(4 * n, 4 * n + 4):
            jobs.append(((0, 4 * n, -1, 0), functools.partial(finish, columns[m])))
    jobs.append(((1, -1, 0, 0), functools.partial(finish, later + inner_copy)))
    run_interleaved(jobs)
    fields[pl.ds(0, 64 * CH), :] = inner16[...].astype(jnp.float32).reshape(64 * CH, 128)
    out[...] = fields[pl.ds(64 * CH, 64 * CH), :].astype(jnp.bfloat16).reshape(out.shape)
    finish(place_copies)
    lane = lax.broadcasted_iota(jnp.int32, (8, 128), 1)

    def block(k, carry):
        found = [jnp.zeros((8, 128), jnp.float32)] * 3
        for j in range(128):
            for q in range(3):
                cell = fields[pl.ds(pl.multiple_of(rows[8 * q + k, j], 8), 8), :]
                cell = pltpu.roll(cell, turns[8 * q + k, j], axis=1)
                found[q] = jnp.where(lane == j, cell, found[q])
        for q in range(3):
            picked[8 * q + k] = found[q].astype(jnp.bfloat16)
        return carry

    lax.fori_loop(0, 8, block, 0)


def edge_forecast(inner, cells, left, right, wide16, wide32):
    bf16, f32 = jnp.bfloat16, jnp.float32
    members = wide16.shape[0]
    return pl.pallas_call(
        edge_kernel,
        in_specs=[anywhere()] * 6,
        out_specs=[vmem()] * 2,
        out_shape=[
            jax.ShapeDtypeStruct((8, CH, 8, 128), bf16),
            jax.ShapeDtypeStruct((24, 8, 128), bf16),
        ],
        scratch_shapes=[
            pltpu.VMEM((2, 3 * CH, 256), bf16),
            pltpu.VMEM((2, members, 8 * CH, 128), bf16),
            pltpu.VMEM((2, members, 6 * CH, 128), bf16),
            pltpu.VMEM((2, members, 6 * CH, 128), bf16),
            pltpu.VMEM((2, members, 6 * CH, 128), bf16),
            pltpu.VMEM((2, members, 2 * CH, 128), f32),
            pltpu.VMEM((members, 4 * CH, 128), f32),
            pltpu.VMEM((128 * CH, 128), f32),
            pltpu.VMEM((8, CH, 8, 128), bf16),
            pltpu.VMEM((2, 32, 128), bf16),
            pltpu.VMEM((8, 128), jnp.int32),
            pltpu.VMEM((2, 24, 128), jnp.int32),
            pltpu.SMEM((24, 128), jnp.int32),
            pltpu.SMEM((24, 128), jnp.int32),
            pltpu.SemaphoreType.DMA((4 * members + 11,)),
            pltpu.SemaphoreType.DMA((4,)),
            pltpu.SemaphoreType.DMA((2,)),
        ],
        compiler_params=vmem_params(),
        cost_estimate=pl.CostEstimate(
            flops=9_000_000_000, bytes_accessed=8_000_000, transcendentals=2_000_000
        ),
    )(inner, cells, left, right, wide16, wide32)


def transform_kernel(parts, cells, numbers, observed, variance, out, values, stack, sem):
    f32 = jnp.float32
    exact = lax.Precision.HIGHEST
    load = pltpu.make_async_copy(parts.at[:, pl.ds(CH, 8)], values, sem)
    load.start()
    load.wait()
    for group in range(8):
        for block in range(8):
            stack[pl.ds(8 * group, 8), pl.ds(128 * block, 128)] = values[group, block].astype(f32)
    model_obs = stack[...]
    center = jnp.sum(model_obs, axis=0, keepdims=True) * (1.0 / 64.0)
    spread = model_obs - center
    cell = cells[...]
    strip = cell >> 7
    lon = strip - 48 * ((strip * 43691) >> 21)
    scaled = (lon.astype(f32) - 23.5) / numbers[1].astype(f32)
    taper = jnp.exp(-0.5 * scaled * scaled)
    slot = lax.broadcasted_iota(jnp.int32, cell.shape, 1)
    weight = jnp.where(slot < numbers[0], taper / variance[...], 0.0)
    weighted = spread * weight

    def product(x, y):
        return jnp.dot(x, y, precision=exact, preferred_element_type=f32)

    gram = lax.dot_general(
        weighted, spread, (((1,), (1,)), ((), ())), precision=exact, preferred_element_type=f32
    )
    right_side = jnp.sum(weighted * (observed[...] - center), axis=1, keepdims=True)
    i = lax.broadcasted_iota(jnp.int32, (64, 64), 0)
    j = lax.broadcasted_iota(jnp.int32, (64, 64), 1)
    eye = jnp.where(i == j, 1.0, 0.0).astype(f32)
    norm = 63.0 + jnp.sqrt(jnp.sum(jnp.sum(gram * gram, axis=1, keepdims=True), axis=0, keepdims=True))
    iterate = (63.0 * eye + gram) / norm
    root = 1.5 * eye - 0.5 * iterate
    iterate = product(iterate, root)
    for sweep in range(1, NS_ITERS):
        factor = 1.5 * eye - 0.5 * product(root, iterate)
        if sweep < NS_ITERS - 1:
            iterate = product(iterate, factor)
        root = product(factor, root)
    wide = jnp.broadcast_to(right_side, (64, 128))
    shift = product(root, product(root, wide)) / norm
    transform = (shift[:, :64] + jnp.sqrt(63.0 / norm) * root).astype(jnp.bfloat16)
    i = lax.broadcasted_iota(jnp.int32, (64, 256), 0)
    j = lax.broadcasted_iota(jnp.int32, (64, 256), 1)
    for q in range(4):
        place = jnp.where(j == i + 64 * q, 1.0, 0.0).astype(jnp.bfloat16)
        turned = lax.dot_general(
            transform, place, (((0,), (0,)), ((), ())), preferred_element_type=f32
        )
        out[pl.ds(64 * q, 64), :] = turned.astype(jnp.bfloat16)


def transform_of(parts, cells, numbers, observed, variance):
    smem = pl.BlockSpec(memory_space=pltpu.SMEM)
    return pl.pallas_call(
        transform_kernel,
        in_specs=[anywhere(), vmem(), smem, vmem(), vmem()],
        out_specs=vmem(),
        out_shape=jax.ShapeDtypeStruct((256, 256), jnp.bfloat16),
        scratch_shapes=[
            pltpu.VMEM((8, 8, 8, 128), jnp.bfloat16),
            pltpu.VMEM((64, 1024), jnp.float32),
            pltpu.SemaphoreType.DMA,
        ],
        compiler_params=vmem_params(),
        cost_estimate=pl.CostEstimate(
            flops=100_000_000, bytes_accessed=500_000, transcendentals=1000
        ),
    )(parts, cells, numbers, observed, variance)


def mix_rows(parts, first, w, out, start):
    centers = []
    halves = []
    for half in range(2):
        stack = []
        for q in range(4):
            value = parts[:, first + 4 * half + q].astype(jnp.float32)
            center = jnp.sum(jnp.sum(value, axis=0), axis=0, keepdims=True) * (1.0 / 64.0)
            centers.append(center)
            stack.append((value.reshape(64, 128) - center).astype(jnp.bfloat16))
        halves.append(jnp.concatenate(stack, axis=0))
    mixed = jnp.dot(w, jnp.concatenate(halves, axis=1), preferred_element_type=jnp.float32)
    for half in range(2):
        for q in range(4):
            value = mixed[64 * q : 64 * q + 64, 128 * half : 128 * half + 128]
            value = value + centers[4 * half + q]
            out[:, start + 4 * half + q] = value.astype(jnp.bfloat16).reshape(8, 8, 128)


def mix_kernel(first, second, weights, out):
    w = weights[...]

    def half(parts, start):
        def block(n, carry):
            for k in range(5):
                row = (5 * n + k) * 8
                mix_rows(parts, row, w, out, start + row)
            return carry

        lax.fori_loop(0, 2, block, 0)

    half(first, 0)
    half(second, CH)


def mix(first, second, weights):
    return pl.pallas_call(
        mix_kernel,
        in_specs=[vmem()] * 3,
        out_specs=vmem(),
        out_shape=jax.ShapeDtypeStruct((8, 160, 8, 128), jnp.bfloat16),
        compiler_params=vmem_params(),
        cost_estimate=pl.CostEstimate(
            flops=700_000_000, bytes_accessed=5_300_000, transcendentals=0
        ),
    )(first, second, weights)


CHUNKS = 5


def order_kernel(cells, out, scratch, sems):
    to = lax.broadcasted_iota(jnp.int32, (128, 128), 0)
    at = lax.broadcasted_iota(jnp.int32, (128, 128), 1)
    source = at >> 4
    side = (at >> 3) & 1
    column = jnp.where(side == 0, source + 4, jnp.where(source < 4, source, source + 8))
    move = jnp.where(to == (at & 7) * 16 + column, 1.0, 0.0).astype(jnp.bfloat16)

    def rows(c):
        return jnp.concatenate(
            [cells[:, c][:, None], cells[:, CH + c][:, None]], axis=1
        ).reshape(128, 128)

    depth = CH // CHUNKS
    copies = []
    for chunk in range(CHUNKS):
        for c in range(depth * chunk, depth * (chunk + 1), 2):
            both = jnp.concatenate([rows(c), rows(c + 1)], axis=1)
            moved = jnp.dot(move, both, preferred_element_type=jnp.float32).astype(jnp.bfloat16)
            scratch[:, c] = moved[:, :128].reshape(8, 16, 128)
            scratch[:, c + 1] = moved[:, 128:].reshape(8, 16, 128)
        span = pl.ds(depth * chunk, depth)
        copy = pltpu.make_async_copy(scratch.at[:, span], out.at[:, span], sems.at[chunk])
        copy.start()
        copies.append(copy)
    for copy in copies:
        copy.wait()


def order(cells):
    return pl.pallas_call(
        order_kernel,
        in_specs=[vmem()],
        out_specs=anywhere(),
        out_shape=jax.ShapeDtypeStruct((8, CH, 16, 128), jnp.bfloat16),
        scratch_shapes=[
            pltpu.VMEM((8, CH, 16, 128), jnp.bfloat16),
            pltpu.SemaphoreType.DMA((CHUNKS,)),
        ],
        compiler_params=vmem_params(),
        cost_estimate=pl.CostEstimate(
            flops=600_000_000, bytes_accessed=5_300_000, transcendentals=0
        ),
    )(cells)


def ring(cells, step):
    count = lax.axis_size("space")
    return lax.ppermute(cells, "space", [(i, (i + step) % count) for i in range(count)])


def per_device(
    prior_ensemble,
    initial_kernel_taps,
    latter_kernel_taps,
    observed_cells,
    observed_count,
    local_radius,
    observed_value,
    error_variance,
):
    members = prior_ensemble.shape[0]
    bf16 = jnp.bfloat16
    own = jnp.swapaxes(prior_ensemble, 1, 2).reshape(members, 16 * CH, 128)
    cells = observed_cells.reshape(8, 128)
    digits = jnp.stack([cells // 6144, cells // 128 % 48, cells % 128]).reshape(24, 128).astype(bf16)
    digits = jnp.concatenate([digits, jnp.zeros((8, 128), bf16)])
    tail = own[:, (16 - HALO) * CH :].reshape(-1, 128)
    head = own[:, : HALO * CH].reshape(-1, 128)
    left = ring(jnp.concatenate([tail, digits]), 1)
    right = ring(jnp.concatenate([head, digits]), -1)

    inner, wide16, wide32 = inner_forecast(own, initial_kernel_taps, latter_kernel_taps)
    first_parts = lax.all_to_all(inner, "mem", split_axis=0, concat_axis=0, tiled=True)
    edge, picked = edge_forecast(inner, cells, left, right, wide16, wide32)

    picked = picked.reshape(3, 8, 8, 128)
    from_left = ring(picked[2], 1)
    from_right = ring(picked[0], -1)
    part = (cells // 128 % 48 // 16).reshape(8, 1, 128)
    here = jnp.where(part == 0, from_left, jnp.where(part == 1, picked[1], from_right))
    message = jnp.concatenate(
        [edge, jnp.broadcast_to(here[None], (8, 8, 8, 128))], axis=1
    )
    message, first_parts = lax.optimization_barrier((message, first_parts))
    second_parts = lax.all_to_all(message, "mem", split_axis=0, concat_axis=0, tiled=True)
    numbers = jnp.stack([observed_count[0], local_radius[0]])
    weights = transform_of(
        second_parts, observed_cells, numbers, observed_value, error_variance
    )
    mixed = mix(first_parts, second_parts, weights)
    back = lax.all_to_all(mixed, "mem", split_axis=0, concat_axis=0, tiled=True)
    return order(back)


def solution(mesh):
    return jax.shard_map(
        per_device,
        mesh=mesh,
        in_specs=(
            P("mem", None, "space", None),
            P(),
            P(),
            P("space", None),
            P("space"),
            P("space"),
            P("space", None),
            P("space", None),
        ),
        out_specs=P("mem", None, "space", None),
        check_vma=False,
    )
```

```python
import functools

import jax
import jax.numpy as jnp
from jax import lax
from jax.experimental import pallas as pl
from jax.experimental.pallas import tpu as pltpu
from jax.sharding import PartitionSpec as P

NS_ITERS = 4
STEP_SIZE = 0.5
HALO = 4
CH = 80
PAIR_A = 8
LAG = 3


def vmem_params():
    return pltpu.CompilerParams(vmem_limit_bytes=40 << 20)


def gelu(x):
    c = 0.7978845608028654
    return 0.5 * x * (1.0 + jnp.tanh(c * (x + 0.044715 * (x * x * x))))


def shifted_sum(p, lane):
    below = pltpu.roll(p[0:80], 1, axis=1)
    above = pltpu.roll(p[160:240], 127, axis=1)
    return p[80:160] + jnp.where(lane == 0, 0.0, below) + jnp.where(lane == 127, 0.0, above)


def conv_pair(source, at, taps, emit, k):
    lane = lax.broadcasted_iota(jnp.int32, (CH, 128), 1)
    window = jnp.concatenate(
        [source[pl.ds(CH * at, 3 * CH), :], source[pl.ds(CH * (at + 1), 3 * CH), :]], axis=1
    )
    partial = jnp.dot(taps, window, preferred_element_type=jnp.float32)
    emit(k, shifted_sum(partial[:, :128], lane))
    emit(k + 1, shifted_sum(partial[:, 128:], lane))


def build_taps(taps, matrix):
    for b in range(3):
        row = jnp.concatenate([taps[3 * a + b].astype(jnp.float32) for a in range(3)], axis=1)
        row = jnp.concatenate([row, jnp.zeros((CH, 256 - 3 * CH), jnp.float32)], axis=1)
        matrix[pl.ds(CH * b, CH), :] = row.astype(jnp.bfloat16)


def run_interleaved(jobs):
    for _, step in sorted(jobs, key=lambda job: job[0]):
        step()


SAVED = 0
OWN = 12 * CH
TAPS = 20 * CH
WIDE16 = 32768
WIDE32 = 16384


def vmem():
    return pl.BlockSpec(memory_space=pltpu.VMEM)


def anywhere():
    return pl.BlockSpec(memory_space=pl.ANY)


def begin(copies, sems, first=0):
    copies = [
        pltpu.make_async_copy(source, target, sems.at[first + i])
        for i, (source, target) in enumerate(copies)
    ]
    for copy in copies:
        copy.start()
    return copies


def finish(copies):
    for copy in copies:
        copy.wait()


def taps_moves(taps, wide):
    moves = []
    for t in range(2):
        for half in range(2):
            here = taps.at[t, :, pl.ds(128 * half, 128)]
            moves.append((here, wide.at[2 * t + half, pl.ds(TAPS, 3 * CH)]))
    return moves


def inner_kernel(
    own, first_taps, second_taps, out, wide16, wide32, taps, h, s, g, rate, fields, cells16, sems
):
    members = own.shape[0]
    build_taps(first_taps, taps.at[0])
    build_taps(second_taps, taps.at[1])
    a = taps[0, :, : 3 * CH]
    b = taps[1, :, : 3 * CH]
    early = [
        (own.at[:, pl.ds(12 * CH * side, 4 * CH)], wide16.at[:, pl.ds(OWN + 4 * CH * side, 4 * CH)])
        for side in range(2)
    ]
    early = begin(early + taps_moves(taps, wide16), sems)

    def group(n, carry):
        jobs = []
        for i in range(PAIR_A):
            m = n * PAIR_A + i
            v, hm, sm, gm, rm = own.at[m], h.at[m], s.at[m], g.at[m], rate.at[m]

            def put_first(k, value, hm=hm):
                hm[pl.ds(CH * k, CH), :] = gelu(value).astype(jnp.bfloat16)

            def put_section(k, value, v=v, sm=sm, rm=rm):
                base = v[pl.ds(CH * (k + 2), CH), :].astype(jnp.float32)
                sm[pl.ds(CH * k, CH), :] = (base + STEP_SIZE * value).astype(jnp.bfloat16)
                rm[pl.ds(CH * k, CH), :] = base + 0.5 * STEP_SIZE * value

            def put_second(k, value, gm=gm):
                gm[pl.ds(CH * k, CH), :] = gelu(value).astype(jnp.bfloat16)

            def put_forecast(k, value, rm=rm, m=m):
                cells = rm[pl.ds(CH * (k + 2), CH), :] + 0.5 * STEP_SIZE * value
                fields[pl.ds(8 * CH * k + m, CH, stride=8), :] = cells

            stages = (
                (v, a, 14, put_first),
                (hm, b, 12, put_section),
                (sm, a, 10, put_second),
                (gm, b, 8, put_forecast),
            )
            for level, (source, matrix, columns, emit) in enumerate(stages):
                for k in range(0, columns, 2):
                    step = functools.partial(conv_pair, source, k, matrix, emit, k)
                    jobs.append(((k // 2 + LAG * level, i, level), step))
        run_interleaved(jobs)
        return carry

    lax.fori_loop(0, members // PAIR_A, group, 0)
    late = []
    for side in range(2):
        for k, (ref, right) in enumerate(((h, 12), (s, 10), (g, 8))):
            target = wide16.at[:, pl.ds(SAVED + 6 * CH * side + 2 * CH * k, 2 * CH)]
            late.append((ref.at[:, pl.ds(CH * right * side, 2 * CH)], target))
        target = wide32.at[:, pl.ds(2 * CH * side, 2 * CH)]
        late.append((rate.at[:, pl.ds(10 * CH * side, 2 * CH)], target))
    late = begin(late, sems, len(early))
    last = []
    for x in range(8):
        column = fields[pl.ds(8 * CH * x, 8 * CH), :].astype(jnp.bfloat16)
        cells16[x] = column.reshape(CH, 8, 128)
        if x % 2:
            pair = pl.ds(x - 1, 2)
            last += begin([(cells16.at[pair], out.at[pair])], sems, len(early) + len(late) + x // 2)
    finish(early + late + last)


def inner_forecast(own, first_taps, second_taps):
    members = own.shape[0]
    bf16, f32 = jnp.bfloat16, jnp.float32
    return pl.pallas_call(
        inner_kernel,
        in_specs=[vmem()] * 3,
        out_specs=[anywhere()] * 3,
        out_shape=[
            jax.ShapeDtypeStruct((8, CH, 8, 128), bf16),
            jax.ShapeDtypeStruct((members, WIDE16, 128), bf16),
            jax.ShapeDtypeStruct((members, WIDE32, 128), f32),
        ],
        scratch_shapes=[
            pltpu.VMEM((2, 3 * CH, 256), bf16),
            pltpu.VMEM((members, 14 * CH, 128), bf16),
            pltpu.VMEM((members, 12 * CH, 128), bf16),
            pltpu.VMEM((members, 10 * CH, 128), bf16),
            pltpu.VMEM((members, 12 * CH, 128), f32),
            pltpu.VMEM((64 * CH, 128), f32),
            pltpu.VMEM((8, CH, 8, 128), bf16),
            pltpu.SemaphoreType.DMA((18,)),
        ],
        compiler_params=vmem_params(),
        cost_estimate=pl.CostEstimate(
            flops=12_000_000_000, bytes_accessed=8_000_000, transcendentals=2_000_000
        ),
    )(own, first_taps, second_taps)


def edge_jobs(side, taps, v, h, s, g, rate, rated, fields, start):
    a = taps[0, :, : 3 * CH]
    b = taps[1, :, : 3 * CH]
    jobs = []
    made = 0 if side == 0 else 2
    for m in range(v.shape[1]):
        vm, hm, sm, gm = v.at[side, m], h.at[side, m], s.at[side, m], g.at[side, m]
        rm, rdm = rate.at[side, m], rated.at[m, pl.ds(2 * CH * side, 2 * CH)]

        def hidden(ref):
            def put(k, value):
                ref[pl.ds(CH * (made + k), CH), :] = gelu(value).astype(jnp.bfloat16)

            return put

        def section(k, value, vm=vm, sm=sm, rm=rm):
            base = vm[pl.ds(CH * (k + 2), CH), :].astype(jnp.float32)
            sm[pl.ds(CH * (made + k), CH), :] = (base + STEP_SIZE * value).astype(jnp.bfloat16)
            inside = k - 2 if side == 0 else k
            if 0 <= inside < 2:
                rm[pl.ds(CH * inside, CH), :] = base + 0.5 * STEP_SIZE * value

        def forecast(k, value, rm=rm, rdm=rdm, m=m):
            source = rm if (k < 2) == (side == 0) else rdm
            value = source[pl.ds(CH * (k % 2), CH), :] + 0.5 * STEP_SIZE * value
            value = value.astype(jnp.bfloat16).astype(jnp.float32)
            fields[pl.ds(start + 8 * CH * k + m, CH, stride=8), :] = value

        stages = (
            (vm, made, a, hidden(hm)),
            (hm, 0, b, section),
            (sm, 0, a, hidden(gm)),
            (gm, 0, b, forecast),
        )
        for level, (source, at, matrix, emit) in enumerate(stages):
            for k in (0, 2):
                step = functools.partial(conv_pair, source, at + k, matrix, emit, k)
                jobs.append(((level, m, side, k), step))
    return jobs


def place_of(channel, lon, lat, part):
    slot = lax.broadcasted_iota(jnp.int32, (8, 128), 1)
    lon = lon - 16 * part
    column = jnp.where(lon < 4, lon + 8, jnp.where(lon < 12, lon - 4, lon))
    here = (lon >= 0) & (lon < 16)
    return jnp.where(here, (column * CH + channel) * 8, 0), (slot - lat) & 127


def edge_kernel(
    inner, cells, left, right, wide16, wide32, out, picked,
    taps, v, h, s, g, rate, rated, fields, inner16, lists, own_list, places, rows, turns,
    sems, list_sems, place_sems,
):
    members = v.shape[1]
    halo = CH * HALO
    digits = halo * members
    early = begin([(there, here) for here, there in taps_moves(taps, wide16)], sems)
    list_copies = begin(
        [(left.at[pl.ds(digits, 32)], lists.at[0]), (right.at[pl.ds(digits, 32)], lists.at[1]), (cells, own_list)],
        list_sems,
    )
    columns = []
    used = len(early)
    for m in range(members):
        moves = []
        for side, source in enumerate((left, right)):
            edge = v.at[side, m]
            moves.append((source.at[pl.ds(halo * m, halo)], edge.at[pl.ds(4 * CH * side, 4 * CH)]))
            source = wide16.at[m, pl.ds(OWN + 4 * CH * side, 4 * CH)]
            moves.append((source, edge.at[pl.ds(4 * CH * (1 - side), 4 * CH)]))
        columns.append(begin(moves, sems, used))
        used += len(moves)
    moves = []
    for k, ref in enumerate((h, s, g)):
        for side in range(2):
            source = wide16.at[:, pl.ds(SAVED + 6 * CH * side + 2 * CH * k, 2 * CH)]
            moves.append((source, ref.at[side, :, pl.ds(4 * CH * (1 - side), 2 * CH)]))
    moves.append((wide32.at[:, pl.ds(0, 4 * CH)], rated))
    later = begin(moves, sems, used)
    inner_copy = begin([(inner, inner16)], list_sems, 3)
    finish(list_copies)
    for k in range(3):
        if k == 1:
            cell = own_list[...]
            strip = cell >> 7
            channel = (strip * 43691) >> 21
            parts = (channel, strip - 48 * channel, cell & 127)
        else:
            block = lists[k // 2].astype(jnp.float32).astype(jnp.int32)
            parts = (block[0:8], block[8:16], block[16:24])
        row, turn = place_of(*parts, 2 - k)
        places[0, pl.ds(8 * k, 8), :] = row
        places[1, pl.ds(8 * k, 8), :] = turn
    place_copies = begin([(places.at[0], rows), (places.at[1], turns)], place_sems)
    finish(early)
    jobs = []
    for side in range(2):
        jobs += edge_jobs(side, taps, v, h, s, g, rate, rated, fields, (64 + 32 * side) * CH)

    for n in range(2):
        for m in range(4 * n, 4 * n + 4):
            jobs.append(((0, 4 * n, -1, 0), functools.partial(finish, columns[m])))
    jobs.append(((1, -1, 0, 0), functools.partial(finish, later + inner_copy)))
    run_interleaved(jobs)
    fields[pl.ds(0, 64 * CH), :] = inner16[...].astype(jnp.float32).reshape(64 * CH, 128)
    out[...] = fields[pl.ds(64 * CH, 64 * CH), :].astype(jnp.bfloat16).reshape(out.shape)
    finish(place_copies)
    lane = lax.broadcasted_iota(jnp.int32, (8, 128), 1)

    def block(k, carry):
        found = [jnp.zeros((8, 128), jnp.float32)] * 3
        for j in range(128):
            for q in range(3):
                cell = fields[pl.ds(pl.multiple_of(rows[8 * q + k, j], 8), 8), :]
                cell = pltpu.roll(cell, turns[8 * q + k, j], axis=1)
                found[q] = jnp.where(lane == j, cell, found[q])
        for q in range(3):
            picked[8 * q + k] = found[q].astype(jnp.bfloat16)
        return carry

    lax.fori_loop(0, 8, block, 0)


def edge_forecast(inner, cells, left, right, wide16, wide32):
    bf16, f32 = jnp.bfloat16, jnp.float32
    members = wide16.shape[0]
    return pl.pallas_call(
        edge_kernel,
        in_specs=[anywhere()] * 6,
        out_specs=[vmem()] * 2,
        out_shape=[
            jax.ShapeDtypeStruct((8, CH, 8, 128), bf16),
            jax.ShapeDtypeStruct((24, 8, 128), bf16),
        ],
        scratch_shapes=[
            pltpu.VMEM((2, 3 * CH, 256), bf16),
            pltpu.VMEM((2, members, 8 * CH, 128), bf16),
            pltpu.VMEM((2, members, 6 * CH, 128), bf16),
            pltpu.VMEM((2, members, 6 * CH, 128), bf16),
            pltpu.VMEM((2, members, 6 * CH, 128), bf16),
            pltpu.VMEM((2, members, 2 * CH, 128), f32),
            pltpu.VMEM((members, 4 * CH, 128), f32),
            pltpu.VMEM((128 * CH, 128), f32),
            pltpu.VMEM((8, CH, 8, 128), bf16),
            pltpu.VMEM((2, 32, 128), bf16),
            pltpu.VMEM((8, 128), jnp.int32),
            pltpu.VMEM((2, 24, 128), jnp.int32),
            pltpu.SMEM((24, 128), jnp.int32),
            pltpu.SMEM((24, 128), jnp.int32),
            pltpu.SemaphoreType.DMA((4 * members + 11,)),
            pltpu.SemaphoreType.DMA((4,)),
            pltpu.SemaphoreType.DMA((2,)),
        ],
        compiler_params=vmem_params(),
        cost_estimate=pl.CostEstimate(
            flops=9_000_000_000, bytes_accessed=8_000_000, transcendentals=2_000_000
        ),
    )(inner, cells, left, right, wide16, wide32)


def transform_kernel(here, pair, ahead, across, behind, cells, numbers, observed, variance, out, stack):
    f32 = jnp.float32
    exact = lax.Precision.HIGH
    depth = numbers[2] & 3
    half = numbers[2] >> 2
    for step, ref in enumerate((None, ahead, across, behind)):
        for other in range(2):
            group = 4 * (half ^ other) + ((depth + step) & 3)
            rows = pl.ds(pl.multiple_of(8 * group, 8), 8)
            for block in range(8):
                if ref is None:
                    value = (here, pair)[other][block]
                else:
                    value = ref[other, block]
                stack[rows, pl.ds(128 * block, 128)] = value.astype(f32)
    model_obs = stack[...]
    center = jnp.sum(model_obs, axis=0, keepdims=True) * (1.0 / 64.0)
    spread = model_obs - center
    cell = cells[...]
    strip = cell >> 7
    lon = strip - 48 * ((strip * 43691) >> 21)
    scaled = (lon.astype(f32) - 23.5) / numbers[1].astype(f32)
    taper = jnp.exp(-0.5 * scaled * scaled)
    slot = lax.broadcasted_iota(jnp.int32, cell.shape, 1)
    weight = jnp.where(slot < numbers[0], taper / variance[...], 0.0)
    weighted = spread * weight

    def product(x, y):
        return jnp.dot(x, y, precision=exact, preferred_element_type=f32)

    gram = lax.dot_general(
        weighted, spread, (((1,), (1,)), ((), ())), precision=exact, preferred_element_type=f32
    )
    right_side = jnp.sum(weighted * (observed[...] - center), axis=1, keepdims=True)
    i = lax.broadcasted_iota(jnp.int32, (64, 64), 0)
    j = lax.broadcasted_iota(jnp.int32, (64, 64), 1)
    eye = jnp.where(i == j, 1.0, 0.0).astype(f32)
    norm = 63.0 + jnp.sqrt(jnp.sum(jnp.sum(gram * gram, axis=1, keepdims=True), axis=0, keepdims=True))
    iterate = (63.0 * eye + gram) / norm
    root = 1.5 * eye - 0.5 * iterate
    iterate = product(iterate, root)
    for sweep in range(1, NS_ITERS):
        factor = 1.5 * eye - 0.5 * product(root, iterate)
        if sweep < NS_ITERS - 1:
            iterate = product(iterate, factor)
        root = product(factor, root)
    wide = jnp.broadcast_to(right_side, (64, 128))
    shift = product(root, product(root, wide)) / norm
    transform = (shift[:, :64] + jnp.sqrt(63.0 / norm) * root).astype(jnp.bfloat16)
    i = lax.broadcasted_iota(jnp.int32, (64, 256), 0)
    j = lax.broadcasted_iota(jnp.int32, (64, 256), 1)
    for q in range(4):
        place = jnp.where(j == i + 64 * q, 1.0, 0.0).astype(jnp.bfloat16)
        turned = lax.dot_general(
            transform, place, (((0,), (0,)), ((), ())), preferred_element_type=f32
        )
        out[pl.ds(64 * q, 64), :] = turned.astype(jnp.bfloat16)


def transform_of(pieces, cells, numbers, observed, variance):
    smem = pl.BlockSpec(memory_space=pltpu.SMEM)
    return pl.pallas_call(
        transform_kernel,
        in_specs=[vmem()] * 6 + [smem, vmem(), vmem()],
        out_specs=vmem(),
        out_shape=jax.ShapeDtypeStruct((256, 256), jnp.bfloat16),
        scratch_shapes=[pltpu.VMEM((64, 1024), jnp.float32)],
        compiler_params=vmem_params(),
        cost_estimate=pl.CostEstimate(
            flops=100_000_000, bytes_accessed=500_000, transcendentals=1000
        ),
    )(*pieces, cells, numbers, observed, variance)


def spread_rows(parts, first):
    centers = []
    halves = []
    for half in range(2):
        stack = []
        for q in range(4):
            value = parts[:, first + 4 * half + q].astype(jnp.float32)
            center = jnp.sum(jnp.sum(value, axis=0), axis=0, keepdims=True) * (1.0 / 64.0)
            centers.append(center)
            stack.append((value.reshape(64, 128) - center).astype(jnp.bfloat16))
        halves.append(jnp.concatenate(stack, axis=0))
    return jnp.concatenate(halves, axis=1), centers


def mix_rows(spread, centers, w, out, start):
    mixed = jnp.dot(w, spread, preferred_element_type=jnp.float32)
    for half in range(2):
        for q in range(4):
            value = mixed[64 * q : 64 * q + 64, 128 * half : 128 * half + 128]
            value = value + centers[4 * half + q]
            out[:, start + 4 * half + q] = value.astype(jnp.bfloat16).reshape(8, 8, 128)


def mix_kernel(first, second, weights, out):
    w = weights[...]

    def half(parts, start):
        def block(n, carry):
            for k in range(5):
                row = (5 * n + k) * 8
                mix_rows(*spread_rows(parts, row), w, out, start + row)
            return carry

        lax.fori_loop(0, 2, block, 0)

    half(first, 0)
    half(second, CH)


def mix(first, second, weights):
    return pl.pallas_call(
        mix_kernel,
        in_specs=[vmem()] * 3,
        out_specs=vmem(),
        out_shape=jax.ShapeDtypeStruct((8, 160, 8, 128), jnp.bfloat16),
        compiler_params=vmem_params(),
        cost_estimate=pl.CostEstimate(
            flops=700_000_000, bytes_accessed=5_300_000, transcendentals=0
        ),
    )(first, second, weights)


CHUNKS = 5


def order_kernel(cells, out, scratch, sems):
    to = lax.broadcasted_iota(jnp.int32, (128, 128), 0)
    at = lax.broadcasted_iota(jnp.int32, (128, 128), 1)
    source = at >> 4
    side = (at >> 3) & 1
    column = jnp.where(side == 0, source + 4, jnp.where(source < 4, source, source + 8))
    move = jnp.where(to == (at & 7) * 16 + column, 1.0, 0.0).astype(jnp.bfloat16)

    def rows(c):
        return jnp.concatenate(
            [cells[:, c][:, None], cells[:, CH + c][:, None]], axis=1
        ).reshape(128, 128)

    depth = CH // CHUNKS
    copies = []
    for chunk in range(CHUNKS):
        for c in range(depth * chunk, depth * (chunk + 1), 2):
            both = jnp.concatenate([rows(c), rows(c + 1)], axis=1)
            moved = jnp.dot(move, both, preferred_element_type=jnp.float32).astype(jnp.bfloat16)
            scratch[:, c] = moved[:, :128].reshape(8, 16, 128)
            scratch[:, c + 1] = moved[:, 128:].reshape(8, 16, 128)
        span = pl.ds(depth * chunk, depth)
        copy = pltpu.make_async_copy(scratch.at[:, span], out.at[:, span], sems.at[chunk])
        copy.start()
        copies.append(copy)
    for copy in copies:
        copy.wait()


def order(cells):
    return pl.pallas_call(
        order_kernel,
        in_specs=[vmem()],
        out_specs=anywhere(),
        out_shape=jax.ShapeDtypeStruct((8, CH, 16, 128), jnp.bfloat16),
        scratch_shapes=[
            pltpu.VMEM((8, CH, 16, 128), jnp.bfloat16),
            pltpu.SemaphoreType.DMA((CHUNKS,)),
        ],
        compiler_params=vmem_params(),
        cost_estimate=pl.CostEstimate(
            flops=600_000_000, bytes_accessed=5_300_000, transcendentals=0
        ),
    )(cells)


def ring(cells, step):
    count = lax.axis_size("space")
    return lax.ppermute(cells, "space", [(i, (i + step) % count) for i in range(count)])


def depth_ring(cells, step):
    return lax.ppermute(
        cells, "mem", [(4 * y + (z + step) % 4, 4 * y + z) for y in range(2) for z in range(4)]
    )


def per_device(
    prior_ensemble,
    initial_kernel_taps,
    latter_kernel_taps,
    observed_cells,
    observed_count,
    local_radius,
    observed_value,
    error_variance,
):
    members = prior_ensemble.shape[0]
    bf16 = jnp.bfloat16
    own = jnp.swapaxes(prior_ensemble, 1, 2).reshape(members, 16 * CH, 128)
    cells = observed_cells.reshape(8, 128)
    digits = jnp.stack([cells // 6144, cells // 128 % 48, cells % 128]).reshape(24, 128).astype(bf16)
    digits = jnp.concatenate([digits, jnp.zeros((8, 128), bf16)])
    tail = own[:, (16 - HALO) * CH :].reshape(-1, 128)
    head = own[:, : HALO * CH].reshape(-1, 128)
    left = ring(jnp.concatenate([tail, digits]), 1)
    right = ring(jnp.concatenate([head, digits]), -1)

    inner, wide16, wide32 = inner_forecast(own, initial_kernel_taps, latter_kernel_taps)
    first_parts = lax.all_to_all(inner, "mem", split_axis=0, concat_axis=0, tiled=True)
    edge, picked = edge_forecast(inner, cells, left, right, wide16, wide32)

    picked = picked.reshape(3, 8, 8, 128)
    from_left = ring(picked[2], 1)
    from_right = ring(picked[0], -1)
    part = (cells // 128 % 48 // 16).reshape(8, 1, 128)
    here = jnp.where(part == 0, from_left, jnp.where(part == 1, picked[1], from_right))
    edge, first_parts = lax.optimization_barrier((edge, first_parts))
    second_parts = lax.all_to_all(edge, "mem", split_axis=0, concat_axis=0, tiled=True)
    pair = lax.ppermute(here, "mem", [(i, i ^ 4) for i in range(8)])
    both = jnp.stack([here, pair])
    pieces = (here, pair, depth_ring(both, 1), depth_ring(both, 2), depth_ring(both, 3))
    group = lax.axis_index("mem").astype(jnp.int32)
    numbers = jnp.stack([observed_count[0], local_radius[0], group])
    weights = transform_of(pieces, observed_cells, numbers, observed_value, error_variance)
    mixed = mix(first_parts, second_parts, weights)
    back = lax.all_to_all(mixed, "mem", split_axis=0, concat_axis=0, tiled=True)
    return order(back)


def solution(mesh):
    return jax.shard_map(
        per_device,
        mesh=mesh,
        in_specs=(
            P("mem", None, "space", None),
            P(),
            P(),
            P("space", None),
            P("space"),
            P("space"),
            P("space", None),
            P("space", None),
        ),
        out_specs=P("mem", None, "space", None),
        check_vma=False,
    )
```

```python
import functools

import jax
import jax.numpy as jnp
from jax import lax
from jax.experimental import pallas as pl
from jax.experimental.pallas import tpu as pltpu
from jax.sharding import PartitionSpec as P

NS_ITERS = 4
STEP_SIZE = 0.5
HALO = 4
CH = 80
LAG = 4


def vmem_params():
    return pltpu.CompilerParams(vmem_limit_bytes=40 << 20)


def gelu(x):
    c = 0.7978845608028654
    return 0.5 * x * (1.0 + jnp.tanh(c * (x + 0.044715 * (x * x * x))))


def shifted_sum(p, lane):
    below = pltpu.roll(p[0:80], 1, axis=1)
    above = pltpu.roll(p[160:240], 127, axis=1)
    return p[80:160] + jnp.where(lane == 0, 0.0, below) + jnp.where(lane == 127, 0.0, above)


def conv_pair(source, at, taps, emit, k):
    lane = lax.broadcasted_iota(jnp.int32, (CH, 128), 1)
    window = jnp.concatenate(
        [source[pl.ds(CH * at, 3 * CH), :], source[pl.ds(CH * (at + 1), 3 * CH), :]], axis=1
    )
    partial = jnp.dot(taps, window, preferred_element_type=jnp.float32)
    emit(k, shifted_sum(partial[:, :128], lane))
    emit(k + 1, shifted_sum(partial[:, 128:], lane))


def build_taps(taps, matrix):
    for b in range(3):
        row = jnp.concatenate([taps[3 * a + b].astype(jnp.float32) for a in range(3)], axis=1)
        row = jnp.concatenate([row, jnp.zeros((CH, 256 - 3 * CH), jnp.float32)], axis=1)
        matrix[pl.ds(CH * b, CH), :] = row.astype(jnp.bfloat16)


def run_interleaved(jobs):
    for _, step in sorted(jobs, key=lambda job: job[0]):
        step()


SAVED = 0
OWN = 12 * CH
TAPS = 20 * CH
WIDE16 = 32768
WIDE32 = 16384


def vmem():
    return pl.BlockSpec(memory_space=pltpu.VMEM)


def anywhere():
    return pl.BlockSpec(memory_space=pl.ANY)


def begin(copies, sems, first=0):
    copies = [
        pltpu.make_async_copy(source, target, sems.at[first + i])
        for i, (source, target) in enumerate(copies)
    ]
    for copy in copies:
        copy.start()
    return copies


def finish(copies):
    for copy in copies:
        copy.wait()


def taps_moves(taps, wide):
    moves = []
    for t in range(2):
        for half in range(2):
            here = taps.at[t, :, pl.ds(128 * half, 128)]
            moves.append((here, wide.at[2 * t + half, pl.ds(TAPS, 3 * CH)]))
    return moves


def inner_kernel(
    own, first_taps, second_taps, out, wide16, wide32, taps, h, s, g, rate, fields, cells16, sems
):
    members = own.shape[0]
    build_taps(first_taps, taps.at[0])
    build_taps(second_taps, taps.at[1])
    a = taps[0, :, : 3 * CH]
    b = taps[1, :, : 3 * CH]
    early = [
        (own.at[:, pl.ds(12 * CH * side, 4 * CH)], wide16.at[:, pl.ds(OWN + 4 * CH * side, 4 * CH)])
        for side in range(2)
    ]
    early = begin(early + taps_moves(taps, wide16), sems)

    sent = []

    def save(source, target):
        sent.extend(begin([(source, target)], sems, len(early) + len(sent)))

    def send(x):
        for column in (x, x + 1):
            cells = fields[pl.ds(8 * CH * column, 8 * CH), :].astype(jnp.bfloat16)
            cells16[column] = cells.reshape(CH, 8, 128)
        save(cells16.at[pl.ds(x, 2)], out.at[pl.ds(x, 2)])

    jobs = []
    for side in range(2):
        for level, ref, right, ready in ((0, h, 12, 6), (1, s, 10, 5 + LAG), (2, g, 8, 4 + 2 * LAG)):
            source = ref.at[:, pl.ds(CH * right * side, 2 * CH)]
            target = wide16.at[:, pl.ds(SAVED + 6 * CH * side + 2 * CH * level, 2 * CH)]
            jobs.append(((ready, members, side), functools.partial(save, source, target)))
        source = rate.at[:, pl.ds(10 * CH * side, 2 * CH)]
        target = wide32.at[:, pl.ds(2 * CH * side, 2 * CH)]
        jobs.append(((5 + LAG, members, 2 + side), functools.partial(save, source, target)))
    for k in range(0, 8, 2):
        jobs.append(((k // 2 + 3 * LAG, members, 4), functools.partial(send, k)))
    for m in range(members):
        v, hm, sm, gm, rm = own.at[m], h.at[m], s.at[m], g.at[m], rate.at[m]

        def put_first(k, value, hm=hm):
            hm[pl.ds(CH * k, CH), :] = gelu(value).astype(jnp.bfloat16)

        def put_section(k, value, v=v, sm=sm, rm=rm):
            base = v[pl.ds(CH * (k + 2), CH), :].astype(jnp.float32)
            sm[pl.ds(CH * k, CH), :] = (base + STEP_SIZE * value).astype(jnp.bfloat16)
            rm[pl.ds(CH * k, CH), :] = base + 0.5 * STEP_SIZE * value

        def put_second(k, value, gm=gm):
            gm[pl.ds(CH * k, CH), :] = gelu(value).astype(jnp.bfloat16)

        def put_forecast(k, value, rm=rm, m=m):
            cells = rm[pl.ds(CH * (k + 2), CH), :] + 0.5 * STEP_SIZE * value
            fields[pl.ds(8 * CH * k + m, CH, stride=8), :] = cells

        stages = (
            (v, a, 14, put_first),
            (hm, b, 12, put_section),
            (sm, a, 10, put_second),
            (gm, b, 8, put_forecast),
        )
        for level, (source, matrix, columns, emit) in enumerate(stages):
            for k in range(0, columns, 2):
                step = functools.partial(conv_pair, source, k, matrix, emit, k)
                jobs.append(((k // 2 + LAG * level, m, level), step))
    run_interleaved(jobs)
    finish(early + sent)


def inner_forecast(own, first_taps, second_taps):
    members = own.shape[0]
    bf16, f32 = jnp.bfloat16, jnp.float32
    return pl.pallas_call(
        inner_kernel,
        in_specs=[vmem()] * 3,
        out_specs=[anywhere()] * 3,
        out_shape=[
            jax.ShapeDtypeStruct((8, CH, 8, 128), bf16),
            jax.ShapeDtypeStruct((members, WIDE16, 128), bf16),
            jax.ShapeDtypeStruct((members, WIDE32, 128), f32),
        ],
        scratch_shapes=[
            pltpu.VMEM((2, 3 * CH, 256), bf16),
            pltpu.VMEM((members, 14 * CH, 128), bf16),
            pltpu.VMEM((members, 12 * CH, 128), bf16),
            pltpu.VMEM((members, 10 * CH, 128), bf16),
            pltpu.VMEM((members, 12 * CH, 128), f32),
            pltpu.VMEM((64 * CH, 128), f32),
            pltpu.VMEM((8, CH, 8, 128), bf16),
            pltpu.SemaphoreType.DMA((18,)),
        ],
        compiler_params=vmem_params(),
        cost_estimate=pl.CostEstimate(
            flops=12_000_000_000, bytes_accessed=8_000_000, transcendentals=2_000_000
        ),
    )(own, first_taps, second_taps)


def edge_jobs(side, taps, v, h, s, g, rate, rated, fields, start):
    a = taps[0, :, : 3 * CH]
    b = taps[1, :, : 3 * CH]
    jobs = []
    made = 0 if side == 0 else 2
    for m in range(v.shape[1]):
        vm, hm, sm, gm = v.at[side, m], h.at[side, m], s.at[side, m], g.at[side, m]
        rm, rdm = rate.at[side, m], rated.at[m, pl.ds(2 * CH * side, 2 * CH)]

        def hidden(ref):
            def put(k, value):
                ref[pl.ds(CH * (made + k), CH), :] = gelu(value).astype(jnp.bfloat16)

            return put

        def section(k, value, vm=vm, sm=sm, rm=rm):
            base = vm[pl.ds(CH * (k + 2), CH), :].astype(jnp.float32)
            sm[pl.ds(CH * (made + k), CH), :] = (base + STEP_SIZE * value).astype(jnp.bfloat16)
            inside = k - 2 if side == 0 else k
            if 0 <= inside < 2:
                rm[pl.ds(CH * inside, CH), :] = base + 0.5 * STEP_SIZE * value

        def forecast(k, value, rm=rm, rdm=rdm, m=m):
            source = rm if (k < 2) == (side == 0) else rdm
            value = source[pl.ds(CH * (k % 2), CH), :] + 0.5 * STEP_SIZE * value
            value = value.astype(jnp.bfloat16).astype(jnp.float32)
            fields[pl.ds(start + 8 * CH * k + m, CH, stride=8), :] = value

        stages = (
            (vm, made, a, hidden(hm)),
            (hm, 0, b, section),
            (sm, 0, a, hidden(gm)),
            (gm, 0, b, forecast),
        )
        for level, (source, at, matrix, emit) in enumerate(stages):
            for k in (0, 2):
                step = functools.partial(conv_pair, source, at + k, matrix, emit, k)
                jobs.append(((level, m, side, k), step))
    return jobs


def place_of(channel, lon, lat, part):
    slot = lax.broadcasted_iota(jnp.int32, (8, 128), 1)
    lon = lon - 16 * part
    column = jnp.where(lon < 4, lon + 8, jnp.where(lon < 12, lon - 4, lon))
    here = (lon >= 0) & (lon < 16)
    return jnp.where(here, (column * CH + channel) * 8, 0), (slot - lat) & 127


def edge_kernel(
    inner, cells, left, right, wide16, wide32, out, picked,
    taps, v, h, s, g, rate, rated, fields, inner16, cells16, lists, own_list, places, rows, turns,
    sems, list_sems, place_sems,
):
    members = v.shape[1]
    halo = CH * HALO
    digits = halo * members
    early = begin([(there, here) for here, there in taps_moves(taps, wide16)], sems)
    list_copies = begin(
        [(left.at[pl.ds(digits, 32)], lists.at[0]), (right.at[pl.ds(digits, 32)], lists.at[1]), (cells, own_list)],
        list_sems,
    )
    columns = []
    used = len(early)
    for m in range(members):
        moves = []
        for side, source in enumerate((left, right)):
            edge = v.at[side, m]
            moves.append((source.at[pl.ds(halo * m, halo)], edge.at[pl.ds(4 * CH * side, 4 * CH)]))
            source = wide16.at[m, pl.ds(OWN + 4 * CH * side, 4 * CH)]
            moves.append((source, edge.at[pl.ds(4 * CH * (1 - side), 4 * CH)]))
        columns.append(begin(moves, sems, used))
        used += len(moves)
    moves = []
    for k, ref in enumerate((h, s, g)):
        for side in range(2):
            source = wide16.at[:, pl.ds(SAVED + 6 * CH * side + 2 * CH * k, 2 * CH)]
            moves.append((source, ref.at[side, :, pl.ds(4 * CH * (1 - side), 2 * CH)]))
    moves.append((wide32.at[:, pl.ds(0, 4 * CH)], rated))
    later = begin(moves, sems, used)
    inner_copy = begin([(inner, inner16)], list_sems, 3)
    finish(list_copies)
    for k in range(3):
        if k == 1:
            cell = own_list[...]
            strip = cell >> 7
            channel = (strip * 43691) >> 21
            parts = (channel, strip - 48 * channel, cell & 127)
        else:
            block = lists[k // 2].astype(jnp.float32).astype(jnp.int32)
            parts = (block[0:8], block[8:16], block[16:24])
        row, turn = place_of(*parts, 2 - k)
        places[0, pl.ds(8 * k, 8), :] = row
        places[1, pl.ds(8 * k, 8), :] = turn
    place_copies = begin([(places.at[0], rows), (places.at[1], turns)], place_sems)
    finish(early)
    jobs = []
    for side in range(2):
        jobs += edge_jobs(side, taps, v, h, s, g, rate, rated, fields, (64 + 32 * side) * CH)

    for n in range(2):
        for m in range(4 * n, 4 * n + 4):
            jobs.append(((0, 4 * n, -1, 0), functools.partial(finish, columns[m])))
    jobs.append(((1, -1, 0, 0), functools.partial(finish, later + inner_copy)))
    run_interleaved(jobs)
    cells16[...] = fields[pl.ds(64 * CH, 64 * CH), :].astype(jnp.bfloat16).reshape(cells16.shape)
    out_copy = begin([(cells16, out)], sems, 0)
    fields[pl.ds(0, 64 * CH), :] = inner16[...].astype(jnp.float32).reshape(64 * CH, 128)
    finish(place_copies)
    lane = lax.broadcasted_iota(jnp.int32, (8, 128), 1)

    def block(k, carry):
        found = [jnp.zeros((8, 128), jnp.float32)] * 3
        for j in range(128):
            for q in range(3):
                cell = fields[pl.ds(pl.multiple_of(rows[8 * q + k, j], 8), 8), :]
                cell = pltpu.roll(cell, turns[8 * q + k, j], axis=1)
                found[q] = jnp.where(lane == j, cell, found[q])
        for q in range(3):
            picked[8 * q + k] = found[q].astype(jnp.bfloat16)
        return carry

    lax.fori_loop(0, 8, block, 0)
    finish(out_copy)


def edge_forecast(inner, cells, left, right, wide16, wide32):
    bf16, f32 = jnp.bfloat16, jnp.float32
    members = wide16.shape[0]
    return pl.pallas_call(
        edge_kernel,
        in_specs=[anywhere()] * 6,
        out_specs=[anywhere(), vmem()],
        out_shape=[
            jax.ShapeDtypeStruct((8, CH, 8, 128), bf16),
            jax.ShapeDtypeStruct((24, 8, 128), bf16),
        ],
        scratch_shapes=[
            pltpu.VMEM((2, 3 * CH, 256), bf16),
            pltpu.VMEM((2, members, 8 * CH, 128), bf16),
            pltpu.VMEM((2, members, 6 * CH, 128), bf16),
            pltpu.VMEM((2, members, 6 * CH, 128), bf16),
            pltpu.VMEM((2, members, 6 * CH, 128), bf16),
            pltpu.VMEM((2, members, 2 * CH, 128), f32),
            pltpu.VMEM((members, 4 * CH, 128), f32),
            pltpu.VMEM((128 * CH, 128), f32),
            pltpu.VMEM((8, CH, 8, 128), bf16),
            pltpu.VMEM((8, CH, 8, 128), bf16),
            pltpu.VMEM((2, 32, 128), bf16),
            pltpu.VMEM((8, 128), jnp.int32),
            pltpu.VMEM((2, 24, 128), jnp.int32),
            pltpu.SMEM((24, 128), jnp.int32),
            pltpu.SMEM((24, 128), jnp.int32),
            pltpu.SemaphoreType.DMA((4 * members + 11,)),
            pltpu.SemaphoreType.DMA((4,)),
            pltpu.SemaphoreType.DMA((2,)),
        ],
        compiler_params=vmem_params(),
        cost_estimate=pl.CostEstimate(
            flops=9_000_000_000, bytes_accessed=8_000_000, transcendentals=2_000_000
        ),
    )(inner, cells, left, right, wide16, wide32)


def transform_kernel(
    here, pair, ahead, across, behind, cells, numbers, observed, variance, edge, out, stack
):
    del edge
    f32 = jnp.float32
    exact = lax.Precision.HIGH
    depth = numbers[2] & 3
    half = numbers[2] >> 2
    for step, ref in enumerate((None, ahead, across, behind)):
        for other in range(2):
            group = 4 * (half ^ other) + ((depth + step) & 3)
            rows = pl.ds(pl.multiple_of(8 * group, 8), 8)
            for block in range(8):
                if ref is None:
                    value = (here, pair)[other][block]
                else:
                    value = ref[other, block]
                stack[rows, pl.ds(128 * block, 128)] = value.astype(f32)
    model_obs = stack[...]
    center = jnp.sum(model_obs, axis=0, keepdims=True) * (1.0 / 64.0)
    spread = model_obs - center
    cell = cells[...]
    strip = cell >> 7
    lon = strip - 48 * ((strip * 43691) >> 21)
    scaled = (lon.astype(f32) - 23.5) / numbers[1].astype(f32)
    taper = jnp.exp(-0.5 * scaled * scaled)
    slot = lax.broadcasted_iota(jnp.int32, cell.shape, 1)
    weight = jnp.where(slot < numbers[0], taper / variance[...], 0.0)
    weighted = spread * weight

    def product(x, y):
        return jnp.dot(x, y, precision=exact, preferred_element_type=f32)

    gram = lax.dot_general(
        weighted, spread, (((1,), (1,)), ((), ())), precision=exact, preferred_element_type=f32
    )
    right_side = jnp.sum(weighted * (observed[...] - center), axis=1, keepdims=True)
    i = lax.broadcasted_iota(jnp.int32, (64, 64), 0)
    j = lax.broadcasted_iota(jnp.int32, (64, 64), 1)
    eye = jnp.where(i == j, 1.0, 0.0).astype(f32)
    norm = 63.0 + jnp.sqrt(jnp.sum(jnp.sum(gram * gram, axis=1, keepdims=True), axis=0, keepdims=True))
    iterate = (63.0 * eye + gram) / norm
    root = 1.5 * eye - 0.5 * iterate
    iterate = product(iterate, root)
    for sweep in range(1, NS_ITERS):
        factor = 1.5 * eye - 0.5 * product(root, iterate)
        if sweep < NS_ITERS - 1:
            iterate = product(iterate, factor)
        root = product(factor, root)
    wide = jnp.broadcast_to(right_side, (64, 128))
    shift = product(root, product(root, wide)) / norm
    transform = (shift[:, :64] + jnp.sqrt(63.0 / norm) * root).astype(jnp.bfloat16)
    i = lax.broadcasted_iota(jnp.int32, (64, 256), 0)
    j = lax.broadcasted_iota(jnp.int32, (64, 256), 1)
    for q in range(4):
        place = jnp.where(j == i + 64 * q, 1.0, 0.0).astype(jnp.bfloat16)
        turned = lax.dot_general(
            transform, place, (((0,), (0,)), ((), ())), preferred_element_type=f32
        )
        out[pl.ds(64 * q, 64), :] = turned.astype(jnp.bfloat16)


def transform_of(pieces, cells, numbers, observed, variance, edge):
    smem = pl.BlockSpec(memory_space=pltpu.SMEM)
    return pl.pallas_call(
        transform_kernel,
        in_specs=[vmem()] * 6 + [smem, vmem(), vmem(), anywhere()],
        out_specs=vmem(),
        out_shape=jax.ShapeDtypeStruct((256, 256), jnp.bfloat16),
        scratch_shapes=[pltpu.VMEM((64, 1024), jnp.float32)],
        compiler_params=vmem_params(),
        cost_estimate=pl.CostEstimate(
            flops=100_000_000, bytes_accessed=500_000, transcendentals=1000
        ),
    )(*pieces, cells, numbers, observed, variance, edge)


def spread_rows(parts, first):
    centers = []
    halves = []
    for half in range(2):
        stack = []
        for q in range(4):
            value = parts[:, first + 4 * half + q].astype(jnp.float32)
            center = jnp.sum(jnp.sum(value, axis=0), axis=0, keepdims=True) * (1.0 / 64.0)
            centers.append(center)
            stack.append((value.reshape(64, 128) - center).astype(jnp.bfloat16))
        halves.append(jnp.concatenate(stack, axis=0))
    return jnp.concatenate(halves, axis=1), centers


def mix_rows(spread, centers, w, out, start):
    mixed = jnp.dot(w, spread, preferred_element_type=jnp.float32)
    for half in range(2):
        for q in range(4):
            value = mixed[64 * q : 64 * q + 64, 128 * half : 128 * half + 128]
            value = value + centers[4 * half + q]
            out[:, start + 4 * half + q] = value.astype(jnp.bfloat16).reshape(8, 8, 128)


def mix_kernel(first, second, weights, out):
    w = weights[...]

    def half(parts, start):
        def block(n, carry):
            for k in range(5):
                row = (5 * n + k) * 8
                mix_rows(*spread_rows(parts, row), w, out, start + row)
            return carry

        lax.fori_loop(0, 2, block, 0)

    half(first, 0)
    half(second, CH)


def mix(first, second, weights):
    return pl.pallas_call(
        mix_kernel,
        in_specs=[vmem()] * 3,
        out_specs=vmem(),
        out_shape=jax.ShapeDtypeStruct((8, 160, 8, 128), jnp.bfloat16),
        compiler_params=vmem_params(),
        cost_estimate=pl.CostEstimate(
            flops=700_000_000, bytes_accessed=5_300_000, transcendentals=0
        ),
    )(first, second, weights)


CHUNKS = 5


def order_kernel(cells, out, scratch, sems):
    to = lax.broadcasted_iota(jnp.int32, (128, 128), 0)
    at = lax.broadcasted_iota(jnp.int32, (128, 128), 1)
    source = at >> 4
    side = (at >> 3) & 1
    column = jnp.where(side == 0, source + 4, jnp.where(source < 4, source, source + 8))
    move = jnp.where(to == (at & 7) * 16 + column, 1.0, 0.0).astype(jnp.bfloat16)

    def rows(c):
        return jnp.concatenate(
            [cells[:, c][:, None], cells[:, CH + c][:, None]], axis=1
        ).reshape(128, 128)

    depth = CH // CHUNKS
    copies = []
    for chunk in range(CHUNKS):
        for c in range(depth * chunk, depth * (chunk + 1), 2):
            both = jnp.concatenate([rows(c), rows(c + 1)], axis=1)
            moved = jnp.dot(move, both, preferred_element_type=jnp.float32).astype(jnp.bfloat16)
            scratch[:, c] = moved[:, :128].reshape(8, 16, 128)
            scratch[:, c + 1] = moved[:, 128:].reshape(8, 16, 128)
        span = pl.ds(depth * chunk, depth)
        copy = pltpu.make_async_copy(scratch.at[:, span], out.at[:, span], sems.at[chunk])
        copy.start()
        copies.append(copy)
    for copy in copies:
        copy.wait()


def order(cells):
    return pl.pallas_call(
        order_kernel,
        in_specs=[vmem()],
        out_specs=anywhere(),
        out_shape=jax.ShapeDtypeStruct((8, CH, 16, 128), jnp.bfloat16),
        scratch_shapes=[
            pltpu.VMEM((8, CH, 16, 128), jnp.bfloat16),
            pltpu.SemaphoreType.DMA((CHUNKS,)),
        ],
        compiler_params=vmem_params(),
        cost_estimate=pl.CostEstimate(
            flops=600_000_000, bytes_accessed=5_300_000, transcendentals=0
        ),
    )(cells)


def ring(cells, step):
    count = lax.axis_size("space")
    return lax.ppermute(cells, "space", [(i, (i + step) % count) for i in range(count)])


def depth_ring(cells, step):
    return lax.ppermute(
        cells, "mem", [(4 * y + (z + step) % 4, 4 * y + z) for y in range(2) for z in range(4)]
    )


def per_device(
    prior_ensemble,
    initial_kernel_taps,
    latter_kernel_taps,
    observed_cells,
    observed_count,
    local_radius,
    observed_value,
    error_variance,
):
    members = prior_ensemble.shape[0]
    bf16 = jnp.bfloat16
    own = jnp.swapaxes(prior_ensemble, 1, 2).reshape(members, 16 * CH, 128)
    cells = observed_cells.reshape(8, 128)
    digits = jnp.stack([cells // 6144, cells // 128 % 48, cells % 128]).reshape(24, 128).astype(bf16)
    digits = jnp.concatenate([digits, jnp.zeros((8, 128), bf16)])
    tail = own[:, (16 - HALO) * CH :].reshape(-1, 128)
    head = own[:, : HALO * CH].reshape(-1, 128)
    left = ring(jnp.concatenate([tail, digits]), 1)
    right = ring(jnp.concatenate([head, digits]), -1)

    inner, wide16, wide32 = inner_forecast(own, initial_kernel_taps, latter_kernel_taps)
    first_parts = lax.all_to_all(inner, "mem", split_axis=0, concat_axis=0, tiled=True)
    edge, picked = edge_forecast(inner, cells, left, right, wide16, wide32)

    picked = picked.reshape(3, 8, 8, 128)
    from_left = ring(picked[2], 1)
    from_right = ring(picked[0], -1)
    part = (cells // 128 % 48 // 16).reshape(8, 1, 128)
    here = jnp.where(part == 0, from_left, jnp.where(part == 1, picked[1], from_right))
    edge, first_parts = lax.optimization_barrier((edge, first_parts))
    second_parts = lax.all_to_all(edge, "mem", split_axis=0, concat_axis=0, tiled=True)
    pair = lax.ppermute(here, "mem", [(i, i ^ 4) for i in range(8)])
    both = jnp.stack([here, pair])
    pieces = (here, pair, depth_ring(both, 1), depth_ring(both, 2), depth_ring(both, 3))
    group = lax.axis_index("mem").astype(jnp.int32)
    numbers = jnp.stack([observed_count[0], local_radius[0], group])
    weights = transform_of(
        pieces, observed_cells, numbers, observed_value, error_variance, edge
    )
    mixed = mix(first_parts, second_parts, weights)
    back = lax.all_to_all(mixed, "mem", split_axis=0, concat_axis=0, tiled=True)
    return order(back)


def solution(mesh):
    return jax.shard_map(
        per_device,
        mesh=mesh,
        in_specs=(
            P("mem", None, "space", None),
            P(),
            P(),
            P("space", None),
            P("space"),
            P("space"),
            P("space", None),
            P("space", None),
        ),
        out_specs=P("mem", None, "space", None),
        check_vma=False,
    )
```
